128 devices in a mesh: section: 2 (over core), dp: 16 (over y, x), tensor: 4 (over z).
Axes of the slice: x: 4, y: 4, z: 4, core: 2. Of those that a mesh axis runs over, the one named last changes fastest.
Arguments:
- ends: bfloat16 [2, 4096, 1536], P('section', 'dp'), may hold values from -6 to 6
- segment_ids: int32 [4096], P('dp'), may hold values from 0 to 7, as said below
- norm_gains: float32 [2, 2, 1536], P('section'), may hold values from 0.5 to 1.5
- conv_in: bfloat16 [1536, 3, 1536], P(('section', 'dp'), None, 'tensor'), may hold values from -0.15625 to 0.15625
- conv_kernel: float32 [3, 1536], P(None, 'tensor'), may hold values from -3 to 3
- qkv_weight: bfloat16 [1536, 8, 5, 64], P(('section', 'dp'), 'tensor'), may hold values from -0.15625 to 0.15625
- qk_gains: float32 [2, 64], replicated, may hold values from 0.5 to 1.5
- mix_out: bfloat16 [2, 1536, 1536], P('section', 'tensor', 'dp'), may hold values from -0.3125 to 0.3125
- gate_up: bfloat16 [2, 1536, 2, 6912], P('section', 'dp', None, 'tensor'), may hold values from -0.15625 to 0.15625
- down: bfloat16 [2, 6912, 1536], P('section', 'tensor', 'dp'), may hold values from -0.078125 to 0.078125
Outputs:
- out_acts: bfloat16 [2, 4096, 1536], P('section', 'dp')
- in_grads: float32 [2, 4096, 1536], P('section', 'dp')
- gains_grad: float32 [2, 2, 1536], P('section')
- conv_in_grad: float32 [1536, 3, 1536], P(('section', 'dp'), None, 'tensor')
- kernel_grad: float32 [3, 1536], P(None, 'tensor')
- qkv_grad: float32 [1536, 8, 5, 64], P(('section', 'dp'), 'tensor')
- qk_grad: float32 [2, 64], replicated
- mix_out_grad: float32 [2, 1536, 1536], P('section', 'tensor', 'dp')
- gate_up_grad: float32 [2, 1536, 2, 6912], P('section', 'dp', None, 'tensor')
- down_grad: float32 [2, 6912, 1536], P('section', 'tensor', 'dp')
The draws below stay inside these ranges and needn't reach their ends.
Inputs may be any that keep to these rules, and one draw needn't show every extreme that they name: `segment_ids`: within each block of 128 consecutive tokens the ids start at 0 and rise by one at the first token of each new sequence; a block holds at most 8 sequences, the last of which takes the rest of the block; in every draw some block holds a single sequence of 128 tokens and some block holds 8 sequences.
All inputs are finite; a program needn't handle non-finite values.
Results may differ from the reference program's by a relative error of at most 0.025.
Values may be sent and summed in bfloat16 or wider, within the bound.
A program may use at most 256 MiB of HBM per device.

```python
import jax
import jax.numpy as jnp
from jax import lax

D = 1536
KVH = 8
HD = 64
FF = 6912
KW = 3
MBT = 128
G = 3
TOKENS = 4096


def draw_segment_ids(key, part):
    key = jax.random.fold_in(key, 7)
    rate_key, bits_key, whole_key, many_key = jax.random.split(key, 4)
    blocks = TOKENS // MBT
    rate_rows = jax.random.randint(rate_key, (blocks, 1), 1, 9)
    random_draws = jax.random.randint(bits_key, (blocks, MBT), 0, MBT)
    column = jnp.arange(MBT, dtype=jnp.int32)[None, :]
    row_ids = jnp.arange(blocks, dtype=jnp.int32)[:, None]
    single = jax.random.randint(whole_key, (), 0, blocks)
    crowded = (single + jax.random.randint(many_key, (), 1, blocks)) % blocks
    spacing = MBT // 8
    forced = (row_ids == crowded) & (column % spacing == 0)
    starts = ((random_draws < rate_rows) | forced) & (column > 0) & (row_ids != single)
    counted = jnp.cumsum(starts.astype(jnp.int32), axis=1)
    return jnp.minimum(counted, 7).reshape(TOKENS).astype(jnp.int32)


def shard_levels(own_key, dims, shards, low, top_value):
    def one(dim, blocks):
        steps = jax.random.uniform(jax.random.fold_in(jax.random.fold_in(own_key, 6), dim), (blocks,), jnp.float32, low / len(shards), top_value / len(shards))
        return jnp.repeat(jnp.exp(steps), dims[dim] // blocks).reshape((-1,) + (1,) * (len(dims) - dim - 1))

    loudness = one(*shards[0])
    for cut in shards[1:]:
        loudness = loudness * one(*cut)
    return loudness


def centred(own_key, extent, deviation, most, cuts=(), kind=jnp.bfloat16):
    array = deviation * jax.random.normal(own_key, extent, jnp.float32)
    if cuts:
        array = array * shard_levels(own_key, extent, cuts, -0.22, 0.18)
    return jnp.clip(array, -most, most).astype(kind)


def setup_inputs(seed: int = 0) -> dict:
    arg_keys = jax.random.split(jax.random.key(seed), 11)
    return {
        "ends": centred(arg_keys[0], (2, TOKENS, D), 1.0, 6.0, ((0, 2), (1, 16))),
        "segment_ids": draw_segment_ids(jax.random.fold_in(arg_keys[10], 71), 0),
        "norm_gains": jnp.clip(1.0 + 0.1 * jax.random.normal(arg_keys[2], (2, 2, D), jnp.float32), 0.5, 1.5),
        "conv_in": centred(arg_keys[3], (D, 3, D), D ** -0.5, 0.15625, ((0, 32), (2, 4))),
        "conv_kernel": centred(arg_keys[4], (KW, D), 0.5, 3.0, ((1, 4),), jnp.float32),
        "qkv_weight": centred(arg_keys[5], (D, KVH, G + 2, HD), D ** -0.5, 0.15625, ((0, 32), (1, 4))),
        "qk_gains": jnp.clip(1.0 + 0.1 * jax.random.normal(arg_keys[6], (2, HD), jnp.float32), 0.5, 1.5),
        "mix_out": centred(arg_keys[7], (2, D, D), (D // 4) ** -0.5, 0.3125, ((0, 2), (1, 4), (2, 16))),
        "gate_up": centred(arg_keys[8], (2, D, 2, FF), D ** -0.5, 0.15625, ((0, 2), (1, 16), (3, 4))),
        "down": centred(arg_keys[9], (2, FF, D), FF ** -0.5, 0.078125, ((0, 2), (1, 4), (2, 16))),
    }


@jax.custom_vjp
def low(v):
    return lax.optimization_barrier(v.astype(jnp.bfloat16)).astype(jnp.float32)

@jax.custom_vjp
def low_back(v):
    return v

def low_keep(v):
    return (low(v), None)

def low_pass(kept, grad):
    return (grad,)

def back_keep(v):
    return (v, None)

def back_low(kept, grad):
    return (low(grad),)
low.defvjp(low_keep, low_pass)
low_back.defvjp(back_keep, back_low)
epsilon = 1e-05
rope_base = 1000000.0
neg_large = -1e+30
highest = lax.Precision.HIGHEST

def rms_norm(values, gain_row):
    return values * lax.rsqrt(lax.optimization_barrier(jnp.mean(values * values, axis=-1, keepdims=True)) + epsilon) * gain_row

def rotate_heads(values, cosine_table, sine_table):
    half_size = values.shape[-1] // 2
    first_half = values[..., :half_size]
    second_half = values[..., half_size:]
    return jnp.concatenate([first_half * cosine_table - second_half * sine_table, second_half * cosine_table + first_half * sine_table], axis=-1)

def rope_tables(segments):
    length = segments.shape[0]
    places = jnp.arange(length, dtype=jnp.int32)
    begins = jnp.concatenate([jnp.ones((1,), jnp.bool_), segments[1:] != segments[:-1]])
    first_row = lax.cummax(jnp.where(begins, places, 0), axis=0)
    offset = (places - first_row).astype(jnp.float32)
    frequency = rope_base ** (-jnp.arange(HD // 2, dtype=jnp.float32) * 2.0 / HD)
    angles = offset[:, None] * frequency[None, :]
    return (jnp.cos(angles), jnp.sin(angles))

def short_conv(values, kernel_rows, segments):
    total = kernel_rows[0] * values
    for lag_count in range(1, KW):
        moved = jnp.concatenate([jnp.zeros((lag_count, values.shape[1]), values.dtype), values[:-lag_count]], axis=0)
        same_rows = jnp.concatenate([jnp.zeros((lag_count,), jnp.bool_), segments[lag_count:] == segments[:-lag_count]])
        total = total + kernel_rows[lag_count] * jnp.where(same_rows[:, None], moved, 0.0)
    return total

def feed_forward(middle, gain_row, gate_up_w, down_w):
    normed = low(rms_norm(middle, gain_row))
    gate_vals = low_back(jnp.dot(normed, gate_up_w.reshape(D, 2 * FF), precision=highest)).reshape(-1, 2, FF)
    hidden = low(jax.nn.silu(gate_vals[:, 0]) * gate_vals[:, 1])
    return middle + low_back(jnp.dot(hidden, down_w, precision=highest))

def conv_section(block_in, segments, params):
    normed = low(rms_norm(block_in, params['gains'][0, 0]))
    projected = low_back(jnp.dot(normed, params['conv_in'].reshape(D, 3 * D), precision=highest)).reshape(-1, 3, D)
    mixed_vals = short_conv(projected[:, 0] * projected[:, 2], params['kernel'], segments)
    mixer_out = low(projected[:, 1] * mixed_vals)
    middle = block_in + low_back(jnp.dot(mixer_out, params['mix_out'][0], precision=highest))
    return feed_forward(middle, params['gains'][0, 1], params['gate_up'][0], params['down'][0])

def attend_section(block_in, segments, params):
    normed = low(rms_norm(block_in, params['gains'][1, 0]))
    projected = low_back(jnp.dot(normed, params['qkv'].reshape(D, KVH * (G + 2) * HD), precision=highest)).reshape(-1, KVH, G + 2, HD)
    cosine_table, sine_table = rope_tables(segments)
    queries = low(rotate_heads(rms_norm(projected[:, :, :G], params['qk_gains'][0]), cosine_table[:, None, None], sine_table[:, None, None]))
    key_rows = low(rotate_heads(rms_norm(projected[:, :, G], params['qk_gains'][1]), cosine_table[:, None], sine_table[:, None]))
    value_rows = low(projected[:, :, G + 1])
    places = jnp.arange(segments.shape[0], dtype=jnp.int32)
    allowed = (segments[:, None] == segments[None, :]) & (places[None, :] <= places[:, None])
    scores = low_back(jnp.einsum('tkgd,skd->kgts', queries, key_rows, precision=highest) * HD ** (-0.5))
    scores = jnp.where(allowed, scores, neg_large)
    soft_weights = jax.nn.softmax(scores, axis=-1)
    attended = jnp.einsum('kgts,skd->tkgd', low(soft_weights), value_rows, precision=highest)
    mixer_out = low_back(low(attended)).reshape(-1, D)
    middle = block_in + low_back(jnp.dot(mixer_out, params['mix_out'][1], precision=highest))
    return feed_forward(middle, params['gains'][1, 1], params['gate_up'][1], params['down'][1])

def block_pair(params, block_in, probe, segments):
    first_out = conv_section(block_in, segments, params)
    sent = low_back(low(first_out) + probe)
    return (attend_section(sent, segments, params), low(first_out))

def reference(ends, segment_ids, norm_gains, conv_in, conv_kernel, qkv_weight, qk_gains, mix_out, gate_up, down):
    params = {'gains': norm_gains.astype(jnp.float32), 'conv_in': conv_in.astype(jnp.float32), 'kernel': conv_kernel.astype(jnp.float32), 'qkv': qkv_weight.astype(jnp.float32), 'qk_gains': qk_gains.astype(jnp.float32), 'mix_out': mix_out.astype(jnp.float32), 'gate_up': gate_up.astype(jnp.float32), 'down': down.astype(jnp.float32)}
    blocks = TOKENS // MBT
    block_in = ends[0].astype(jnp.float32)
    cotangent = ends[1].astype(jnp.float32)
    segments = segment_ids.reshape(blocks, MBT).astype(jnp.int32)
    probe = jnp.zeros((TOKENS, D), jnp.float32)

    def forward(weights, inputs, probes):

        def one_block(block_item):
            return jax.checkpoint(block_pair)(weights, block_item[0], block_item[1], block_item[2])
        finals, firsts = lax.map(one_block, (inputs.reshape(blocks, MBT, D), probes.reshape(blocks, MBT, D), segments))
        return (finals.reshape(TOKENS, D), firsts.reshape(TOKENS, D))
    finals, pull_back, firsts = jax.vjp(forward, params, block_in, probe, has_aux=True)
    grad_params, grad_in, grad_sent = pull_back(cotangent)
    out_acts = jnp.stack([firsts, finals]).astype(jnp.bfloat16)
    in_grads = jnp.stack([grad_in, grad_sent]).astype(jnp.float32)
    return (out_acts, in_grads, grad_params['gains'], grad_params['conv_in'], grad_params['kernel'], grad_params['qkv'], grad_params['qk_gains'], grad_params['mix_out'], grad_params['gate_up'], grad_params['down'])
```

```python
import functools

import jax
import jax.numpy as jnp
from jax import lax
from jax.experimental import pallas as pl
from jax.experimental.pallas import tpu as pltpu
from jax.sharding import PartitionSpec as P

SEC, DP, TEN = "section", "dp", "tensor"
MESH = pl.DeviceIdType.MESH
F32, BF = jnp.float32, jnp.bfloat16
ANY = pl.BlockSpec(memory_space=pl.ANY)
VM = pl.BlockSpec(memory_space=pltpu.VMEM)
DMA = pltpu.SemaphoreType.DMA
MIB = 1 << 20

MBT = 128
ROWS = 48
CHUNK = 64
epsilon = 1e-05
rope_base = 1000000.0
neg_large = -1e30


def place():
    d = lax.axis_index(DP)
    return lax.axis_index(SEC), d // 4, d % 4, lax.axis_index(TEN)


def near(axis, y, x, step):
    return (y, (x + step) % 4) if axis == 0 else ((y + step) % 4, x)


def greet(devices):
    barrier = pltpu.get_barrier_semaphore()
    for device in devices:
        pl.semaphore_signal(barrier, inc=1, device_id=device, device_id_type=MESH)
    pl.semaphore_wait(barrier, len(devices))


def remote(src, dst, send_sem, recv_sem, device):
    return pltpu.make_async_remote_copy(
        src_ref=src, dst_ref=dst, send_sem=send_sem, recv_sem=recv_sem, device_id=device, device_id_type=MESH
    )


def arrived(ref, sem):
    pltpu.make_async_copy(ref, ref, sem).wait()


def cut(columns):
    return (columns // 128 + 1) // 2 * 128


def root(values):
    return lax.rsqrt(jnp.mean(values * values, axis=-1, keepdims=True) + epsilon)


def gather_kernel(widths, own, other, mix, gu, dt, o_m, o_mix, o_gu, o_dt, local_sem, swap_sem, send_sem, recv_sem, turn):
    s, y, x, z = place()
    d = y * 4 + x
    outs = (o_m, o_mix, o_gu, o_dt)
    partner = (1 - s, d, z)

    def device(yx):
        return (s, yx[0] * 4 + yx[1], z)

    def block(a, h, yx):
        b = yx[0] * 4 + yx[1]
        return outs[a].at[h, b] if a == 0 else outs[a].at[b, h]

    greet([partner] + [device(near(k, y, x, step)) for k in (0, 1) for step in (1, -1)])
    swap = remote(other, o_m.at[s, d], swap_sem.at[0], swap_sem.at[1], partner)
    swap.start()
    copies = [pltpu.make_async_copy(own, o_m.at[s, d], local_sem.at[0])]
    copies += [pltpu.make_async_copy(src, dst.at[d], local_sem.at[1 + i]) for i, (src, dst) in enumerate(((mix, o_mix), (gu, o_gu), (dt, o_dt)))]
    for c in copies:
        c.start()
    for c in copies:
        c.wait()
    swap.wait()

    @pl.when(s == 1)
    def _():
        pl.semaphore_wait(turn, 1)

    def send(a, h, yx, lo, hi, to):
        ref = block(a, h, yx)
        if (lo, hi) != (0, widths[a]):
            ref = ref.at[:, lo:hi]
        remote(ref, ref, send_sem.at[a], recv_sem.at[a * 2 + h, yx[0] * 4 + yx[1]], device(to)).start()

    def wait(a, h, yx):
        arrived(block(a, h, yx), recv_sem.at[a * 2 + h, yx[0] * 4 + yx[1]])

    me = (y, x)
    pairs = [(a, h) for a in range(4) for h in (0, 1)]
    for a, h in pairs:
        for step in (1, -1):
            send(a, h, me, 0, widths[a], near(h, y, x, step))
    for a, h in pairs:
        for step in (1, -1):
            send(a, h, me, 0, widths[a], near(1 - h, y, x, step))
    for a, h in pairs:
        c = cut(widths[a])
        for step, lo, hi in ((1, 0, c), (-1, c, widths[a])):
            wait(a, h, near(h, y, x, -step))
            send(a, h, near(h, y, x, -step), lo, hi, near(h, y, x, step))
            for on in (1, -1):
                send(a, h, near(h, y, x, -step), 0, widths[a], near(1 - h, y, x, on))
    for a, h in pairs:
        far = near(h, y, x, 2)
        wait(a, h, far)
        for on in (1, -1):
            send(a, h, far, 0, widths[a], near(1 - h, y, x, on))
    for a, h in pairs:
        c = cut(widths[a])

        def relay(j, carry, a=a, h=h, c=c):
            line = near(h, y, x, j)
            for step, lo, hi in ((1, 0, c), (-1, c, widths[a])):
                src = near(1 - h, line[0], line[1], -step)
                wait(a, h, src)
                send(a, h, src, lo, hi, near(1 - h, y, x, step))
            return carry

        lax.fori_loop(0, 4, relay, 0)

    @pl.when(s == 0)
    def _():
        pl.semaphore_signal(turn, inc=1, device_id=partner, device_id_type=MESH)

    for a, h in pairs:

        def last(j, carry, a=a, h=h):
            line = near(h, y, x, j)
            wait(a, h, near(1 - h, line[0], line[1], 2))
            return carry

        lax.fori_loop(0, 4, last, 0)
    for a in range(4):
        sent = outs[a].at[:, 0:15] if a == 0 else outs[a].at[0:15]
        arrived(sent, send_sem.at[a])


def gather(own, other, mix, gu, dt):
    widths = tuple(v.shape[-1] for v in (own, mix, gu, dt))
    halves = [v.reshape(2, ROWS, v.shape[-1]) for v in (mix, gu, dt)]
    shapes = [jax.ShapeDtypeStruct((2, 16, ROWS, widths[0]), BF)]
    shapes += [jax.ShapeDtypeStruct((16, 2, ROWS, w), BF) for w in widths[1:]]
    full = pl.pallas_call(
        functools.partial(gather_kernel, widths),
        out_shape=shapes,
        in_specs=[ANY] * 5,
        out_specs=[ANY] * 4,
        scratch_shapes=[DMA((4,)), DMA((2,)), DMA((4,)), DMA((8, 16)), pltpu.SemaphoreType.REGULAR],
        compiler_params=pltpu.CompilerParams(collective_id=0, has_side_effects=True),
        name="gather_weights",
    )(own, other, *halves)
    return [f.reshape(-1, f.shape[-1]) for f in full]


def add_rows(dst, pieces):
    rows = dst.shape[-2]
    lead = dst.shape[0] if len(dst.shape) == 3 else 1

    def body(i, carry):
        at = pl.ds(pl.multiple_of(i % (rows // 16) * 16, 16), 16)
        k = i // (rows // 16)
        get = (lambda r: r[k, at, :]) if len(dst.shape) == 3 else (lambda r: r[at, :])
        total = get(pieces[0]).astype(F32)
        for p in pieces[1:]:
            total = total + get(p).astype(F32)
        if len(dst.shape) == 3:
            dst[k, at, :] = total.astype(dst.dtype)
        else:
            dst[at, :] = total.astype(dst.dtype)
        return carry

    lax.fori_loop(0, lead * (rows // 16), body, 0)


def scatter_kernel(widths, *refs):
    n = len(widths)
    grads, small = refs[:n], refs[n]
    outs, small_out = refs[n + 1 : 2 * n + 1], refs[2 * n + 1]
    refs = refs[2 * n + 2 :]
    per = 11
    buffers = [refs[a * per : (a + 1) * per] for a in range(n)]
    small_in, small_acc, load_sem, recv_sem, send_sem, small_send, small_recv = refs[n * per :]
    s, y, x, z = place()

    def device(yx):
        return (s, yx[0] * 4 + yx[1], z)

    peers = [[device(near(k, y, x, j)) for j in (1, 2, 3)] for k in (0, 1)]
    peers.append([(s, y * 4 + x, (z + j) % 4) for j in (1, 2, 3)])
    greet([p for group in peers for p in group])

    def line(a, h, yx):
        return grads[a].at[yx[0], :, h] if h == 0 else grads[a].at[:, yx[1], h]

    pairs = [(a, h) for a in range(n) for h in (0, 1)]
    loads = {}
    for a, h in pairs:
        t_up, t_dn, total = (buffers[a][i].at[h] for i in (4, 5, 6))
        c, w = cut(widths[a]), widths[a]
        r1_up, r1_dn, r2_up, r2_dn = (buffers[a][i].at[h] for i in (0, 1, 2, 3))
        first = 1 - h
        up, dn, far = (near(first, y, x, step) for step in (1, -1, 2))
        sem = recv_sem.at[a * 2 + h]
        sends = [
            remote(line(a, h, far).at[:, :, 0:c], r1_up, send_sem.at[a * 2 + h, 0], sem.at[0], device(up)),
            remote(line(a, h, far).at[:, :, c:w], r1_dn, send_sem.at[a * 2 + h, 1], sem.at[1], device(dn)),
            remote(line(a, h, up).at[:, :, c:w], r2_up.at[:, :, c:w], send_sem.at[a * 2 + h, 2], sem.at[2], device(up)),
            remote(line(a, h, dn).at[:, :, 0:c], r2_dn.at[:, :, 0:c], send_sem.at[a * 2 + h, 3], sem.at[3], device(dn)),
        ]
        fetch = [
            pltpu.make_async_copy(line(a, h, up).at[:, :, 0:c], t_up, load_sem.at[a * 2 + h, 0]),
            pltpu.make_async_copy(line(a, h, dn).at[:, :, c:w], t_dn, load_sem.at[a * 2 + h, 1]),
            pltpu.make_async_copy(line(a, h, (y, x)), total, load_sem.at[a * 2 + h, 2]),
        ]
        for copy in sends + fetch:
            copy.start()
        loads[a, h] = (sends, fetch)

    small_acc[...] = small[...]
    for k in range(3):
        hops = []
        for j in range(3):
            hop = remote(small_acc, small_in.at[k * 3 + j], small_send.at[k * 3 + j], small_recv.at[k * 3 + j], peers[k][j])
            hop.start()
            hops.append(hop)
        for hop in hops:
            hop.wait()
        summed = small_acc[...] + small_in[k * 3] + small_in[k * 3 + 1] + small_in[k * 3 + 2]
        if k == 2:
            row = lax.broadcasted_iota(jnp.int32, summed.shape, 0)
            summed = jnp.where(row == 3, small_acc[...], summed)
        small_acc[...] = summed
    small_out[...] = small_acc[...]

    for a, h in pairs:
        t_up, t_dn = (buffers[a][i].at[h] for i in (4, 5))
        c, w = cut(widths[a]), widths[a]
        r1_up, r1_dn, r2_up, r2_dn = (buffers[a][i].at[h] for i in (0, 1, 2, 3))
        first = 1 - h
        up, dn = (near(first, y, x, step) for step in (1, -1))
        sends, fetch = loads[a, h]
        sem = recv_sem.at[a * 2 + h]
        fetch[0].wait()
        sends[0].wait_recv()
        add_rows(t_up, [t_up, r1_up])
        go = remote(t_up, r2_up.at[:, :, 0:c], send_sem.at[a * 2 + h, 4], sem.at[4], device(up))
        go.start()
        fetch[1].wait()
        sends[1].wait_recv()
        add_rows(t_dn, [t_dn, r1_dn])
        back = remote(t_dn, r2_dn.at[:, :, c:w], send_sem.at[a * 2 + h, 5], sem.at[5], device(dn))
        back.start()
        sends += [go, back]

    for a, h in pairs:
        total = buffers[a][6].at[h]
        q1_up, q1_dn, q2_up, q2_dn = (buffers[a][i].at[h] for i in (7, 8, 9, 10))
        c, w = cut(widths[a]), widths[a]
        sends, fetch = loads[a, h]
        sem = recv_sem.at[a * 2 + h]
        fetch[2].wait()
        for copy in sends[2:]:
            copy.wait_recv()
        add_rows(total, [total, buffers[a][2].at[h], buffers[a][3].at[h]])
        own = x if h == 0 else y
        up, dn = (near(h, y, x, step) for step in (1, -1))
        far, i_up, i_dn = ((own + step) % 4 for step in (2, 1, -1))
        more = [
            remote(total.at[far, :, 0:c], q1_up, send_sem.at[a * 2 + h, 6], sem.at[6], device(up)),
            remote(total.at[far, :, c:w], q1_dn, send_sem.at[a * 2 + h, 7], sem.at[7], device(dn)),
            remote(total.at[i_up, :, c:w], q2_up.at[:, c:w], send_sem.at[a * 2 + h, 8], sem.at[8], device(up)),
            remote(total.at[i_dn, :, 0:c], q2_dn.at[:, 0:c], send_sem.at[a * 2 + h, 9], sem.at[9], device(dn)),
        ]
        for copy in more:
            copy.start()
        sends += more

    for a, h in pairs:
        total = buffers[a][6].at[h]
        q1_up, q1_dn, q2_up, q2_dn = (buffers[a][i].at[h] for i in (7, 8, 9, 10))
        c, w = cut(widths[a]), widths[a]
        sends, fetch = loads[a, h]
        sem = recv_sem.at[a * 2 + h]
        own = x if h == 0 else y
        up, dn = (near(h, y, x, step) for step in (1, -1))
        i_up, i_dn = ((own + step) % 4 for step in (1, -1))
        sends[6].wait_recv()
        add_rows(q1_up, [q1_up, total.at[i_up, :, 0:c]])
        go = remote(q1_up, q2_up.at[:, 0:c], send_sem.at[a * 2 + h, 10], sem.at[10], device(up))
        go.start()
        sends[7].wait_recv()
        add_rows(q1_dn, [q1_dn, total.at[i_dn, :, c:w]])
        back = remote(q1_dn, q2_dn.at[:, c:w], send_sem.at[a * 2 + h, 11], sem.at[11], device(dn))
        back.start()
        sends += [go, back]

    for a, h in pairs:
        total = buffers[a][6].at[h]
        sends, fetch = loads[a, h]
        own = x if h == 0 else y
        for copy in sends[8:]:
            copy.wait_recv()
        add_rows(outs[a].at[h], [total.at[own], buffers[a][9].at[h], buffers[a][10].at[h]])
    for a, h in pairs:
        for copy in loads[a, h][0]:
            copy.wait_send()


def scatter(grads, small):
    widths = tuple(g.shape[-1] for g in grads)
    scratch = []
    for w in widths:
        c = cut(w)
        scratch += [pltpu.VMEM((2, 4, ROWS, k), BF) for k in (c, w - c, w, w, c, w - c, w)]
        scratch += [pltpu.VMEM((2, ROWS, k), BF) for k in (c, w - c, w, w)]
    n = len(grads)
    scratch += [pltpu.VMEM((9,) + small.shape, F32), pltpu.VMEM(small.shape, F32)]
    scratch += [DMA((2 * n, 3)), DMA((2 * n, 12)), DMA((2 * n, 12)), DMA((9,)), DMA((9,))]
    return pl.pallas_call(
        functools.partial(scatter_kernel, widths),
        out_shape=[jax.ShapeDtypeStruct((2, ROWS, w), F32) for w in widths] + [jax.ShapeDtypeStruct(small.shape, F32)],
        in_specs=[ANY] * n + [VM],
        out_specs=[VM] * (n + 1),
        scratch_shapes=scratch,
        compiler_params=pltpu.CompilerParams(collective_id=1, has_side_effects=True, vmem_limit_bytes=56 * MIB),
        name="sum_gradients",
    )(*grads, small)


def swap_kernel(mixer, small, own, other, small_own, small_other, sem):
    s, y, x, z = place()
    partner = (1 - s, y * 4 + x, z)
    greet([partner])
    copies = [
        remote(mixer.at[1 - s], other, sem.at[0], sem.at[1], partner),
        remote(small, small_other, sem.at[2], sem.at[3], partner),
    ]
    for copy in copies:
        copy.start()
    own[...] = mixer[s]
    small_own[...] = small[...]
    for copy in copies:
        copy.wait()


def swap_halves(mixer, small):
    half = jax.ShapeDtypeStruct(mixer.shape[1:], F32)
    rows = jax.ShapeDtypeStruct(small.shape, F32)
    return pl.pallas_call(
        swap_kernel,
        out_shape=[half, half, rows, rows],
        in_specs=[VM, VM],
        out_specs=[VM] * 4,
        scratch_shapes=[DMA((4,))],
        compiler_params=pltpu.CompilerParams(collective_id=2, has_side_effects=True),
        name="swap_halves",
    )(mixer, small)


def chunk_norm(hidden, gain):
    return hidden * root(hidden) * gain


def chunk_norm_back(values, gain, grad):
    factor = root(values)
    weighted = grad * gain
    grad_in = factor * weighted - values * (factor * factor * factor) * jnp.mean(values * weighted, axis=-1, keepdims=True)
    return grad_in, jnp.sum(grad * values * factor, axis=0, keepdims=True)


def mixer_out_chunk(total, mine, block_in, gain, full, middle):
    hidden = block_in[mine, :].astype(F32) + total
    middle[...] = hidden
    full[mine, :] = chunk_norm(hidden, gain[...]).astype(BF)


def ffn_out_chunk(total, mine, middle, full):
    full[mine, :] = (middle[...] + total).astype(BF)


def ffn_back_chunk(total, mine, middle, gain, top, full, grad_middle, grad_gain):
    grad_in, grad_gain[...] = chunk_norm_back(middle[...], gain[...], total)
    grad = top[mine, :].astype(F32) + grad_in
    grad_middle[...] = grad
    full[mine, :] = grad.astype(BF)


def mixer_back_chunk(total, mine, block_in, gain, grad_middle, full, grad_gain):
    grad_in, grad_gain[...] = chunk_norm_back(block_in[mine, :].astype(F32), gain[...], total)
    full[mine, :] = (grad_middle[...] + grad_in).astype(BF)


def sum_kernel(act, hand_over, chunk, n_in, n_out, part, *refs):
    ins, outs = refs[:n_in], refs[n_in : n_in + n_out]
    refs = refs[n_in + n_out :]
    if hand_over:
        handed, refs = refs[0], refs[1:]
    inbox, send_sem, recv_sem, give_sem = refs
    full = outs[0]
    s, y, x, z = place()
    d = y * 4 + x
    mates = [(s, d, (z + j) % 4) for j in (1, 2, 3)]
    partner = (1 - s, d, z)

    def rows(k):
        return pl.ds(pl.multiple_of(k % 4 * CHUNK, CHUNK), CHUNK)

    def work():
        greet(mates + [partner] if hand_over else mates)
        hops = []
        for j in (1, 2, 3):
            hop = remote(part.at[rows(z + j)], inbox.at[j - 1], send_sem.at[j - 1], recv_sem.at[j - 1], mates[j - 1])
            hop.start()
            hops.append(hop)
        total = part[rows(z), :].astype(F32)
        for hop in hops:
            hop.wait_recv()
        for j in range(3):
            total = total + inbox[j].astype(F32)
        chunk(total, rows(z), *ins, *outs)
        for j in (1, 2, 3):
            hop = remote(full.at[rows(z)], full.at[rows(z)], send_sem.at[2 + j], recv_sem.at[2 + j], mates[j - 1])
            hop.start()
            hops.append(hop)
        for j in (1, 2, 3):
            arrived(full.at[rows(z - j)], recv_sem.at[2 + j])
        if hand_over:
            give = remote(full, handed, give_sem.at[0], give_sem.at[1], partner)
            give.start()
            give.wait_send()
        for hop in hops:
            hop.wait_send()

    pl.when(s == act)(work)
    if hand_over:

        @pl.when(s != act)
        def _():
            greet([partner])
            arrived(handed, give_sem.at[1])


def sum_rows(act, hand_over, chunk, number, part, ins, outs):
    rows, width = part.shape
    shapes = [jax.ShapeDtypeStruct((rows, width), BF)] + outs
    n_out = len(shapes)
    if hand_over:
        shapes.append(jax.ShapeDtypeStruct((rows, width), BF))
    return pl.pallas_call(
        functools.partial(sum_kernel, act, hand_over, chunk, len(ins), n_out),
        out_shape=shapes,
        in_specs=[VM] * (1 + len(ins)),
        out_specs=[VM] * len(shapes),
        scratch_shapes=[pltpu.VMEM((3, CHUNK, width), BF), DMA((6,)), DMA((6,)), DMA((2,))],
        compiler_params=pltpu.CompilerParams(collective_id=number, has_side_effects=True, vmem_limit_bytes=24 * MIB),
        name="sum_rows_%d" % number,
    )(part, *ins)


def rope_tables(segments, head_size):
    length = segments.shape[0]
    places = jnp.arange(length, dtype=jnp.int32)
    begins = jnp.concatenate([jnp.ones((1,), jnp.bool_), segments[1:] != segments[:-1]])
    first_row = lax.cummax(jnp.where(begins, places, 0), axis=0)
    offset = (places - first_row).astype(F32)
    frequency = rope_base ** (-jnp.arange(head_size // 2, dtype=F32) * 2.0 / head_size)
    angles = offset[:, None] * frequency[None, :]
    return (jnp.cos(angles), jnp.sin(angles))


def rotate_heads(values, cosine, sine):
    a, b = jnp.split(values, 2, axis=-1)
    return jnp.concatenate([a * cosine - b * sine, b * cosine + a * sine], axis=-1)


def rotate_back(grads, cosine, sine):
    a, b = jnp.split(grads, 2, axis=-1)
    return jnp.concatenate([a * cosine + b * sine, b * cosine - a * sine], axis=-1)


def norm_back(values, gain_row, grad_out):
    factor = root(values)
    weighted = grad_out * gain_row
    grad_in = factor * weighted - values * (factor * factor * factor) * jnp.mean(values * weighted, axis=-1, keepdims=True)
    return (grad_in, grad_out * values * factor)


def lag_rows(values, lag):
    return jnp.concatenate([jnp.zeros((lag,) + values.shape[1:], values.dtype), values[:-lag]], axis=0)


def lead_rows(values, lag):
    return jnp.concatenate([values[lag:], jnp.zeros((lag,) + values.shape[1:], values.dtype)], axis=0)


def same_sequence(segments, lag):
    return jnp.concatenate([jnp.zeros((lag,), jnp.bool_), segments[lag:] == segments[:-lag]])[:, None]


def dot(a, b):
    return jnp.dot(a, b, preferred_element_type=F32)


def dot_bt(a, b):
    return lax.dot_general(a, b, (((1,), (1,)), ((), ())), preferred_element_type=F32)


def dot_at(a, b):
    return lax.dot_general(a, b, (((0,), (0,)), ((), ())), preferred_element_type=F32)


def held(values, after):
    return lax.optimization_barrier((values, after))[0]


def local(ends, segment_ids, norm_gains, conv_in, conv_kernel, qkv_weight, qk_gains, mix_out, gate_up, down):
    is_first = lax.axis_index(SEC) == 0
    width = ends.shape[2]
    channels = mix_out.shape[1]
    hidden = gate_up.shape[3]
    padded = (hidden + 127) // 128 * 128
    kv, group, head = qkv_weight.shape[1], qkv_weight.shape[2] - 2, qkv_weight.shape[3]
    qkv_width = kv * (group + 2) * head
    taps = conv_kernel.shape[0]
    tokens = ends.shape[1]
    blocks = tokens // MBT
    inv_sqrt = head ** (-0.5)
    spare = ((0, 0), (0, padded - hidden))

    conv_rows = conv_in.reshape(ROWS, taps * channels)
    qkv_rows = jnp.pad(qkv_weight.reshape(ROWS, qkv_width), ((0, 0), (0, taps * channels - qkv_width)))
    gate_rows = jnp.pad(gate_up[0], ((0, 0),) + spare).reshape(2 * ROWS, 2 * padded)
    down_rows = jnp.pad(down[0].T, spare)
    w_mixer, w_mix, w_gate, w_down = gather(
        jnp.where(is_first, conv_rows, qkv_rows),
        jnp.where(is_first, qkv_rows, conv_rows),
        mix_out[0].T,
        gate_rows,
        down_rows,
    )
    w_qkv = w_mixer[:, :qkv_width]
    gain_mixer, gain_ffn = norm_gains[0, 0:1], norm_gains[0, 1:2]
    segments = segment_ids + 8 * (jnp.arange(tokens, dtype=jnp.int32) // MBT)
    own_rows = ends[0]
    row_f32 = jax.ShapeDtypeStruct((1, width), F32)
    chunk_f32 = jax.ShapeDtypeStruct((CHUNK, width), F32)

    def ffn_forward(normed):
        pair = dot(normed, w_gate)
        gate, up = pair[:, :padded], pair[:, padded:]
        return gate, up, (jax.nn.silu(gate) * up).astype(BF)

    def ffn_backward(gate, up, top):
        grad_hidden = dot_bt_rows(top, w_down)
        sig = jax.nn.sigmoid(gate)
        act = gate * sig
        grad_gate = grad_hidden * up * sig * (1.0 + gate * (1.0 - sig))
        grad_pair = jnp.concatenate([grad_gate.astype(BF), (grad_hidden * act).astype(BF)], axis=1)
        return grad_pair, dot_bt(grad_pair, w_gate).astype(BF)

    def dot_bt_rows(top, weight):
        return dot(top, weight)

    block_a = own_rows.astype(F32)
    normed_a = (block_a * root(block_a) * gain_mixer).astype(BF)
    projected = dot(normed_a, w_mixer)
    part_b, part_c, part_x = (projected[:, i * channels : (i + 1) * channels] for i in range(3))
    product = part_b * part_x
    mixed = conv_kernel[0] * product
    for lag in range(1, taps):
        mixed = mixed + conv_kernel[lag] * jnp.where(same_sequence(segments, lag), lag_rows(product, lag), 0.0)
    mixer_a = (part_c * mixed).astype(BF)
    ffn_in_a, middle_a = sum_rows(
        0, False, mixer_out_chunk, 3, dot_bt(mixer_a, w_mix).astype(BF), [own_rows, gain_ffn], [chunk_f32]
    )
    gate_a, up_a, hidden_a = ffn_forward(ffn_in_a)
    result_a, sent = sum_rows(0, True, ffn_out_chunk, 4, dot_bt(hidden_a, w_down).astype(BF), [middle_a], [])

    block_b = sent.astype(F32)
    normed_b = (block_b * root(block_b) * gain_mixer).astype(BF)
    heads = dot(normed_b, w_qkv).reshape(blocks, MBT, kv, group + 2, head)
    cosine, sine = rope_tables(segments, head)
    cosine, sine = (v.reshape(blocks, MBT, 1, 1, head // 2) for v in (cosine, sine))
    query_raw, key_raw = heads[:, :, :, :group], heads[:, :, :, group : group + 1]
    queries = rotate_heads(query_raw * root(query_raw) * qk_gains[0], cosine, sine).astype(BF)
    keys = rotate_heads(key_raw * root(key_raw) * qk_gains[1], cosine, sine).astype(BF)[:, :, :, 0]
    values = heads[:, :, :, group + 1].astype(BF)
    rows = segments.reshape(blocks, MBT)
    order = jnp.arange(MBT, dtype=jnp.int32)
    allowed = (rows[:, :, None] == rows[:, None, :]) & (order[None, :] <= order[:, None])
    scores = jnp.einsum("btkgd,bskd->bkgts", queries, keys, preferred_element_type=F32) * inv_sqrt
    scores = jnp.where(allowed[:, None, None], scores, neg_large)
    exponent = jnp.exp(scores - jnp.max(scores, axis=-1, keepdims=True))
    soft = exponent / jnp.sum(exponent, axis=-1, keepdims=True)
    soft_low = soft.astype(BF)
    attended = jnp.einsum("bkgts,bskd->btkgd", soft_low, values, preferred_element_type=F32)
    mixer_b = attended.astype(BF).reshape(tokens, channels)
    ffn_in_b, middle_b = sum_rows(
        1, False, mixer_out_chunk, 5, dot_bt(mixer_b, w_mix).astype(BF), [sent, gain_ffn], [chunk_f32]
    )
    gate_b, up_b, hidden_b = ffn_forward(ffn_in_b)

    grad_pair_b, grad_in_b = ffn_backward(gate_b, up_b, own_rows)
    grad_mid_b, grad_chunk_b, gain_b1 = sum_rows(
        1, False, ffn_back_chunk, 6, grad_in_b, [middle_b, gain_ffn, own_rows], [chunk_f32, row_f32]
    )
    grad_att = dot(grad_mid_b, w_mix).astype(BF).reshape(blocks, MBT, kv, group, head)
    grad_soft = jnp.einsum("btkgd,bskd->bkgts", grad_att, values, preferred_element_type=F32)
    grad_value = jnp.einsum("bkgts,btkgd->bskd", soft_low, grad_att, preferred_element_type=F32)
    delta = jnp.sum(soft * grad_soft, axis=-1, keepdims=True)
    grad_scores = (soft * (grad_soft - delta)).astype(BF)
    grad_query = jnp.einsum("bkgts,bskd->btkgd", grad_scores, keys, preferred_element_type=F32) * inv_sqrt
    grad_key = jnp.einsum("bkgts,btkgd->bskd", grad_scores, queries, preferred_element_type=F32) * inv_sqrt
    grad_qraw, query_gain = norm_back(query_raw, qk_gains[0], rotate_back(grad_query, cosine, sine))
    grad_kraw, key_gain = norm_back(key_raw, qk_gains[1], rotate_back(grad_key[:, :, :, None], cosine, sine))
    grad_heads = jnp.concatenate([grad_qraw, grad_kraw, grad_value[:, :, :, None]], axis=3)
    grad_heads = grad_heads.astype(BF).reshape(tokens, qkv_width)
    grad_b, given, gain_b0 = None, None, None
    grad_b, gain_b0, given = sum_rows(
        1,
        True,
        mixer_back_chunk,
        7,
        dot_bt(grad_heads, w_qkv).astype(BF),
        [sent, gain_mixer, grad_chunk_b],
        [row_f32],
    )

    late_hidden = held(hidden_b, given)
    result_b = sum_rows(1, False, ffn_out_chunk, 8, dot_bt(late_hidden, w_down).astype(BF), [middle_b], [])[0]

    def second_ffn():
        return (
            dot_at(ffn_in_b, grad_pair_b).astype(BF),
            dot_at(own_rows, hidden_b).astype(BF),
            grad_in_b,
        )

    def first_ffn():
        grad_pair, grad_in = ffn_backward(gate_a, up_a, given)
        return (
            dot_at(ffn_in_a, grad_pair).astype(BF),
            dot_at(given, hidden_a).astype(BF),
            grad_in,
        )

    grad_gate_w, grad_down_w, grad_in_a = lax.cond(is_first, first_ffn, second_ffn)
    grad_mid_a, grad_chunk_a, gain_a1 = sum_rows(
        0, False, ffn_back_chunk, 9, grad_in_a, [middle_a, gain_ffn, given], [chunk_f32, row_f32]
    )

    def first_mixer():
        grad_y = dot(grad_mid_a, w_mix)
        grad_c = grad_y * mixed
        grad_mixed = grad_y * part_c
        grad_product = conv_kernel[0] * grad_mixed
        kernel_rows = [jnp.sum(grad_mixed * product, axis=0)]
        for lag in range(1, taps):
            masked = jnp.where(same_sequence(segments, lag), grad_mixed, 0.0)
            kernel_rows.append(jnp.sum(masked * lag_rows(product, lag), axis=0))
            grad_product = grad_product + conv_kernel[lag] * lead_rows(masked, lag)
        grad_proj = jnp.concatenate([grad_product * part_x, grad_c, grad_product * part_b], axis=1).astype(BF)
        return (
            dot_bt(grad_proj, w_mixer).astype(BF),
            dot_at(normed_a, grad_proj).astype(BF),
            dot_at(grad_mid_a, mixer_a).astype(BF),
            jnp.pad(jnp.concatenate(kernel_rows), (0, width - taps * channels)),
        )

    def second_mixer():
        row = jnp.concatenate([jnp.sum(query_gain, axis=(0, 1, 2, 3)), jnp.sum(key_gain, axis=(0, 1, 2, 3))])
        return (
            grad_in_b,
            jnp.pad(dot_at(normed_b, grad_heads).astype(BF), ((0, 0), (0, taps * channels - qkv_width))),
            dot_at(grad_mid_b, mixer_b).astype(BF),
            jnp.pad(row, (0, width - 2 * head)),
        )

    grad_part_a, grad_mixer_w, grad_mix_w, extra = lax.cond(is_first, first_mixer, second_mixer)
    grad_a, gain_a0 = sum_rows(
        0, False, mixer_back_chunk, 10, grad_part_a, [own_rows, gain_mixer, grad_chunk_a], [row_f32]
    )

    def view(grad):
        return grad.reshape(4, 4, 2, ROWS, grad.shape[-1])

    mixer_view = grad_mixer_w.reshape(2, 4, 4, ROWS, -1).transpose(1, 2, 0, 3, 4)
    zero = jnp.zeros((1, width), F32)
    small = jnp.concatenate(
        [
            jnp.where(is_first, gain_a0, gain_b0),
            jnp.where(is_first, gain_a1, gain_b1),
            jnp.where(is_first, zero, extra[None]),
            jnp.where(is_first, extra[None], zero),
            jnp.zeros((4, width), F32),
        ]
    )
    sum_gate, sum_down, sum_mix, sum_mixer, small_sum = scatter(
        [view(grad_gate_w), view(grad_down_w), view(grad_mix_w), mixer_view], small
    )
    mixer_own, mixer_other, small_own, small_other = swap_halves(sum_mixer, small_sum)
    conv_grad = jnp.where(is_first, mixer_own, mixer_other)
    qkv_grad = jnp.where(is_first, mixer_other, mixer_own)[:, :qkv_width]
    of_first = jnp.where(is_first, small_own, small_other)
    of_second = jnp.where(is_first, small_other, small_own)
    return (
        jnp.where(is_first, result_a, result_b)[None],
        jnp.where(is_first, grad_a, grad_b).astype(F32)[None],
        small_own[None, 0:2],
        conv_grad.reshape(conv_in.shape),
        of_first[3, : taps * channels].reshape(taps, channels),
        qkv_grad.reshape(qkv_weight.shape),
        of_second[2, : 2 * head].reshape(2, head),
        sum_mix.reshape(2 * ROWS, channels).T[None],
        sum_gate.reshape(2 * ROWS, 2, padded)[None, :, :, :hidden],
        sum_down.reshape(2 * ROWS, padded)[:, :hidden].T[None],
    )


def solution(mesh):
    dims = (
        P(SEC, DP, None),
        P(DP),
        P(SEC, None, None),
        P((SEC, DP), None, TEN),
        P(None, TEN),
        P((SEC, DP), TEN, None, None),
        P(),
        P(SEC, TEN, DP),
        P(SEC, DP, None, TEN),
        P(SEC, TEN, DP),
    )
    results = (dims[0], dims[0], dims[2], dims[3], dims[4], dims[5], dims[6], dims[7], dims[8], dims[9])
    return jax.shard_map(local, mesh=mesh, in_specs=dims, out_specs=results, check_vma=False)
```

```python
import functools

import jax
import jax.numpy as jnp
import numpy as np
from jax import lax
from jax.experimental import pallas as pl
from jax.experimental.pallas import tpu as pltpu
from jax.sharding import PartitionSpec as P

SEC, DP, TEN = "section", "dp", "tensor"
MESH = pl.DeviceIdType.MESH
F32, BF = jnp.float32, jnp.bfloat16
ANY = pl.BlockSpec(memory_space=pl.ANY)
VM = pl.BlockSpec(memory_space=pltpu.VMEM)
DMA = pltpu.SemaphoreType.DMA
MIB = 1 << 20
CHAIN_VMEM = 30

MBT = 128
ROWS = 48
CHUNK = 64
epsilon = 1e-05
rope_base = 1000000.0
neg_large = -1e30


def place():
    d = lax.axis_index(DP)
    return lax.axis_index(SEC), d // 4, d % 4, lax.axis_index(TEN)


def near(axis, y, x, step):
    return (y, (x + step) % 4) if axis == 0 else ((y + step) % 4, x)


def greet(devices):
    barrier = pltpu.get_barrier_semaphore()
    for device in devices:
        pl.semaphore_signal(barrier, inc=1, device_id=device, device_id_type=MESH)
    pl.semaphore_wait(barrier, len(devices))


def remote(src, dst, send_sem, recv_sem, device):
    return pltpu.make_async_remote_copy(
        src_ref=src, dst_ref=dst, send_sem=send_sem, recv_sem=recv_sem, device_id=device, device_id_type=MESH
    )


def arrived(ref, sem):
    pltpu.make_async_copy(ref, ref, sem).wait()


def cut(columns):
    return (columns // 128 + 1) // 2 * 128


def root(values):
    return lax.rsqrt(jnp.mean(values * values, axis=-1, keepdims=True) + epsilon)


def gather_kernel(widths, own, other, mix, gu, dt, o_m, o_mix, o_gu, o_dt, local_sem, swap_sem, send_sem, recv_sem, turn):
    s, y, x, z = place()
    d = y * 4 + x
    outs = (o_m, o_mix, o_gu, o_dt)
    partner = (1 - s, d, z)

    def device(yx):
        return (s, yx[0] * 4 + yx[1], z)

    def block(a, h, yx):
        b = yx[0] * 4 + yx[1]
        return outs[a].at[h, b] if a == 0 else outs[a].at[b, h]

    greet([partner] + [device(near(k, y, x, step)) for k in (0, 1) for step in (1, -1)])
    swap = remote(other, o_m.at[s, d], swap_sem.at[0], swap_sem.at[1], partner)
    swap.start()
    copies = [pltpu.make_async_copy(own, o_m.at[s, d], local_sem.at[0])]
    copies += [pltpu.make_async_copy(src, dst.at[d], local_sem.at[1 + i]) for i, (src, dst) in enumerate(((mix, o_mix), (gu, o_gu), (dt, o_dt)))]
    for c in copies:
        c.start()
    for c in copies:
        c.wait()
    swap.wait()

    @pl.when(s == 1)
    def _():
        pl.semaphore_wait(turn, 1)

    def send(a, h, yx, lo, hi, to):
        ref = block(a, h, yx)
        if (lo, hi) != (0, widths[a]):
            ref = ref.at[:, lo:hi]
        remote(ref, ref, send_sem.at[a], recv_sem.at[a * 2 + h, yx[0] * 4 + yx[1]], device(to)).start()

    def wait(a, h, yx):
        arrived(block(a, h, yx), recv_sem.at[a * 2 + h, yx[0] * 4 + yx[1]])

    me = (y, x)
    pairs = [(a, h) for a in range(4) for h in (0, 1)]
    for a, h in pairs:
        for step in (1, -1):
            send(a, h, me, 0, widths[a], near(h, y, x, step))
    for a, h in pairs:
        for step in (1, -1):
            send(a, h, me, 0, widths[a], near(1 - h, y, x, step))
    for a, h in pairs:
        c = cut(widths[a])
        for step, lo, hi in ((1, 0, c), (-1, c, widths[a])):
            wait(a, h, near(h, y, x, -step))
            send(a, h, near(h, y, x, -step), lo, hi, near(h, y, x, step))
            for on in (1, -1):
                send(a, h, near(h, y, x, -step), 0, widths[a], near(1 - h, y, x, on))
    for a, h in pairs:
        far = near(h, y, x, 2)
        wait(a, h, far)
        for on in (1, -1):
            send(a, h, far, 0, widths[a], near(1 - h, y, x, on))
    for a, h in pairs:
        c = cut(widths[a])

        def relay(j, carry, a=a, h=h, c=c):
            line = near(h, y, x, j)
            for step, lo, hi in ((1, 0, c), (-1, c, widths[a])):
                src = near(1 - h, line[0], line[1], -step)
                wait(a, h, src)
                send(a, h, src, lo, hi, near(1 - h, y, x, step))
            return carry

        lax.fori_loop(0, 4, relay, 0)

    for a, h in pairs:

        def last(j, carry, a=a, h=h):
            line = near(h, y, x, j)
            wait(a, h, near(1 - h, line[0], line[1], 2))
            return carry

        lax.fori_loop(0, 4, last, 0)
    for a in range(4):
        sent = outs[a].at[:, 0:15] if a == 0 else outs[a].at[0:15]
        arrived(sent, send_sem.at[a])

    @pl.when(s == 0)
    def _():
        pl.semaphore_signal(turn, inc=1, device_id=partner, device_id_type=MESH)


def gather(own, other, mix, gu, dt):
    widths = tuple(v.shape[-1] for v in (own, mix, gu, dt))
    halves = [v.reshape(2, ROWS, v.shape[-1]) for v in (mix, gu, dt)]
    shapes = [jax.ShapeDtypeStruct((2, 16, ROWS, widths[0]), BF)]
    shapes += [jax.ShapeDtypeStruct((16, 2, ROWS, w), BF) for w in widths[1:]]
    full = pl.pallas_call(
        functools.partial(gather_kernel, widths),
        out_shape=shapes,
        in_specs=[ANY] * 5,
        out_specs=[ANY] * 4,
        scratch_shapes=[DMA((4,)), DMA((2,)), DMA((4,)), DMA((8, 16)), pltpu.SemaphoreType.REGULAR],
        compiler_params=pltpu.CompilerParams(collective_id=0, has_side_effects=True, vmem_limit_bytes=4 * MIB),
        name="gather_weights",
    )(own, other, *halves)
    return [f.reshape(-1, f.shape[-1]) for f in full]


def add_rows(dst, pieces):
    rows = dst.shape[-2]
    lead = dst.shape[0] if len(dst.shape) == 3 else 1

    def body(i, carry):
        at = pl.ds(pl.multiple_of(i % (rows // 16) * 16, 16), 16)
        k = i // (rows // 16)
        get = (lambda r: r[k, at, :]) if len(dst.shape) == 3 else (lambda r: r[at, :])
        total = get(pieces[0]).astype(F32)
        for p in pieces[1:]:
            total = total + get(p).astype(F32)
        if len(dst.shape) == 3:
            dst[k, at, :] = total.astype(dst.dtype)
        else:
            dst[at, :] = total.astype(dst.dtype)
        return carry

    lax.fori_loop(0, lead * (rows // 16), body, 0)


def scatter_kernel(widths, *refs):
    n = len(widths)
    grads, small = refs[:n], refs[n]
    outs, small_out = refs[n + 1 : 2 * n + 1], refs[2 * n + 1]
    refs = refs[2 * n + 2 :]
    per = 11
    buffers = [refs[a * per : (a + 1) * per] for a in range(n)]
    small_in, small_acc, load_sem, recv_sem, send_sem, small_send, small_recv = refs[n * per :]
    s, y, x, z = place()

    def device(yx):
        return (s, yx[0] * 4 + yx[1], z)

    peers = [[device(near(k, y, x, j)) for j in (1, 2, 3)] for k in (0, 1)]
    peers.append([(s, y * 4 + x, (z + j) % 4) for j in (1, 2, 3)])
    greet([p for group in peers for p in group])

    def line(a, h, yx):
        return grads[a].at[yx[0], :, h] if h == 0 else grads[a].at[:, yx[1], h]

    pairs = [(a, h) for a in range(n) for h in (0, 1)]
    loads = {}
    for a, h in pairs:
        t_up, t_dn, total = (buffers[a][i].at[h] for i in (4, 5, 6))
        c, w = cut(widths[a]), widths[a]
        r1_up, r1_dn, r2_up, r2_dn = (buffers[a][i].at[h] for i in (0, 1, 2, 3))
        first = 1 - h
        up, dn, far = (near(first, y, x, step) for step in (1, -1, 2))
        sem = recv_sem.at[a * 2 + h]
        sends = [
            remote(line(a, h, far).at[:, :, 0:c], r1_up, send_sem.at[a * 2 + h, 0], sem.at[0], device(up)),
            remote(line(a, h, far).at[:, :, c:w], r1_dn, send_sem.at[a * 2 + h, 1], sem.at[1], device(dn)),
            remote(line(a, h, up).at[:, :, c:w], r2_up.at[:, :, c:w], send_sem.at[a * 2 + h, 2], sem.at[2], device(up)),
            remote(line(a, h, dn).at[:, :, 0:c], r2_dn.at[:, :, 0:c], send_sem.at[a * 2 + h, 3], sem.at[3], device(dn)),
        ]
        fetch = [
            pltpu.make_async_copy(line(a, h, up).at[:, :, 0:c], t_up, load_sem.at[a * 2 + h, 0]),
            pltpu.make_async_copy(line(a, h, dn).at[:, :, c:w], t_dn, load_sem.at[a * 2 + h, 1]),
            pltpu.make_async_copy(line(a, h, (y, x)), total, load_sem.at[a * 2 + h, 2]),
        ]
        for copy in sends + fetch:
            copy.start()
        loads[a, h] = (sends, fetch)

    small_acc[...] = small[...]
    for k in range(3):
        hops = []
        for j in range(3):
            hop = remote(small_acc, small_in.at[k * 3 + j], small_send.at[k * 3 + j], small_recv.at[k * 3 + j], peers[k][j])
            hop.start()
            hops.append(hop)
        for hop in hops:
            hop.wait()
        summed = small_acc[...] + small_in[k * 3] + small_in[k * 3 + 1] + small_in[k * 3 + 2]
        if k == 2:
            row = lax.broadcasted_iota(jnp.int32, summed.shape, 0)
            summed = jnp.where(row == 3, small_acc[...], summed)
        small_acc[...] = summed
    small_out[...] = small_acc[...]

    for a, h in pairs:
        t_up, t_dn = (buffers[a][i].at[h] for i in (4, 5))
        c, w = cut(widths[a]), widths[a]
        r1_up, r1_dn, r2_up, r2_dn = (buffers[a][i].at[h] for i in (0, 1, 2, 3))
        first = 1 - h
        up, dn = (near(first, y, x, step) for step in (1, -1))
        sends, fetch = loads[a, h]
        sem = recv_sem.at[a * 2 + h]
        fetch[0].wait()
        sends[0].wait_recv()
        add_rows(t_up, [t_up, r1_up])
        go = remote(t_up, r2_up.at[:, :, 0:c], send_sem.at[a * 2 + h, 4], sem.at[4], device(up))
        go.start()
        fetch[1].wait()
        sends[1].wait_recv()
        add_rows(t_dn, [t_dn, r1_dn])
        back = remote(t_dn, r2_dn.at[:, :, c:w], send_sem.at[a * 2 + h, 5], sem.at[5], device(dn))
        back.start()
        sends += [go, back]

    for a, h in pairs:
        total = buffers[a][6].at[h]
        q1_up, q1_dn, q2_up, q2_dn = (buffers[a][i].at[h] for i in (7, 8, 9, 10))
        c, w = cut(widths[a]), widths[a]
        sends, fetch = loads[a, h]
        sem = recv_sem.at[a * 2 + h]
        fetch[2].wait()
        for copy in sends[2:]:
            copy.wait_recv()
        add_rows(total, [total, buffers[a][2].at[h], buffers[a][3].at[h]])
        own = x if h == 0 else y
        up, dn = (near(h, y, x, step) for step in (1, -1))
        far, i_up, i_dn = ((own + step) % 4 for step in (2, 1, -1))
        more = [
            remote(total.at[far, :, 0:c], q1_up, send_sem.at[a * 2 + h, 6], sem.at[6], device(up)),
            remote(total.at[far, :, c:w], q1_dn, send_sem.at[a * 2 + h, 7], sem.at[7], device(dn)),
            remote(total.at[i_up, :, c:w], q2_up.at[:, c:w], send_sem.at[a * 2 + h, 8], sem.at[8], device(up)),
            remote(total.at[i_dn, :, 0:c], q2_dn.at[:, 0:c], send_sem.at[a * 2 + h, 9], sem.at[9], device(dn)),
        ]
        for copy in more:
            copy.start()
        sends += more

    for a, h in pairs:
        total = buffers[a][6].at[h]
        q1_up, q1_dn, q2_up, q2_dn = (buffers[a][i].at[h] for i in (7, 8, 9, 10))
        c, w = cut(widths[a]), widths[a]
        sends, fetch = loads[a, h]
        sem = recv_sem.at[a * 2 + h]
        own = x if h == 0 else y
        up, dn = (near(h, y, x, step) for step in (1, -1))
        i_up, i_dn = ((own + step) % 4 for step in (1, -1))
        sends[6].wait_recv()
        add_rows(q1_up, [q1_up, total.at[i_up, :, 0:c]])
        go = remote(q1_up, q2_up.at[:, 0:c], send_sem.at[a * 2 + h, 10], sem.at[10], device(up))
        go.start()
        sends[7].wait_recv()
        add_rows(q1_dn, [q1_dn, total.at[i_dn, :, c:w]])
        back = remote(q1_dn, q2_dn.at[:, c:w], send_sem.at[a * 2 + h, 11], sem.at[11], device(dn))
        back.start()
        sends += [go, back]

    for a, h in pairs:
        total = buffers[a][6].at[h]
        sends, fetch = loads[a, h]
        own = x if h == 0 else y
        for copy in sends[8:]:
            copy.wait_recv()
        add_rows(outs[a].at[h], [total.at[own], buffers[a][9].at[h], buffers[a][10].at[h]])
    for a, h in pairs:
        for copy in loads[a, h][0]:
            copy.wait_send()


def scatter(grads, small):
    widths = tuple(g.shape[-1] for g in grads)
    scratch = []
    for w in widths:
        c = cut(w)
        scratch += [pltpu.VMEM((2, 4, ROWS, k), BF) for k in (c, w - c, w, w, c, w - c, w)]
        scratch += [pltpu.VMEM((2, ROWS, k), BF) for k in (c, w - c, w, w)]
    n = len(grads)
    scratch += [pltpu.VMEM((9,) + small.shape, F32), pltpu.VMEM(small.shape, F32)]
    scratch += [DMA((2 * n, 3)), DMA((2 * n, 12)), DMA((2 * n, 12)), DMA((9,)), DMA((9,))]
    return pl.pallas_call(
        functools.partial(scatter_kernel, widths),
        out_shape=[jax.ShapeDtypeStruct((2, ROWS, w), F32) for w in widths] + [jax.ShapeDtypeStruct(small.shape, F32)],
        in_specs=[ANY] * n + [VM],
        out_specs=[VM] * (n + 1),
        scratch_shapes=scratch,
        compiler_params=pltpu.CompilerParams(collective_id=1, has_side_effects=True, vmem_limit_bytes=56 * MIB),
        name="sum_gradients",
    )(*grads, small)


def swap_kernel(mixer, small, own, other, small_own, small_other, sem):
    s, y, x, z = place()
    partner = (1 - s, y * 4 + x, z)
    greet([partner])
    copies = [
        remote(mixer.at[1 - s], other, sem.at[0], sem.at[1], partner),
        remote(small, small_other, sem.at[2], sem.at[3], partner),
    ]
    for copy in copies:
        copy.start()
    own[...] = mixer[s]
    small_own[...] = small[...]
    for copy in copies:
        copy.wait()


def swap_halves(mixer, small):
    half = jax.ShapeDtypeStruct(mixer.shape[1:], F32)
    rows = jax.ShapeDtypeStruct(small.shape, F32)
    return pl.pallas_call(
        swap_kernel,
        out_shape=[half, half, rows, rows],
        in_specs=[VM, VM],
        out_specs=[VM] * 4,
        scratch_shapes=[DMA((4,))],
        compiler_params=pltpu.CompilerParams(collective_id=2, has_side_effects=True),
        name="swap_halves",
    )(mixer, small)


def dot(a, b):
    return jnp.dot(a, b, preferred_element_type=F32)


def dot_bt(a, b):
    return lax.dot_general(a, b, (((1,), (1,)), ((), ())), preferred_element_type=F32)


def dot_at(a, b):
    return lax.dot_general(a, b, (((0,), (0,)), ((), ())), preferred_element_type=F32)


def norm_back(values, gain, grad):
    factor = root(values)
    weighted = grad * gain
    grad_in = factor * weighted - values * (factor * factor * factor) * jnp.mean(values * weighted, axis=-1, keepdims=True)
    return grad_in, jnp.sum(grad * values * factor, axis=0, keepdims=True)


def lanes(i, size=128):
    return pl.ds(pl.multiple_of(i * size, size), size)


def times(count, body):
    def step(i, carry):
        body(i)
        return carry

    lax.fori_loop(0, count, step, 0)


def chain_kernel(
    own,
    seg_col,
    seg_row,
    gains,
    taps,
    qk_gains,
    tables,
    w_mixer,
    w_mix,
    w_gate,
    w_down,
    result,
    grad_in,
    normed,
    grad_proj,
    mixer,
    ffn_in,
    grad_pair,
    hidden,
    top,
    grad_mid,
    small,
    sent,
    part,
    inbox,
    middle,
    grad_chunk,
    proj,
    mixed,
    gate_up,
    heads,
    soft,
    turns,
    grad_heads,
    send_sem,
    recv_sem,
    give_sem,
    ready,
):
    s, y, x, z = place()
    d = y * 4 + x
    mates = [(s, d, (z + j) % 4) for j in (1, 2, 3)]
    partner = (1 - s, d, z)
    tokens, width = own.shape
    channels = mixer.shape[1]
    padded = hidden.shape[1]
    head = 64
    blocks = tokens // MBT
    barrier = pltpu.get_barrier_semaphore()

    def rows(k):
        return pl.ds(pl.multiple_of(k % 4 * CHUNK, CHUNK), CHUNK)

    mine = rows(z)

    def spread(a, b, depth, start=0):
        def body(j):
            part[:, lanes(j, 256)] = dot_bt(a[:, 0:depth], b[lanes(j, 256), 0:depth]).astype(BF)

        times(width // 256, body)

    def sum_over_mates(phase, full, work):
        hops = []
        for j in (1, 2, 3):
            sems = (send_sem.at[phase, j - 1], recv_sem.at[phase, j - 1])
            hop = remote(part.at[rows(z + j)], inbox.at[phase, j - 1], *sems, mates[j - 1])
            hop.start()
            hops.append(hop)
        total = part[mine, :].astype(F32)
        for j, hop in enumerate(hops):
            hop.wait_recv()
            total = total + inbox[phase, j].astype(F32)
        full[mine, :] = work(total).astype(BF)
        for j in (1, 2, 3):
            sems = (send_sem.at[phase, 2 + j], recv_sem.at[phase, 2 + j])
            hop = remote(full.at[mine], full.at[mine], *sems, mates[j - 1])
            hop.start()
            hops.append(hop)
        for j in (1, 2, 3):
            arrived(full.at[rows(z - j)], recv_sem.at[phase, 2 + j])
        for hop in hops:
            hop.wait_send()

    def norm_rows(src):
        def body(i):
            values = src[rows(i), :].astype(F32)
            normed[rows(i), :] = (values * root(values) * gains[0:1, :]).astype(BF)

        times(tokens // CHUNK, body)

    def after_mixer(src):
        def work(total):
            value = src[mine, :].astype(F32) + total
            middle[...] = value
            return value * root(value) * gains[1:2, :]

        spread(mixer, w_mix, channels)
        sum_over_mates(0, ffn_in, work)

    def ffn_forward():
        def body(j):
            gate = dot(ffn_in[...], w_gate[:, lanes(j, 256)])
            up = dot(ffn_in[...], w_gate[:, pl.ds(pl.multiple_of(padded + j * 256, 256), 256)])
            gate_up[0, :, lanes(j, 256)] = gate
            gate_up[1, :, lanes(j, 256)] = up
            hidden[:, lanes(j, 256)] = (gate * jax.nn.sigmoid(gate) * up).astype(BF)

        times(padded // 256, body)

    def ffn_out():
        spread(hidden, w_down, padded)
        sum_over_mates(1, result, lambda total: middle[...] + total)

    def ffn_backward():
        def body(j):
            grad = dot(top[...], w_down[:, lanes(j, 256)])
            gate, up = gate_up[0, :, lanes(j, 256)], gate_up[1, :, lanes(j, 256)]
            sig = jax.nn.sigmoid(gate)
            grad_pair[:, lanes(j, 256)] = (grad * up * sig * (1.0 + gate * (1.0 - sig))).astype(BF)
            grad_pair[:, pl.ds(pl.multiple_of(padded + j * 256, 256), 256)] = (grad * gate * sig).astype(BF)

        times(padded // 256, body)

        def work(total):
            grad, small[1:2, :] = norm_back(middle[...], gains[1:2, :], total)
            grad = top[mine, :].astype(F32) + grad
            grad_chunk[...] = grad
            return grad

        spread(grad_pair, w_gate, 2 * padded)
        sum_over_mates(2, grad_mid, work)

    def mixer_back(src, depth):
        def work(total):
            grad, small[0:1, :] = norm_back(src[mine, :].astype(F32), gains[0:1, :], total)
            return grad_chunk[...] + grad

        spread(grad_proj, w_mixer, depth)
        sum_over_mates(3, grad_in, work)

    def project(count):
        def body(j):
            proj[:, lanes(j)] = dot(normed[...], w_mixer[:, lanes(j)])

        times(count, body)

    def greet_mates():
        for mate in mates:
            pl.semaphore_signal(barrier, inc=1, device_id=mate, device_id_type=MESH)

    small[...] = jnp.zeros_like(small)


    def same(lag):
        seg = seg_col[...] + jnp.zeros((tokens, 128), jnp.int32)
        row = lax.broadcasted_iota(jnp.int32, (tokens, 128), 0)
        return jnp.where((seg == pltpu.roll(seg, lag, 0)) & (row % MBT >= lag), 1.0, 0.0)

    def pieces(j):
        at = [slice(i * channels + j * 128, i * channels + (j + 1) * 128) for i in range(3)]
        return [proj[:, a] for a in at], at

    def first():
        greet_mates()
        pl.semaphore_signal(barrier, inc=1, device_id=partner, device_id_type=MESH)
        norm_rows(own)
        project(3 * channels // 128)
        for j in range(channels // 128):
            (b, c, e), _ = pieces(j)
            at = slice(j * 128, (j + 1) * 128)
            product = b * e
            total = taps[0:1, at] * product
            for lag in (1, 2):
                total = total + taps[lag : lag + 1, at] * (pltpu.roll(product, lag, 0) * same(lag))
            mixed[:, at] = total
            mixer[:, at] = (c * total).astype(BF)
        pl.semaphore_wait(barrier, 3)
        after_mixer(own)
        ffn_forward()
        ffn_out()
        pl.semaphore_wait(ready, 1)
        give = remote(result, sent, give_sem.at[0], give_sem.at[1], partner)
        give.start()
        give.wait_send()
        arrived(top, give_sem.at[3])
        ffn_backward()
        for j in range(channels // 128):
            (b, c, e), at = pieces(j)
            lane = slice(j * 128, (j + 1) * 128)
            grad_y = dot(grad_mid[...], w_mix[:, lane])
            product = b * e
            grad_mixed = grad_y * c
            grad_product = taps[0:1, lane] * grad_mixed
            sums = [jnp.sum(grad_mixed * product, axis=0, keepdims=True)]
            for lag in (1, 2):
                masked = grad_mixed * same(lag)
                sums.append(jnp.sum(masked * pltpu.roll(product, lag, 0), axis=0, keepdims=True))
                grad_product = grad_product + taps[lag : lag + 1, lane] * pltpu.roll(masked, tokens - lag, 0)
            for k in range(3):
                small[3:4, at[k]] = sums[k]
            grad_proj[:, at[0]] = (grad_product * e).astype(BF)
            grad_proj[:, at[1]] = (grad_y * mixed[:, lane]).astype(BF)
            grad_proj[:, at[2]] = (grad_product * b).astype(BF)
        mixer_back(own, 3 * channels)


    half = channels // 3
    lane_of = lax.broadcasted_iota(jnp.int32, (1, half), 1)
    keep = [jnp.where(lane_of // head == k, 1.0, 0.0) for k in (0, 1)]

    def per_head(values):
        first_sum = jnp.sum(values * keep[0], axis=-1, keepdims=True)
        second_sum = jnp.sum(values * keep[1], axis=-1, keepdims=True)
        return (first_sum * keep[0] + second_sum * keep[1]) * (1.0 / head)

    def across(values):
        low = lane_of % head < head // 2
        return jnp.where(low, pltpu.roll(values, half - head // 2, 1), pltpu.roll(values, head // 2, 1))

    def allowed(block):
        at = slice(block * MBT, (block + 1) * MBT)
        t = lax.broadcasted_iota(jnp.int32, (MBT, MBT), 0)
        u = lax.broadcasted_iota(jnp.int32, (MBT, MBT), 1)
        return jnp.where((seg_col[at, :] == seg_row[:, at]) & (u <= t), 1.0, 0.0)

    def turn_tables():
        for block in range(blocks):
            at = slice(block * MBT, (block + 1) * MBT)
            offset = jnp.sum(allowed(block), axis=1, keepdims=True) - 1.0
            column = lax.broadcasted_iota(jnp.int32, (MBT, MBT), 1).astype(F32)
            pick = jnp.where(column == offset, 1.0, 0.0).astype(BF)
            for k in (0, 1):
                turns[k, at, :] = dot(pick, tables[k, 0]) + dot(pick, tables[k, 1]) + dot(pick, tables[k, 2])

    inv_sqrt = head ** (-0.5)
    combos = [(block, g, k) for block in range(blocks) for g in range(3) for k in (0, 1)]

    def masked(i, block, k):
        at = slice(block * MBT, (block + 1) * MBT)
        return heads[i, at, :] * keep[k].astype(BF)

    def second():
        greet_mates()
        pl.semaphore_wait(barrier, 4)
        pl.semaphore_signal(ready, inc=1, device_id=partner, device_id_type=MESH)
        turn_tables()
        top[...] = own[...]
        grad_proj[:, 5 * half :] = jnp.zeros((tokens, grad_proj.shape[1] - 5 * half), BF)
        arrived(sent, give_sem.at[1])
        norm_rows(sent)
        project(5)
        for i in range(4):
            raw = proj[:, i * half : (i + 1) * half]
            gain = qk_gains[min(i // 3, 1) : min(i // 3, 1) + 1, :]
            value = raw * lax.rsqrt(per_head(raw * raw) + epsilon) * gain
            heads[i] = (value * turns[0] + across(value) * turns[1]).astype(BF)
        heads[4] = proj[:, 4 * half : 5 * half].astype(BF)
        for block in range(blocks):
            at = slice(block * MBT, (block + 1) * MBT)
            ok = allowed(block)
            for g in range(3):
                attended = jnp.zeros((MBT, half), F32)
                for k in (0, 1):
                    score = dot_bt(heads[g, at, :], masked(3, block, k)) * inv_sqrt
                    score = jnp.where(ok > 0.0, score, neg_large)
                    power = jnp.exp(score - jnp.max(score, axis=-1, keepdims=True))
                    weight = power / jnp.sum(power, axis=-1, keepdims=True)
                    soft[(block * 3 + g) * 2 + k] = weight
                    attended = attended + dot(weight.astype(BF), masked(4, block, k))
                mixer[at, g * half : (g + 1) * half] = attended.astype(BF)
        after_mixer(sent)
        ffn_forward()
        ffn_backward()
        for block in range(blocks):
            at = slice(block * MBT, (block + 1) * MBT)
            grad_key = jnp.zeros((MBT, half), F32)
            grad_value = jnp.zeros((MBT, half), F32)
            for g in range(3):
                grad_att = dot(grad_mid[at, :], w_mix[:, g * half : (g + 1) * half]).astype(BF)
                grad_query = jnp.zeros((MBT, half), F32)
                for k in (0, 1):
                    weight = soft[(block * 3 + g) * 2 + k]
                    grad_soft = dot_bt(grad_att, masked(4, block, k))
                    delta = jnp.sum(weight * grad_soft, axis=-1, keepdims=True)
                    grad_score = (weight * (grad_soft - delta)).astype(BF)
                    grad_query = grad_query + dot(grad_score, masked(3, block, k))
                    grad_key = grad_key + dot_at(grad_score, masked(g, block, k))
                    grad_value = grad_value + dot_at(weight.astype(BF), grad_att * keep[k].astype(BF))
                grad_heads[g, at, :] = grad_query * inv_sqrt
            grad_heads[3, at, :] = grad_key * inv_sqrt
            grad_proj[at, 4 * half : 5 * half] = grad_value.astype(BF)
        gain_rows = [jnp.zeros((1, half), F32)] * 2
        for i in range(4):
            raw = proj[:, i * half : (i + 1) * half]
            which = min(i // 3, 1)
            gain = qk_gains[which : which + 1, :]
            grad = grad_heads[i]
            grad = grad * turns[0] - across(grad) * turns[1]
            factor = lax.rsqrt(per_head(raw * raw) + epsilon)
            weighted = grad * gain
            gain_rows[which] = gain_rows[which] + jnp.sum(grad * raw * factor, axis=0, keepdims=True)
            grad = factor * weighted - raw * (factor * factor * factor) * per_head(raw * weighted)
            grad_proj[:, i * half : (i + 1) * half] = grad.astype(BF)
        small[2:3, 0:half] = gain_rows[0]
        small[2:3, half : 2 * half] = gain_rows[1]
        mixer_back(sent, 5 * half)
        give = remote(grad_in, top, give_sem.at[2], give_sem.at[3], partner)
        give.start()
        ffn_out()
        give.wait_send()

    pl.when(s == 0)(first)
    pl.when(s == 1)(second)


def rope_parts(head_size):
    frequency = rope_base ** (-np.arange(head_size // 2, dtype=np.float64) * 2.0 / head_size)
    angles = (np.arange(MBT, dtype=np.float32)[:, None] * frequency.astype(np.float32)[None, :]).astype(np.float32)
    cosine, sine = np.cos(angles.astype(np.float64)), np.sin(angles.astype(np.float64))
    both = (np.concatenate([cosine] * 4, axis=1), np.concatenate([-sine, sine, -sine, sine], axis=1))
    parts = []
    for table in both:
        left = table.astype(np.float32)
        for _ in range(3):
            piece = left.astype(jnp.bfloat16)
            parts.append(piece)
            left = left - piece.astype(np.float32)
    return jnp.asarray(np.stack(parts).reshape(2, 3, MBT, 2 * head_size))


def chain(own, segments, gains, taps, qk_gains, w_mixer, w_mix, w_gate, w_down):
    tokens, width = own.shape
    channels, padded = w_mix.shape[1], w_down.shape[1]
    shape = jax.ShapeDtypeStruct
    rows = shape((tokens, width), BF)
    outs = [rows, rows, rows, shape((tokens, 3 * channels), BF), shape((tokens, channels), BF), rows]
    outs += [shape((tokens, 2 * padded), BF), shape((tokens, padded), BF), rows, rows, shape((8, width), F32)]
    scratch = [
        pltpu.VMEM((tokens, width), BF),
        pltpu.VMEM((tokens, width), BF),
        pltpu.VMEM((4, 3, CHUNK, width), BF),
        pltpu.VMEM((CHUNK, width), F32),
        pltpu.VMEM((CHUNK, width), F32),
        pltpu.VMEM((tokens, 3 * channels), F32),
        pltpu.VMEM((tokens, channels), F32),
        pltpu.VMEM((2, tokens, padded), F32),
        pltpu.VMEM((5, tokens, 128), BF),
        pltpu.VMEM((6 * tokens // MBT, MBT, MBT), F32),
        pltpu.VMEM((2, tokens, 128), F32),
        pltpu.VMEM((4, tokens, 128), F32),
        DMA((4, 6)),
        DMA((4, 6)),
        DMA((4,)),
        pltpu.SemaphoreType.REGULAR,
    ]
    return pl.pallas_call(
        chain_kernel,
        out_shape=outs,
        in_specs=[VM] * 11,
        out_specs=[VM] * len(outs),
        scratch_shapes=scratch,
        compiler_params=pltpu.CompilerParams(collective_id=3, has_side_effects=True, vmem_limit_bytes=CHAIN_VMEM * MIB),
        name="both_blocks",
    )(own, segments[:, None], segments[None, :], gains, taps, qk_gains, rope_parts(64), w_mixer, w_mix, w_gate, w_down)


def local(ends, segment_ids, norm_gains, conv_in, conv_kernel, qkv_weight, qk_gains, mix_out, gate_up, down):
    is_first = lax.axis_index(SEC) == 0
    width = ends.shape[2]
    channels = mix_out.shape[1]
    hidden = gate_up.shape[3]
    padded = (hidden + 255) // 256 * 256
    kv, group, head = qkv_weight.shape[1], qkv_weight.shape[2] - 2, qkv_weight.shape[3]
    qkv_width = kv * (group + 2) * head
    taps = conv_kernel.shape[0]
    spare = ((0, 0), (0, padded - hidden))

    conv_rows = conv_in.reshape(ROWS, taps * channels)
    qkv_rows = qkv_weight.transpose(0, 2, 1, 3).reshape(ROWS, qkv_width)
    qkv_rows = jnp.pad(qkv_rows, ((0, 0), (0, taps * channels - qkv_width)))
    mix_rows = mix_out[0].T
    mix_turned = mix_rows.reshape(2 * ROWS, kv, group, head).transpose(0, 2, 1, 3).reshape(2 * ROWS, channels)
    gate_rows = jnp.pad(gate_up[0], ((0, 0),) + spare).reshape(2 * ROWS, 2 * padded)
    down_rows = jnp.pad(down[0].T, spare)
    w_mixer, w_mix, w_gate, w_down = gather(
        jnp.where(is_first, conv_rows, qkv_rows),
        jnp.where(is_first, qkv_rows, conv_rows),
        jnp.where(is_first, mix_rows, mix_turned),
        gate_rows,
        down_rows,
    )
    gains = jnp.concatenate([qk_gains, qk_gains], axis=1)
    result, grad_in, normed, grad_proj, mixer, ffn_in, grad_pair, hidden_rows, top, grad_mid, small = chain(
        ends[0], segment_ids, norm_gains[0], conv_kernel, gains, w_mixer, w_mix, w_gate, w_down
    )

    def product(a, b):
        return dot_at(a, b).astype(BF)

    def view(grad):
        return grad.reshape(4, 4, 2, ROWS, grad.shape[-1])

    mixer_view = product(normed, grad_proj).reshape(2, 4, 4, ROWS, -1).transpose(1, 2, 0, 3, 4)
    sum_gate, sum_down, sum_mix, sum_mixer, small_sum = scatter(
        [view(product(ffn_in, grad_pair)), view(product(top, hidden_rows)), view(product(grad_mid, mixer)), mixer_view], small
    )
    mixer_own, mixer_other, small_own, small_other = swap_halves(sum_mixer, small_sum)
    conv_grad = jnp.where(is_first, mixer_own, mixer_other)
    qkv_grad = jnp.where(is_first, mixer_other, mixer_own)[:, :qkv_width].reshape(ROWS, group + 2, kv, head)
    of_first = jnp.where(is_first, small_own, small_other)
    of_second = jnp.where(is_first, small_other, small_own)
    mix_grad = sum_mix.reshape(2 * ROWS, channels)
    mix_back = mix_grad.reshape(2 * ROWS, group, kv, head).transpose(0, 2, 1, 3).reshape(2 * ROWS, channels)
    return (
        result[None],
        grad_in.astype(F32)[None],
        small_own[None, 0:2],
        conv_grad.reshape(conv_in.shape),
        of_first[3, : taps * channels].reshape(taps, channels),
        qkv_grad.transpose(0, 2, 1, 3),
        of_second[2, : 4 * head].reshape(2, 2, head).sum(1),
        jnp.where(is_first, mix_grad, mix_back).T[None],
        sum_gate.reshape(2 * ROWS, 2, padded)[None, :, :, :hidden],
        sum_down.reshape(2 * ROWS, padded)[:, :hidden].T[None],
    )


def solution(mesh):
    dims = (
        P(SEC, DP, None),
        P(DP),
        P(SEC, None, None),
        P((SEC, DP), None, TEN),
        P(None, TEN),
        P((SEC, DP), TEN, None, None),
        P(),
        P(SEC, TEN, DP),
        P(SEC, DP, None, TEN),
        P(SEC, TEN, DP),
    )
    results = (dims[0], dims[0], dims[2], dims[3], dims[4], dims[5], dims[6], dims[7], dims[8], dims[9])
    return jax.shard_map(local, mesh=mesh, in_specs=dims, out_specs=results, check_vma=False)
```

```python
import functools

import jax
import jax.numpy as jnp
import numpy as np
from jax import lax
from jax.experimental import pallas as pl
from jax.experimental.pallas import tpu as pltpu
from jax.sharding import PartitionSpec as P

SEC, DP, TEN = "section", "dp", "tensor"
MESH = pl.DeviceIdType.MESH
F32, BF = jnp.float32, jnp.bfloat16
ANY = pl.BlockSpec(memory_space=pl.ANY)
VM = pl.BlockSpec(memory_space=pltpu.VMEM)
DMA = pltpu.SemaphoreType.DMA
MIB = 1 << 20

MBT = 128
ROWS = 48
CHUNK = 64
HEAD = 64
epsilon = 1e-05
rope_base = 1000000.0
neg_large = -1e30

HOME = (2, 2, 3, 1, 0)


def place():
    d = lax.axis_index(DP)
    return lax.axis_index(SEC), d // 4, d % 4, lax.axis_index(TEN)


def near(axis, y, x, step):
    return (y, (x + step) % 4) if axis == 0 else ((y + step) % 4, x)


def remote(src, dst, send_sem, recv_sem, device):
    return pltpu.make_async_remote_copy(
        src_ref=src, dst_ref=dst, send_sem=send_sem, recv_sem=recv_sem, device_id=device, device_id_type=MESH
    )


def arrived(ref, sem):
    pltpu.make_async_copy(ref, ref, sem).wait()


def cut(columns):
    return (columns // 128 + 1) // 2 * 128


def root(values):
    return lax.rsqrt(jnp.mean(values * values, axis=-1, keepdims=True) + epsilon)


def dot(a, b):
    return jnp.dot(a, b, preferred_element_type=F32)


def dot_bt(a, b):
    return lax.dot_general(a, b, (((1,), (1,)), ((), ())), preferred_element_type=F32)


def dot_at(a, b):
    return lax.dot_general(a, b, (((0,), (0,)), ((), ())), preferred_element_type=F32)


def norm_back(values, gain, grad):
    factor = root(values)
    weighted = grad * gain
    grad_in = factor * weighted - values * (factor * factor * factor) * jnp.mean(values * weighted, axis=-1, keepdims=True)
    return grad_in, jnp.sum(grad * values * factor, axis=0, keepdims=True)


def lanes(i, size=128, start=0):
    return pl.ds(pl.multiple_of(start + i * size, 128), size)


def times(count, body):
    def step(i, carry):
        body(i)
        return carry

    lax.fori_loop(0, count, step, 0)


def matrix(ref, columns):
    value = ref[:, :, columns]
    return value.reshape(value.shape[0] * value.shape[1], value.shape[2])


def add_rows(dst, pieces):
    rows = dst.shape[-2]
    three = len(dst.shape) == 3
    kind = BF if len(pieces) == 2 else F32

    def body(i):
        at = pl.ds(pl.multiple_of(i % (rows // 16) * 16, 16), 16)
        k = i // (rows // 16)
        get = (lambda r: r[k, at, :]) if three else (lambda r: r[at, :])
        total = get(pieces[0]).astype(kind)
        for p in pieces[1:]:
            total = total + get(p).astype(kind)
        if three:
            dst[k, at, :] = total.astype(dst.dtype)
        else:
            dst[at, :] = total.astype(dst.dtype)

    times((dst.shape[0] if three else 1) * (rows // 16), body)


class Gather:
    def __init__(self, weights, send_sem, recv_sem):
        self.weights, self.send_sem, self.recv_sem = weights, send_sem, recv_sem
        self.s, self.y, self.x, self.z = place()

    def block(self, a, h, yx):
        b = yx[0] * 4 + yx[1]
        return self.weights[a].at[h * 16 + b if a == 0 else b * 2 + h]

    def send(self, a, h, yx, lo, hi, to):
        ref = self.block(a, h, yx)
        if (lo, hi) != (0, ref.shape[-1]):
            ref = ref.at[:, lo:hi]
        recv = self.recv_sem.at[a * 2 + h, yx[0] * 4 + yx[1]]
        remote(ref, ref, self.send_sem.at[a], recv, (self.s, to[0] * 4 + to[1], self.z)).start()

    def wait(self, a, h, yx):
        arrived(self.block(a, h, yx), self.recv_sem.at[a * 2 + h, yx[0] * 4 + yx[1]])

    def near(self, axis, step):
        return near(axis, self.y, self.x, step)

    def start(self, arrays):
        for axis_of in (lambda h: h, lambda h: 1 - h):
            for a in arrays:
                for h in (0, 1):
                    for step in (1, -1):
                        w = self.weights[a].shape[-1]
                        self.send(a, h, (self.y, self.x), 0, w, self.near(axis_of(h), step))

    def spread(self, arrays):
        for a in arrays:
            w = self.weights[a].shape[-1]
            c = cut(w)
            for h in (0, 1):
                for step, lo, hi in ((1, 0, c), (-1, c, w)):
                    src = self.near(h, -step)
                    self.wait(a, h, src)
                    self.send(a, h, src, lo, hi, self.near(h, step))
                    for on in (1, -1):
                        self.send(a, h, src, 0, w, self.near(1 - h, on))
        for a in arrays:
            w = self.weights[a].shape[-1]
            for h in (0, 1):
                far = self.near(h, 2)
                self.wait(a, h, far)
                for on in (1, -1):
                    self.send(a, h, far, 0, w, self.near(1 - h, on))

    def relay(self, a):
        w = self.weights[a].shape[-1]
        c = cut(w)
        for h in (0, 1):

            def body(j, h=h):
                line = self.near(h, j)
                for step, lo, hi in ((1, 0, c), (-1, c, w)):
                    src = near(1 - h, line[0], line[1], -step)
                    self.wait(a, h, src)
                    self.send(a, h, src, lo, hi, self.near(1 - h, step))

            times(4, body)

    def last(self, a):
        for h in (0, 1):

            def body(j, h=h):
                line = self.near(h, j)
                self.wait(a, h, near(1 - h, line[0], line[1], 2))

            times(4, body)

    def sent(self, a):
        arrived(self.weights[a].at[0:30], self.send_sem.at[a])


class Scatter:
    def __init__(self, grads, weights, widths, extras, load_sem, recv_sem, send_sem, free):
        self.grads, self.weights, self.widths, self.extras = grads, weights, widths, extras
        self.load_sem, self.recv_sem, self.send_sem, self.free = load_sem, recv_sem, send_sem, free
        self.s, self.y, self.x, self.z = place()
        self.claimed = set()
        self.loads = {}

    def device(self, yx):
        return (self.s, yx[0] * 4 + yx[1], self.z)

    def near(self, axis, step):
        return near(axis, self.y, self.x, step)

    def release(self, home):
        for axis in (0, 1):
            for step in (1, -1):
                to = self.device(self.near(axis, step))
                pl.semaphore_signal(self.free.at[home], inc=1, device_id=to, device_id_type=MESH)

    def line(self, a, h, yx):
        if a == 4:
            return self.grads[a].at[h, yx[0]] if h == 0 else self.grads[a].at[h, :, yx[1]]
        return self.grads[a].at[yx[0], :, h] if h == 0 else self.grads[a].at[:, yx[1], h]

    def room(self, a, h, lo, hi):
        ref = self.weights[HOME[a]].at[16 * h + lo : 16 * h + hi]
        if a < 2:
            ref = ref.at[:, :, a * self.widths[a] : (a + 1) * self.widths[a]]
        return ref

    def move(self, a, h, i, src, dst, to):
        remote(src, dst, self.send_sem.at[a * 2 + h], self.recv_sem.at[a * 2 + h, i], self.device(to)).start()

    def load(self, a, h, i, src, dst):
        copy = pltpu.make_async_copy(src, dst, self.load_sem.at[a * 2 + h, i])
        copy.start()
        self.loads[a, h, i] = copy

    def begin(self, a, h):
        if HOME[a] not in self.claimed:
            pl.semaphore_wait(self.free.at[HOME[a]], 4)
            self.claimed.add(HOME[a])
        up, dn, far = (self.near(1 - h, step) for step in (1, -1, 2))
        self.move(a, h, 0, self.line(a, h, far).at[0:2], self.room(a, h, 0, 2), up)
        self.move(a, h, 0, self.line(a, h, far).at[2:4], self.room(a, h, 2, 4), dn)
        self.load(a, h, 0, self.line(a, h, up).at[0:2], self.room(a, h, 12, 14))
        self.load(a, h, 1, self.line(a, h, dn).at[2:4], self.room(a, h, 14, 16))

    def pass_on(self, a, h):
        up, dn = (self.near(1 - h, step) for step in (1, -1))
        self.move(a, h, 1, self.line(a, h, up).at[2:4], self.room(a, h, 6, 8), up)
        self.move(a, h, 1, self.line(a, h, dn).at[0:2], self.room(a, h, 8, 10), dn)
        self.loads[a, h, 0].wait()
        self.loads[a, h, 1].wait()
        arrived(self.room(a, h, 0, 4), self.recv_sem.at[a * 2 + h, 0])
        mine = self.room(a, h, 12, 16)
        add_rows(mine, [mine, self.room(a, h, 0, 4)])
        self.move(a, h, 1, self.room(a, h, 12, 14), self.room(a, h, 4, 6), up)
        self.move(a, h, 1, self.room(a, h, 14, 16), self.room(a, h, 10, 12), dn)
        self.load(a, h, 2, self.line(a, h, (self.y, self.x)), self.room(a, h, 0, 4))

    def own(self, h):
        return self.x if h == 0 else self.y

    def turn(self, a, h):
        w = self.widths[a]
        c = cut(w)
        self.loads[a, h, 2].wait()
        arrived(self.room(a, h, 4, 12), self.recv_sem.at[a * 2 + h, 1])
        total, extra = self.room(a, h, 0, 4), self.extras[a].at[h]
        add_rows(total, [total, self.room(a, h, 4, 8), self.room(a, h, 8, 12)])
        up, dn = (self.near(h, step) for step in (1, -1))
        far, i_up, i_dn = ((self.own(h) + step) % 4 for step in (2, 1, -1))
        self.move(a, h, 2, total.at[far, :, 0:c], extra.at[0, :, 0:c], up)
        self.move(a, h, 2, total.at[far, :, c:w], extra.at[0, :, c:w], dn)
        self.move(a, h, 3, total.at[i_up, :, c:w], extra.at[1, :, c:w], up)
        self.move(a, h, 3, total.at[i_dn, :, 0:c], extra.at[2, :, 0:c], dn)

    def pass_back(self, a, h):
        w = self.widths[a]
        c = cut(w)
        total, extra = self.room(a, h, 0, 4), self.extras[a].at[h]
        up, dn = (self.near(h, step) for step in (1, -1))
        i_up, i_dn = ((self.own(h) + step) % 4 for step in (1, -1))
        arrived(extra.at[0], self.recv_sem.at[a * 2 + h, 2])
        lo, hi = extra.at[0, :, 0:c], extra.at[0, :, c:w]
        add_rows(lo, [lo, total.at[i_up, :, 0:c]])
        self.move(a, h, 3, lo, extra.at[1, :, 0:c], up)
        add_rows(hi, [hi, total.at[i_dn, :, c:w]])
        self.move(a, h, 3, hi, extra.at[2, :, c:w], dn)

    def finish(self, a, h, out):
        total, extra = self.room(a, h, 0, 4), self.extras[a].at[h]
        arrived(extra.at[1:3], self.recv_sem.at[a * 2 + h, 3])
        add_rows(out, [total.at[self.own(h)], extra.at[1], extra.at[2]])

    def sent(self, a, h):
        arrived(self.room(a, h, 0, 15), self.send_sem.at[a * 2 + h])


def blocks_kernel(
    own,
    seg_col,
    seg_row,
    gains,
    taps,
    qk_gains,
    tables,
    shard_mixer,
    shard_other,
    shard_mix,
    shard_gate,
    shard_down,
    result,
    grad_in,
    sum_gate,
    sum_up,
    sum_down,
    sum_mix,
    mixer_own,
    mixer_other,
    small,
    small_other,
    grad_gate,
    grad_up,
    grad_down,
    grad_mix,
    grad_mixer,
    w_mixer,
    w_mix,
    w_gate,
    w_down,
    x_gate,
    x_up,
    x_down,
    x_mix,
    x_mixer,
    stage,
    stage_mixer,
    turned,
    normed,
    grad_proj,
    mixer,
    ffn_in,
    grad_pair,
    hidden,
    top,
    grad_mid,
    sent,
    part,
    late_part,
    inbox,
    middle,
    grad_chunk,
    proj,
    mixed,
    gate_up,
    heads,
    soft,
    turns,
    grad_heads,
    mixer_give,
    small_in,
    copy_sem,
    gather_send,
    gather_recv,
    go,
    send_sem,
    recv_sem,
    give_sem,
    stage_sem,
    load_sem,
    sum_recv,
    sum_send,
    free,
    small_send,
    small_recv,
):
    s, y, x, z = place()
    d = y * 4 + x
    mates = [(s, d, (z + j) % 4) for j in (1, 2, 3)]
    partner = (1 - s, d, z)
    plane = [[(s, v[0] * 4 + v[1], z) for v in (near(k, y, x, j) for j in (1, 2, 3))] for k in (0, 1)]
    tokens, width = own.shape
    channels = mixer.shape[1]
    padded = hidden.shape[1]
    blocks = tokens // MBT
    weights = (w_mixer, w_mix, w_gate, w_down)
    gather = Gather(weights, gather_send, gather_recv)
    grads = (grad_gate, grad_up, grad_down, grad_mix, grad_mixer)
    widths = (padded, padded, padded, channels, 3 * channels)
    extras = (x_gate, x_up, x_down, x_mix, x_mixer)
    scatter = Scatter(grads, weights, widths, extras, load_sem, sum_recv, sum_send, free)

    barrier = pltpu.get_barrier_semaphore()
    greeted = [partner] + mates + plane[0] + plane[1]
    for device in greeted:
        pl.semaphore_signal(barrier, inc=1, device_id=device, device_id_type=MESH)
    pl.semaphore_wait(barrier, len(greeted))

    def rows(k):
        return pl.ds(pl.multiple_of(k % 4 * CHUNK, CHUNK), CHUNK)

    mine = rows(z)


    index = d * 2
    swap = remote(shard_other, w_mixer.at[s * 16 + d], copy_sem.at[0], copy_sem.at[1], partner)
    swap.start()
    fills = [pltpu.make_async_copy(shard_mixer, w_mixer.at[s * 16 + d], copy_sem.at[2])]
    for i, (src, dst) in enumerate(((shard_mix, w_mix), (shard_gate, w_gate), (shard_down, w_down))):
        fills.append(pltpu.make_async_copy(src, dst.at[pl.ds(index, 2)], copy_sem.at[3 + i]))
    for copy in fills:
        copy.start()
    small[...] = jnp.zeros_like(small)
    for copy in fills:
        copy.wait()
    swap.wait()

    def gather_most():
        for arrays in ((0, 1), (2, 3)):
            gather.start(arrays)
        for arrays in ((0, 1), (2, 3)):
            gather.spread(arrays)
        for a in (0, 1):
            gather.relay(a)


    def spread(a, weight, depth, to):
        def body(j):
            value = weight[pl.ds(j * 8, 8), :, 0:depth].reshape(8 * ROWS, depth)
            to[:, lanes(j, 384)] = dot_bt(a[:, 0:depth], value).astype(BF)

        times(4, body)

    def sum_start(phase, src):
        for j in (1, 2, 3):
            sems = (send_sem.at[phase, j - 1], recv_sem.at[phase, j - 1])
            remote(src.at[rows(z + j)], inbox.at[phase, j - 1], *sems, mates[j - 1]).start()

    def sum_middle(phase, src, full, work):
        total = src[mine, :].astype(F32)
        for j in range(3):
            arrived(inbox.at[phase, j], recv_sem.at[phase, j])
            total = total + inbox[phase, j].astype(F32)
        full[mine, :] = work(total).astype(BF)
        for j in (1, 2, 3):
            sems = (send_sem.at[phase, 2 + j], recv_sem.at[phase, 2 + j])
            remote(full.at[mine], full.at[mine], *sems, mates[j - 1]).start()

    def sum_end(phase, full):
        for j in (1, 2, 3):
            arrived(full.at[rows(z - j)], recv_sem.at[phase, 2 + j])
        for i in range(6):
            arrived(full.at[mine], send_sem.at[phase, i])

    def nothing():
        pass

    def sum_over_mates(phase, full, work, first_wait=nothing, second_wait=nothing):
        sum_start(phase, part)
        first_wait()
        sum_middle(phase, part, full, work)
        second_wait()
        sum_end(phase, full)


    def norm_rows(src):
        def body(i):
            values = src[rows(i), :].astype(F32)
            normed[rows(i), :] = (values * root(values) * gains[0:1, :]).astype(BF)

        times(tokens // CHUNK, body)

    def project(count):
        def body(j):
            proj[:, lanes(j)] = dot(normed[...], matrix(w_mixer, lanes(j)))

        times(count, body)

    def after_mixer(src, first_wait, second_wait):
        def work(total):
            value = src[mine, :].astype(F32) + total
            middle[...] = value
            return value * root(value) * gains[1:2, :]

        spread(mixer, w_mix, channels, part)
        sum_over_mates(0, ffn_in, work, first_wait, second_wait)

    def ffn_forward():
        gather.last(2)

        def body(j):
            gate = dot(ffn_in[...], matrix(w_gate, lanes(j, 256)))
            up = dot(ffn_in[...], matrix(w_gate, lanes(j, 256, padded)))
            gate_up[0, :, lanes(j, 256)] = gate
            gate_up[1, :, lanes(j, 256)] = up
            hidden[:, lanes(j, 256)] = (gate * jax.nn.sigmoid(gate) * up).astype(BF)

        times(padded // 256, body)
        gather.last(3)

    def add_middle(total):
        return middle[...] + total

    def weight_grad(a, left, right, start=0):
        size = widths[a]
        tile = 256 if size % 256 == 0 else 384
        buffer = stage_mixer if a == 4 else stage
        which = 1 if a == 4 else 0
        for t in range(4):
            slot = t % 2
            room = buffer.at[slot] if a > 3 or size == padded else buffer.at[slot, :, :, :, 0:size]
            if t > 1:
                arrived(room, stage_sem.at[which, slot])
            turned[...] = left[:, t * 384 : (t + 1) * 384].astype(F32).T.astype(BF)

            def body(j, slot=slot):
                value = dot(turned[...], right[:, lanes(j, tile, start)]).astype(BF)
                for k in range(8):
                    at = (k // 4, k % 4) if a == 4 else (k // 2, k % 2)
                    buffer[slot, at[0], at[1], :, lanes(j, tile)] = value[k * ROWS : (k + 1) * ROWS, :]

            times(size // tile, body)
            to = grads[a].at[t // 2, t % 2 * 2 : t % 2 * 2 + 2] if a == 4 else grads[a].at[t]
            pltpu.make_async_copy(room, to, stage_sem.at[which, slot]).start()
        for slot in (0, 1):
            room = buffer.at[slot] if a > 3 or size == padded else buffer.at[slot, :, :, :, 0:size]
            arrived(room, stage_sem.at[which, slot])

    def release(a):
        gather.sent(a)
        scatter.release(a)

    def ffn_backward(first_wait, second_wait):
        def body(j):
            grad = dot(top[...], matrix(w_down, lanes(j, 256)))
            gate, up = gate_up[0, :, lanes(j, 256)], gate_up[1, :, lanes(j, 256)]
            sig = jax.nn.sigmoid(gate)
            grad_pair[:, lanes(j, 256)] = (grad * up * sig * (1.0 + gate * (1.0 - sig))).astype(BF)
            grad_pair[:, lanes(j, 256, padded)] = (grad * gate * sig).astype(BF)

        times(padded // 256, body)

        def work(total):
            grad, small[1:2, :] = norm_back(middle[...], gains[1:2, :], total)
            grad = top[mine, :].astype(F32) + grad
            grad_chunk[...] = grad
            return grad

        spread(grad_pair, w_gate, 2 * padded, part)

        def early():
            release(2)
            first_wait()
            weight_grad(2, top, hidden)

        def late():
            second_wait()
            weight_grad(0, ffn_in, grad_pair)
            weight_grad(1, ffn_in, grad_pair, padded)

        sum_over_mates(2, grad_mid, work, early, late)
        for a in (2, 0, 1):
            for h in (0, 1):
                scatter.begin(a, h)

    def mixer_back(src, depth):
        def work(total):
            grad, small[0:1, :] = norm_back(src[mine, :].astype(F32), gains[0:1, :], total)
            return grad_chunk[...] + grad

        spread(grad_proj, w_mixer, depth, part)

        def early():
            release(1)
            release(0)
            for a, h in ((2, 0), (2, 1), (0, 0), (0, 1)):
                scatter.pass_on(a, h)

        def late():
            for a, h in ((1, 0), (1, 1)):
                scatter.pass_on(a, h)
            weight_grad(3, grad_mid, mixer)
            weight_grad(4, normed, grad_proj)

        sum_over_mates(3, grad_in, work, early, late)

    def small_start(k):
        group = plane[k] if k < 2 else mates
        for j in range(3):
            i = k * 3 + j
            remote(small, small_in.at[i], small_send.at[i], small_recv.at[i], group[j]).start()

    def small_add(k):
        for j in range(3):
            arrived(small, small_send.at[k * 3 + j])
            arrived(small, small_recv.at[k * 3 + j])
        summed = small[...] + small_in[k * 3] + small_in[k * 3 + 1] + small_in[k * 3 + 2]
        if k == 2:
            row = lax.broadcasted_iota(jnp.int32, summed.shape, 0)
            summed = jnp.where(row == 3, small[...], summed)
        small[...] = summed

    def wrap_up(section):
        def both(step, a):
            for h in (0, 1):
                step(a, h)

        def finish(a):
            for h in (0, 1):
                if a == 4:
                    scatter.finish(a, h, mixer_own if h == section else mixer_give)
                else:
                    scatter.finish(a, h, (sum_gate, sum_up, sum_down, sum_mix)[a].at[h])

        small_start(0)
        both(scatter.begin, 4)
        both(scatter.begin, 3)
        both(scatter.turn, 2)
        both(scatter.pass_on, 4)
        both(scatter.pass_on, 3)
        small_add(0)
        small_start(1)
        both(scatter.turn, 0)
        both(scatter.pass_back, 2)
        both(scatter.turn, 1)
        both(scatter.pass_back, 0)
        small_add(1)
        small_start(2)
        both(scatter.turn, 4)
        finish(2)
        both(scatter.turn, 3)
        both(scatter.pass_back, 1)
        finish(0)
        both(scatter.pass_back, 4)
        both(scatter.pass_back, 3)
        finish(1)
        small_add(2)
        give_small = remote(small, small_other, give_sem.at[4], give_sem.at[5], partner)
        give_small.start()
        finish(4)
        give_mixer = remote(mixer_give, mixer_other, give_sem.at[6], give_sem.at[7], partner)
        give_mixer.start()
        finish(3)
        for a in range(5):
            both(scatter.sent, a)
        give_small.wait()
        give_mixer.wait()


    def same(lag):
        seg = seg_col[...] + jnp.zeros((tokens, 128), jnp.int32)
        row = lax.broadcasted_iota(jnp.int32, (tokens, 128), 0)
        return jnp.where((seg == pltpu.roll(seg, lag, 0)) & (row % MBT >= lag), 1.0, 0.0)

    def pieces(j):
        at = [slice(i * channels + j * 128, i * channels + (j + 1) * 128) for i in range(3)]
        return [proj[:, a] for a in at], at

    def first():
        scatter.claimed.clear()
        gather_most()
        norm_rows(own)
        gather.last(0)
        project(3 * channels // 128)
        for j in range(channels // 128):
            (b, c, e), _ = pieces(j)
            at = slice(j * 128, (j + 1) * 128)
            product = b * e
            total = taps[0:1, at] * product
            for lag in (1, 2):
                total = total + taps[lag : lag + 1, at] * (pltpu.roll(product, lag, 0) * same(lag))
            mixed[:, at] = total
            mixer[:, at] = (c * total).astype(BF)
        gather.last(1)

        def rest():
            gather.relay(3)
            pl.semaphore_signal(go, inc=1, device_id=partner, device_id_type=MESH)

        after_mixer(own, lambda: gather.relay(2), rest)
        ffn_forward()
        spread(hidden, w_down, padded, part)
        sum_over_mates(1, result, add_middle)
        give = remote(result, sent, give_sem.at[0], give_sem.at[1], partner)
        give.start()
        give.wait_send()
        arrived(top, give_sem.at[3])
        ffn_backward(lambda: release(3), nothing)
        for j in range(channels // 128):
            (b, c, e), at = pieces(j)
            lane = slice(j * 128, (j + 1) * 128)
            grad_y = dot(grad_mid[...], matrix(w_mix, lane))
            product = b * e
            grad_mixed = grad_y * c
            grad_product = taps[0:1, lane] * grad_mixed
            sums = [jnp.sum(grad_mixed * product, axis=0, keepdims=True)]
            for lag in (1, 2):
                masked = grad_mixed * same(lag)
                sums.append(jnp.sum(masked * pltpu.roll(product, lag, 0), axis=0, keepdims=True))
                grad_product = grad_product + taps[lag : lag + 1, lane] * pltpu.roll(masked, tokens - lag, 0)
            for k in range(3):
                small[3:4, at[k]] = sums[k]
            grad_proj[:, at[0]] = (grad_product * e).astype(BF)
            grad_proj[:, at[1]] = (grad_y * mixed[:, lane]).astype(BF)
            grad_proj[:, at[2]] = (grad_product * b).astype(BF)
        mixer_back(own, 3 * channels)
        wrap_up(0)


    half = channels // 3
    lane_of = lax.broadcasted_iota(jnp.int32, (1, half), 1)
    keep = [jnp.where(lane_of // HEAD == k, 1.0, 0.0) for k in (0, 1)]

    def per_head(values):
        first_sum = jnp.sum(values * keep[0], axis=-1, keepdims=True)
        second_sum = jnp.sum(values * keep[1], axis=-1, keepdims=True)
        return (first_sum * keep[0] + second_sum * keep[1]) * (1.0 / HEAD)

    def across(values):
        low = lane_of % HEAD < HEAD // 2
        return jnp.where(low, pltpu.roll(values, half - HEAD // 2, 1), pltpu.roll(values, HEAD // 2, 1))

    def allowed(block):
        at = slice(block * MBT, (block + 1) * MBT)
        t = lax.broadcasted_iota(jnp.int32, (MBT, MBT), 0)
        u = lax.broadcasted_iota(jnp.int32, (MBT, MBT), 1)
        return jnp.where((seg_col[at, :] == seg_row[:, at]) & (u <= t), 1.0, 0.0)

    def turn_tables():
        for block in range(blocks):
            at = slice(block * MBT, (block + 1) * MBT)
            offset = jnp.sum(allowed(block), axis=1, keepdims=True) - 1.0
            column = lax.broadcasted_iota(jnp.int32, (MBT, MBT), 1).astype(F32)
            pick = jnp.where(column == offset, 1.0, 0.0).astype(BF)
            for k in (0, 1):
                turns[k, at, :] = dot(pick, tables[k, 0]) + dot(pick, tables[k, 1]) + dot(pick, tables[k, 2])

    inv_sqrt = HEAD ** (-0.5)

    def masked(i, block, k):
        at = slice(block * MBT, (block + 1) * MBT)
        return heads[i, at, :] * keep[k].astype(BF)

    def second():
        scatter.claimed.clear()
        turn_tables()
        top[...] = own[...]
        grad_proj[:, 5 * half :] = jnp.zeros((tokens, grad_proj.shape[1] - 5 * half), BF)
        pl.semaphore_wait(go, 1)
        gather_most()
        gather.relay(2)
        arrived(sent, give_sem.at[1])
        norm_rows(sent)
        gather.last(0)
        project(5)
        for i in range(4):
            raw = proj[:, i * half : (i + 1) * half]
            gain = qk_gains[min(i // 3, 1) : min(i // 3, 1) + 1, :]
            value = raw * lax.rsqrt(per_head(raw * raw) + epsilon) * gain
            heads[i] = (value * turns[0] + across(value) * turns[1]).astype(BF)
        heads[4] = proj[:, 4 * half : 5 * half].astype(BF)
        for block in range(blocks):
            at = slice(block * MBT, (block + 1) * MBT)
            ok = allowed(block)
            for g in range(3):
                attended = jnp.zeros((MBT, half), F32)
                for k in (0, 1):
                    score = dot_bt(heads[g, at, :], masked(3, block, k)) * inv_sqrt
                    score = jnp.where(ok > 0.0, score, neg_large)
                    power = jnp.exp(score - jnp.max(score, axis=-1, keepdims=True))
                    weight = power / jnp.sum(power, axis=-1, keepdims=True)
                    soft[(block * 3 + g) * 2 + k] = weight
                    attended = attended + dot(weight.astype(BF), masked(4, block, k))
                mixer[at, g * half : (g + 1) * half] = attended.astype(BF)
        gather.last(1)
        after_mixer(sent, lambda: gather.relay(3), nothing)
        ffn_forward()

        def late_start():
            spread(hidden, w_down, padded, late_part)
            release(3)

        ffn_backward(late_start, lambda: sum_start(1, late_part))
        for block in range(blocks):
            at = slice(block * MBT, (block + 1) * MBT)
            grad_key = jnp.zeros((MBT, half), F32)
            grad_value = jnp.zeros((MBT, half), F32)
            for g in range(3):
                grad_att = dot(grad_mid[at, :], matrix(w_mix, slice(g * half, (g + 1) * half))).astype(BF)
                grad_query = jnp.zeros((MBT, half), F32)
                for k in (0, 1):
                    weight = soft[(block * 3 + g) * 2 + k]
                    grad_soft = dot_bt(grad_att, masked(4, block, k))
                    delta = jnp.sum(weight * grad_soft, axis=-1, keepdims=True)
                    grad_score = (weight * (grad_soft - delta)).astype(BF)
                    grad_query = grad_query + dot(grad_score, masked(3, block, k))
                    grad_key = grad_key + dot_at(grad_score, masked(g, block, k))
                    grad_value = grad_value + dot_at(weight.astype(BF), grad_att * keep[k].astype(BF))
                grad_heads[g, at, :] = grad_query * inv_sqrt
            grad_heads[3, at, :] = grad_key * inv_sqrt
            grad_proj[at, 4 * half : 5 * half] = grad_value.astype(BF)
            if block == 0:
                sum_middle(1, late_part, result, add_middle)
        gain_rows = [jnp.zeros((1, half), F32)] * 2
        for i in range(4):
            raw = proj[:, i * half : (i + 1) * half]
            which = min(i // 3, 1)
            gain = qk_gains[which : which + 1, :]
            grad = grad_heads[i]
            grad = grad * turns[0] - across(grad) * turns[1]
            factor = lax.rsqrt(per_head(raw * raw) + epsilon)
            weighted = grad * gain
            gain_rows[which] = gain_rows[which] + jnp.sum(grad * raw * factor, axis=0, keepdims=True)
            grad = factor * weighted - raw * (factor * factor * factor) * per_head(raw * weighted)
            grad_proj[:, i * half : (i + 1) * half] = grad.astype(BF)
        small[2:3, 0:half] = gain_rows[0]
        small[2:3, half : 2 * half] = gain_rows[1]
        mixer_back(sent, 5 * half)
        give = remote(grad_in, top, give_sem.at[2], give_sem.at[3], partner)
        give.start()
        wrap_up(1)
        sum_end(1, result)
        give.wait_send()

    pl.when(s == 0)(first)
    pl.when(s == 1)(second)


def rope_parts():
    frequency = rope_base ** (-np.arange(HEAD // 2, dtype=np.float64) * 2.0 / HEAD)
    angles = (np.arange(MBT, dtype=np.float32)[:, None] * frequency.astype(np.float32)[None, :]).astype(np.float32)
    cosine, sine = np.cos(angles.astype(np.float64)), np.sin(angles.astype(np.float64))
    both = (np.concatenate([cosine] * 4, axis=1), np.concatenate([-sine, sine, -sine, sine], axis=1))
    parts = []
    for table in both:
        left = table.astype(np.float32)
        for _ in range(3):
            piece = left.astype(jnp.bfloat16)
            parts.append(piece)
            left = left - piece.astype(np.float32)
    return jnp.asarray(np.stack(parts).reshape(2, 3, MBT, 2 * HEAD))


def both_blocks(own, segments, gains, taps, qk_gains, shards):
    tokens, width = own.shape
    channels, padded = shards[2].shape[-1], shards[4].shape[-1]
    wide = 3 * channels
    shape = jax.ShapeDtypeStruct
    rows, vmem = (tokens, width), pltpu.VMEM
    sums = [(2, ROWS, padded)] * 3 + [(2, ROWS, channels), (ROWS, wide), (ROWS, wide), (8, width), (8, width)]
    outs = [shape(rows, BF), shape(rows, BF)] + [shape(v, F32) for v in sums]
    n_vmem = len(outs)
    outs += [shape((4, 4, 2, ROWS, w), BF) for w in (padded, padded, padded, channels)] + [shape((2, 4, 4, ROWS, wide), BF)]
    scratch = [vmem((32, ROWS, w), BF) for w in (wide, channels, 2 * padded, padded)]
    scratch += [vmem((2, 3, ROWS, w), BF) for w in (padded, padded, padded, channels, wide)]
    scratch += [vmem((2, 4, 2, ROWS, padded), BF), vmem((2, 2, 4, ROWS, wide), BF), vmem((384, tokens), BF)]
    sizes = [width, wide, channels, width, 2 * padded, padded, width, width, width, width, width]
    scratch += [vmem((tokens, w), BF) for w in sizes]
    scratch += [
        vmem((4, 3, CHUNK, width), BF),
        vmem((CHUNK, width), F32),
        vmem((CHUNK, width), F32),
        vmem((tokens, wide), F32),
        vmem((tokens, channels), F32),
        vmem((2, tokens, padded), F32),
        vmem((5, tokens, 128), BF),
        vmem((6 * tokens // MBT, MBT, MBT), F32),
        vmem((2, tokens, 128), F32),
        vmem((4, tokens, 128), F32),
        vmem((ROWS, wide), F32),
        vmem((9, 8, width), F32),
        DMA((6,)),
        DMA((4,)),
        DMA((8, 16)),
        pltpu.SemaphoreType.REGULAR,
        DMA((4, 6)),
        DMA((4, 6)),
        DMA((8,)),
        DMA((2, 2)),
        DMA((10, 3)),
        DMA((10, 4)),
        DMA((10,)),
        pltpu.SemaphoreType.REGULAR((4,)),
        DMA((9,)),
        DMA((9,)),
    ]
    return pl.pallas_call(
        blocks_kernel,
        out_shape=outs,
        in_specs=[VM] * 7 + [ANY] * 5,
        out_specs=[VM] * n_vmem + [ANY] * 5,
        scratch_shapes=scratch,
        compiler_params=pltpu.CompilerParams(collective_id=0, has_side_effects=True, vmem_limit_bytes=60 * MIB),
        name="both_blocks",
    )(own, segments[:, None], segments[None, :], gains, taps, qk_gains, rope_parts(), *shards)[:n_vmem]


def local(ends, segment_ids, norm_gains, conv_in, conv_kernel, qkv_weight, qk_gains, mix_out, gate_up, down):
    is_first = lax.axis_index(SEC) == 0
    channels = mix_out.shape[1]
    hidden = gate_up.shape[3]
    padded = (hidden + 255) // 256 * 256
    kv, group, head = qkv_weight.shape[1], qkv_weight.shape[2] - 2, qkv_weight.shape[3]
    qkv_width = kv * (group + 2) * head
    taps = conv_kernel.shape[0]
    spare = ((0, 0), (0, padded - hidden))

    conv_rows = conv_in.reshape(ROWS, taps * channels)
    qkv_rows = qkv_weight.transpose(0, 2, 1, 3).reshape(ROWS, qkv_width)
    qkv_rows = jnp.pad(qkv_rows, ((0, 0), (0, taps * channels - qkv_width)))
    mix_rows = mix_out[0].T
    mix_turned = mix_rows.reshape(2 * ROWS, kv, group, head).transpose(0, 2, 1, 3).reshape(2 * ROWS, channels)
    gate_rows = jnp.pad(gate_up[0], ((0, 0),) + spare).reshape(2, ROWS, 2 * padded)
    down_rows = jnp.pad(down[0].T, spare).reshape(2, ROWS, padded)
    gains = jnp.concatenate([qk_gains, qk_gains], axis=1)
    shards = (
        jnp.where(is_first, conv_rows, qkv_rows),
        jnp.where(is_first, qkv_rows, conv_rows),
        jnp.where(is_first, mix_rows, mix_turned).reshape(2, ROWS, channels),
        gate_rows,
        down_rows,
    )
    result, grad_in, sum_gate, sum_up, sum_down, sum_mix, mixer_own, mixer_other, small_own, small_other = both_blocks(
        ends[0], segment_ids, norm_gains[0], conv_kernel, gains, shards
    )
    conv_grad = jnp.where(is_first, mixer_own, mixer_other)
    qkv_grad = jnp.where(is_first, mixer_other, mixer_own)[:, :qkv_width].reshape(ROWS, group + 2, kv, head)
    of_first = jnp.where(is_first, small_own, small_other)
    of_second = jnp.where(is_first, small_other, small_own)
    mix_grad = sum_mix.reshape(2 * ROWS, channels)
    mix_back = mix_grad.reshape(2 * ROWS, group, kv, head).transpose(0, 2, 1, 3).reshape(2 * ROWS, channels)
    return (
        result[None],
        grad_in.astype(F32)[None],
        small_own[None, 0:2],
        conv_grad.reshape(conv_in.shape),
        of_first[3, : taps * channels].reshape(taps, channels),
        qkv_grad.transpose(0, 2, 1, 3),
        of_second[2, : 4 * head].reshape(2, 2, head).sum(1),
        jnp.where(is_first, mix_grad, mix_back).T[None],
        jnp.stack([v.reshape(2 * ROWS, padded)[:, :hidden] for v in (sum_gate, sum_up)], axis=1)[None],
        sum_down.reshape(2 * ROWS, padded)[:, :hidden].T[None],
    )


def solution(mesh):
    dims = (
        P(SEC, DP, None),
        P(DP),
        P(SEC, None, None),
        P((SEC, DP), None, TEN),
        P(None, TEN),
        P((SEC, DP), TEN, None, None),
        P(),
        P(SEC, TEN, DP),
        P(SEC, DP, None, TEN),
        P(SEC, TEN, DP),
    )
    results = (dims[0], dims[0], dims[2], dims[3], dims[4], dims[5], dims[6], dims[7], dims[8], dims[9])
    return jax.shard_map(local, mesh=mesh, in_specs=dims, out_specs=results, check_vma=False)
```

```python
import functools

import jax
import jax.numpy as jnp
import numpy as np
from jax import lax
from jax.experimental import pallas as pl
from jax.experimental.pallas import tpu as pltpu
from jax.sharding import PartitionSpec as P

SEC, DP, TEN = "section", "dp", "tensor"
MESH = pl.DeviceIdType.MESH
F32, BF = jnp.float32, jnp.bfloat16
ANY = pl.BlockSpec(memory_space=pl.ANY)
VM = pl.BlockSpec(memory_space=pltpu.VMEM)
DMA = pltpu.SemaphoreType.DMA
MIB = 1 << 20

MBT = 128
ROWS = 48
CHUNK = 64
HEAD = 64
epsilon = 1e-05
rope_base = 1000000.0
neg_large = -1e30

HOME = (2, 2, 3, 1, 0)


def place():
    d = lax.axis_index(DP)
    return lax.axis_index(SEC), d // 4, d % 4, lax.axis_index(TEN)


def near(axis, y, x, step):
    return (y, (x + step) % 4) if axis == 0 else ((y + step) % 4, x)


def remote(src, dst, send_sem, recv_sem, device):
    return pltpu.make_async_remote_copy(
        src_ref=src, dst_ref=dst, send_sem=send_sem, recv_sem=recv_sem, device_id=device, device_id_type=MESH
    )


def arrived(ref, sem):
    pltpu.make_async_copy(ref, ref, sem).wait()


def cut(columns):
    return (columns // 128 + 1) // 2 * 128


def root(values):
    return lax.rsqrt(jnp.mean(values * values, axis=-1, keepdims=True) + epsilon)


def dot(a, b):
    return jnp.dot(a, b, preferred_element_type=F32)


def dot_bt(a, b):
    return lax.dot_general(a, b, (((1,), (1,)), ((), ())), preferred_element_type=F32)


def dot_at(a, b):
    return lax.dot_general(a, b, (((0,), (0,)), ((), ())), preferred_element_type=F32)


def norm_back(values, gain, grad):
    factor = root(values)
    weighted = grad * gain
    grad_in = factor * weighted - values * (factor * factor * factor) * jnp.mean(values * weighted, axis=-1, keepdims=True)
    return grad_in, jnp.sum(grad * values * factor, axis=0, keepdims=True)


def lanes(i, size=128, start=0):
    return pl.ds(pl.multiple_of(start + i * size, 128), size)


def times(count, body):
    def step(i, carry):
        body(i)
        return carry

    lax.fori_loop(0, count, step, 0)


def matrix(ref, columns):
    value = ref[:, :, columns]
    return value.reshape(value.shape[0] * value.shape[1], value.shape[2])


def add_rows(dst, pieces):
    rows = dst.shape[-2]
    three = len(dst.shape) == 3
    kind = BF if len(pieces) == 2 else F32

    def body(i):
        at = pl.ds(pl.multiple_of(i % (rows // 16) * 16, 16), 16)
        k = i // (rows // 16)
        get = (lambda r: r[k, at, :]) if three else (lambda r: r[at, :])
        total = get(pieces[0]).astype(kind)
        for p in pieces[1:]:
            total = total + get(p).astype(kind)
        if three:
            dst[k, at, :] = total.astype(dst.dtype)
        else:
            dst[at, :] = total.astype(dst.dtype)

    times((dst.shape[0] if three else 1) * (rows // 16), body)


class Gather:
    def __init__(self, weights, widths, shards, send_sem, recv_sem):
        self.weights, self.widths, self.shards = weights, widths, shards
        self.send_sem, self.recv_sem = send_sem, recv_sem
        self.s, self.y, self.x, self.z = place()

    def narrow(self, a, ref):
        return ref if self.widths[a] == ref.shape[-1] else ref.at[..., 0 : self.widths[a]]

    def block(self, a, h, yx):
        b = yx[0] * 4 + yx[1]
        return self.narrow(a, self.weights[a].at[h * 16 + b if a == 0 else b * 2 + h])

    def send(self, a, h, yx, lo, hi, to, src=None):
        ref = self.block(a, h, yx)
        if (lo, hi) != (0, self.widths[a]):
            ref = ref.at[:, lo:hi]
        recv = self.recv_sem.at[a * 2 + h, yx[0] * 4 + yx[1]]
        remote(ref if src is None else src, ref, self.send_sem.at[a], recv, (self.s, to[0] * 4 + to[1], self.z)).start()

    def wait(self, a, h, yx):
        arrived(self.block(a, h, yx), self.recv_sem.at[a * 2 + h, yx[0] * 4 + yx[1]])

    def near(self, axis, step):
        return near(axis, self.y, self.x, step)

    def start(self, arrays):
        for axis_of in (lambda h: h, lambda h: 1 - h):
            for a in arrays:
                for h in (0, 1):
                    src = None if a == 0 else self.shards[a].at[h]
                    for step in (1, -1):
                        self.send(a, h, (self.y, self.x), 0, self.widths[a], self.near(axis_of(h), step), src)

    def spread(self, arrays):
        for a in arrays:
            w = self.widths[a]
            c = cut(w)
            for h in (0, 1):
                for step, lo, hi in ((1, 0, c), (-1, c, w)):
                    src = self.near(h, -step)
                    self.wait(a, h, src)
                    self.send(a, h, src, lo, hi, self.near(h, step))
                    for on in (1, -1):
                        self.send(a, h, src, 0, w, self.near(1 - h, on))
        for a in arrays:
            for h in (0, 1):
                far = self.near(h, 2)
                self.wait(a, h, far)
                for on in (1, -1):
                    self.send(a, h, far, 0, self.widths[a], self.near(1 - h, on))

    def relay(self, a):
        w = self.widths[a]
        c = cut(w)
        for h in (0, 1):

            def body(j, h=h):
                line = self.near(h, j)
                for step, lo, hi in ((1, 0, c), (-1, c, w)):
                    src = near(1 - h, line[0], line[1], -step)
                    self.wait(a, h, src)
                    self.send(a, h, src, lo, hi, self.near(1 - h, step))

            times(4, body)

    def last(self, a):
        for h in (0, 1):

            def body(j, h=h):
                line = self.near(h, j)
                self.wait(a, h, near(1 - h, line[0], line[1], 2))

            times(4, body)

    def sent(self, a):
        arrived(self.narrow(a, self.weights[a].at[0:30]), self.send_sem.at[a])


class Scatter:
    def __init__(self, grads, weights, widths, extras, load_sem, recv_sem, send_sem, free):
        self.grads, self.weights, self.widths, self.extras = grads, weights, widths, extras
        self.load_sem, self.recv_sem, self.send_sem, self.free = load_sem, recv_sem, send_sem, free
        self.s, self.y, self.x, self.z = place()
        self.claimed = set()
        self.loads = {}

    def device(self, yx):
        return (self.s, yx[0] * 4 + yx[1], self.z)

    def near(self, axis, step):
        return near(axis, self.y, self.x, step)

    def release(self, home):
        for axis in (0, 1):
            for step in (1, -1):
                to = self.device(self.near(axis, step))
                pl.semaphore_signal(self.free.at[home], inc=1, device_id=to, device_id_type=MESH)

    def line(self, a, h, yx):
        if a == 4:
            ref = self.grads[a].at[h, yx[0]] if h == 0 else self.grads[a].at[h, :, yx[1]]
            return ref if self.widths[a] == ref.shape[-1] else ref.at[:, :, 0 : self.widths[a]]
        return self.grads[a].at[yx[0], :, h] if h == 0 else self.grads[a].at[:, yx[1], h]

    def room(self, a, h, lo, hi):
        ref = self.weights[HOME[a]].at[16 * h + lo : 16 * h + hi]
        start = self.widths[a] if a == 1 else 0
        if self.widths[a] != ref.shape[-1]:
            ref = ref.at[:, :, start : start + self.widths[a]]
        return ref

    def extra(self, a, h):
        ref = self.extras[a].at[h]
        return ref if self.widths[a] == ref.shape[-1] else ref.at[:, :, 0 : self.widths[a]]

    def move(self, a, h, i, src, dst, to):
        remote(src, dst, self.send_sem.at[a * 2 + h], self.recv_sem.at[a * 2 + h, i], self.device(to)).start()

    def load(self, a, h, i, src, dst):
        copy = pltpu.make_async_copy(src, dst, self.load_sem.at[a * 2 + h, i])
        copy.start()
        self.loads[a, h, i] = copy

    def begin(self, a, h):
        if HOME[a] not in self.claimed:
            pl.semaphore_wait(self.free.at[HOME[a]], 4)
            self.claimed.add(HOME[a])
        up, dn, far = (self.near(1 - h, step) for step in (1, -1, 2))
        self.move(a, h, 0, self.line(a, h, far).at[0:2], self.room(a, h, 0, 2), up)
        self.move(a, h, 0, self.line(a, h, far).at[2:4], self.room(a, h, 2, 4), dn)
        self.load(a, h, 0, self.line(a, h, up).at[0:2], self.room(a, h, 12, 14))
        self.load(a, h, 1, self.line(a, h, dn).at[2:4], self.room(a, h, 14, 16))

    def begin_near(self, a, h):
        up, dn = (self.near(1 - h, step) for step in (1, -1))
        self.move(a, h, 1, self.line(a, h, up).at[2:4], self.room(a, h, 6, 8), up)
        self.move(a, h, 1, self.line(a, h, dn).at[0:2], self.room(a, h, 8, 10), dn)

    def pass_on(self, a, h):
        up, dn = (self.near(1 - h, step) for step in (1, -1))
        self.loads[a, h, 0].wait()
        self.loads[a, h, 1].wait()
        arrived(self.room(a, h, 0, 4), self.recv_sem.at[a * 2 + h, 0])
        mine = self.room(a, h, 12, 16)
        add_rows(mine, [mine, self.room(a, h, 0, 4)])
        self.move(a, h, 1, self.room(a, h, 12, 14), self.room(a, h, 4, 6), up)
        self.move(a, h, 1, self.room(a, h, 14, 16), self.room(a, h, 10, 12), dn)
        self.load(a, h, 2, self.line(a, h, (self.y, self.x)), self.room(a, h, 0, 4))

    def own(self, h):
        return self.x if h == 0 else self.y

    def turn(self, a, h):
        w = self.widths[a]
        c = cut(w)
        self.loads[a, h, 2].wait()
        arrived(self.room(a, h, 4, 12), self.recv_sem.at[a * 2 + h, 1])
        total, extra = self.room(a, h, 0, 4), self.extra(a, h)
        add_rows(total, [total, self.room(a, h, 4, 8), self.room(a, h, 8, 12)])
        up, dn = (self.near(h, step) for step in (1, -1))
        far, i_up, i_dn = ((self.own(h) + step) % 4 for step in (2, 1, -1))
        self.move(a, h, 2, total.at[far, :, 0:c], extra.at[0, :, 0:c], up)
        self.move(a, h, 2, total.at[far, :, c:w], extra.at[0, :, c:w], dn)
        self.move(a, h, 3, total.at[i_up, :, c:w], extra.at[1, :, c:w], up)
        self.move(a, h, 3, total.at[i_dn, :, 0:c], extra.at[2, :, 0:c], dn)

    def pass_back(self, a, h):
        w = self.widths[a]
        c = cut(w)
        total, extra = self.room(a, h, 0, 4), self.extra(a, h)
        up, dn = (self.near(h, step) for step in (1, -1))
        i_up, i_dn = ((self.own(h) + step) % 4 for step in (1, -1))
        arrived(extra.at[0], self.recv_sem.at[a * 2 + h, 2])
        lo, hi = extra.at[0, :, 0:c], extra.at[0, :, c:w]
        add_rows(lo, [lo, total.at[i_up, :, 0:c]])
        self.move(a, h, 3, lo, extra.at[1, :, 0:c], up)
        add_rows(hi, [hi, total.at[i_dn, :, c:w]])
        self.move(a, h, 3, hi, extra.at[2, :, c:w], dn)

    def finish(self, a, h, out):
        total, extra = self.room(a, h, 0, 4), self.extra(a, h)
        arrived(extra.at[1:3], self.recv_sem.at[a * 2 + h, 3])
        add_rows(out, [total.at[self.own(h)], extra.at[1], extra.at[2]])

    def sent(self, a, h):
        arrived(self.room(a, h, 0, 15), self.send_sem.at[a * 2 + h])


def blocks_kernel(
    own,
    seg_col,
    seg_row,
    gains,
    taps,
    qk_gains,
    tables,
    shard_mixer,
    shard_other,
    shard_mix,
    shard_gate,
    shard_down,
    result,
    grad_in,
    sum_gate,
    sum_up,
    sum_down,
    sum_mix,
    mixer_own,
    mixer_other,
    small,
    small_other,
    grad_gate,
    grad_up,
    grad_down,
    grad_mix,
    grad_mixer,
    w_mixer,
    w_mix,
    w_gate,
    w_down,
    x_gate,
    x_up,
    x_down,
    x_mix,
    x_mixer,
    stage,
    stage_mixer,
    turned,
    normed,
    grad_proj,
    mixer,
    ffn_in,
    grad_pair,
    hidden,
    top,
    grad_mid,
    sent,
    part,
    late_part,
    inbox,
    middle,
    grad_chunk,
    proj,
    mixed,
    gate_up,
    heads,
    soft,
    turns,
    grad_heads,
    mixer_give,
    small_in,
    copy_sem,
    gather_send,
    gather_recv,
    go,
    send_sem,
    recv_sem,
    give_sem,
    stage_sem,
    load_sem,
    sum_recv,
    sum_send,
    free,
    small_send,
    small_recv,
):
    s, y, x, z = place()
    d = y * 4 + x
    mates = [(s, d, (z + j) % 4) for j in (1, 2, 3)]
    partner = (1 - s, d, z)
    plane = [[(s, v[0] * 4 + v[1], z) for v in (near(k, y, x, j) for j in (1, 2, 3))] for k in (0, 1)]
    tokens, width = own.shape
    channels = mixer.shape[1]
    padded = hidden.shape[1]
    blocks = tokens // MBT
    weights = (w_mixer, w_mix, w_gate, w_down)
    grads = (grad_gate, grad_up, grad_down, grad_mix, grad_mixer)
    extras = (x_gate, x_up, x_down, x_mix, x_mixer)
    shards = (None, shard_mix, shard_gate, shard_down)

    def movers(wide):
        gather = Gather(weights, (wide, channels, 2 * padded, padded), shards, gather_send, gather_recv)
        widths = (padded, padded, padded, channels, wide)
        return gather, Scatter(grads, weights, widths, extras, load_sem, sum_recv, sum_send, free)

    barrier = pltpu.get_barrier_semaphore()
    greeted = [partner] + mates + plane[0] + plane[1]
    for device in greeted:
        pl.semaphore_signal(barrier, inc=1, device_id=device, device_id_type=MESH)
    pl.semaphore_wait(barrier, len(greeted))

    def rows(k):
        return pl.ds(pl.multiple_of(k % 4 * CHUNK, CHUNK), CHUNK)

    mine = rows(z)


    index = d * 2
    swap = remote(shard_other, w_mixer.at[s * 16 + d], copy_sem.at[0], copy_sem.at[1], partner)
    swap.start()
    fills = [pltpu.make_async_copy(shard_mixer, w_mixer.at[s * 16 + d], copy_sem.at[2])]
    for i, (src, dst) in enumerate(((shard_mix, w_mix), (shard_gate, w_gate), (shard_down, w_down))):
        fills.append(pltpu.make_async_copy(src, dst.at[pl.ds(index, 2)], copy_sem.at[3 + i]))
    for copy in fills:
        copy.start()
    small[...] = jnp.zeros_like(small)

    def gather_most(gather):
        gather.start((1,))
        fills[0].wait()
        swap.wait()
        gather.start((0,))
        gather.start((2, 3))
        for copy in fills[1:]:
            copy.wait()
        for arrays in ((0, 1), (2, 3)):
            gather.spread(arrays)
        for a in (0, 1):
            gather.relay(a)


    def spread(phase, a, weight, depth, to, send=True):
        for k in range(2):
            value = weight[k * 16 : k * 16 + 16, :, 0:depth].reshape(16 * ROWS, depth)
            columns = slice(k * 16 * ROWS, (k + 1) * 16 * ROWS)
            to[:, columns] = dot_bt(a[:, 0:depth], value).astype(BF)
            if send:
                sum_start(phase, to, columns)

    def sum_start(phase, src, columns=slice(None)):
        for j in (2, 1, 3):
            sems = (send_sem.at[phase, j - 1], recv_sem.at[phase, j - 1])
            remote(src.at[rows(z + j), columns], inbox.at[phase, j - 1, :, columns], *sems, mates[j - 1]).start()

    def sum_middle(phase, src, full, work):
        total = src[mine, :].astype(F32)
        for j in range(3):
            arrived(inbox.at[phase, j], recv_sem.at[phase, j])
            total = total + inbox[phase, j].astype(F32)
        full[mine, :] = work(total).astype(BF)
        for j in (2, 1, 3):
            sems = (send_sem.at[phase, 2 + j], recv_sem.at[phase, 2 + j])
            remote(full.at[mine], full.at[mine], *sems, mates[j - 1]).start()

    def sum_end(phase, full):
        for j in (1, 2, 3):
            arrived(full.at[rows(z - j)], recv_sem.at[phase, 2 + j])
        for i in range(6):
            arrived(full.at[mine], send_sem.at[phase, i])

    def nothing():
        pass

    def sum_over_mates(phase, full, work, first_wait=nothing, second_wait=nothing):
        first_wait()
        sum_middle(phase, part, full, work)
        second_wait()
        sum_end(phase, full)


    def norm_rows(src):
        def body(i):
            values = src[rows(i), :].astype(F32)
            normed[rows(i), :] = (values * root(values) * gains[0:1, :]).astype(BF)

        times(tokens // CHUNK, body)

    def project(count):
        def body(j):
            proj[:, lanes(j)] = dot(normed[...], matrix(w_mixer, lanes(j)))

        times(count, body)

    def after_mixer(src, first_wait, second_wait):
        def work(total):
            value = src[mine, :].astype(F32) + total
            middle[...] = value
            return value * root(value) * gains[1:2, :]

        spread(0, mixer, w_mix, channels, part)
        sum_over_mates(0, ffn_in, work, first_wait, second_wait)

    def ffn_forward(gather):
        gather.last(2)
        for j in range(padded // 256):
            at = slice(j * 256, (j + 1) * 256)
            gate = dot(ffn_in[...], matrix(w_gate, at))
            up = dot(ffn_in[...], matrix(w_gate, slice(padded + j * 256, padded + (j + 1) * 256)))
            gate_up[0, :, at] = gate
            gate_up[1, :, at] = up
            hidden[:, at] = (gate * jax.nn.sigmoid(gate) * up).astype(BF)
        gather.last(3)

    def add_middle(total):
        return middle[...] + total

    def weight_grad(a, left, right, start=0):
        size = right.shape[-1] // 2 if a < 2 else right.shape[-1]
        tile = 896 if size % 896 == 0 else size // 3 if size % 384 == 0 and size > 384 else size
        buffer = stage_mixer if a == 4 else stage
        which = 1 if a == 4 else 0
        if left is not None:
            turned[...] = left[...].T
        whole = size == buffer.shape[-1]
        for t in range(4):
            slot = t % 2
            room = buffer.at[slot] if whole else buffer.at[slot, :, :, :, 0:size]
            if t > 1:
                arrived(room, stage_sem.at[which, slot])
            for k in range(2):
                at = t * 384 + k * 192
                for j in range(size // tile):
                    columns = slice(start + j * tile, start + (j + 1) * tile)
                    value = dot(turned[at : at + 192, :], right[:, columns]).astype(BF)
                    for i in range(4):
                        b = k * 4 + i
                        b = (b // 4, b % 4) if a == 4 else (b // 2, b % 2)
                        buffer[slot, b[0], b[1], :, j * tile : (j + 1) * tile] = value[i * ROWS : (i + 1) * ROWS, :]
            to = grads[a].at[t // 2, t % 2 * 2 : t % 2 * 2 + 2] if a == 4 else grads[a].at[t]
            to = to if whole or a < 4 else to.at[:, :, :, 0:size]
            pltpu.make_async_copy(room, to, stage_sem.at[which, slot]).start()
        for slot in (0, 1):
            room = buffer.at[slot] if whole else buffer.at[slot, :, :, :, 0:size]
            arrived(room, stage_sem.at[which, slot])

    def release(gather, scatter, a):
        gather.sent(a)
        scatter.release(a)

    def ffn_backward(gather, scatter, first_wait, second_wait):
        for j in range(padded // 256):
            at = slice(j * 256, (j + 1) * 256)
            grad = dot(top[...], matrix(w_down, at))
            gate, up = gate_up[0, :, at], gate_up[1, :, at]
            sig = jax.nn.sigmoid(gate)
            grad_pair[:, at] = (grad * up * sig * (1.0 + gate * (1.0 - sig))).astype(BF)
            grad_pair[:, padded + j * 256 : padded + (j + 1) * 256] = (grad * gate * sig).astype(BF)

        def work(total):
            grad, small[1:2, :] = norm_back(middle[...], gains[1:2, :], total)
            grad = top[mine, :].astype(F32) + grad
            grad_chunk[...] = grad
            return grad

        spread(2, grad_pair, w_gate, 2 * padded, part)

        def early():
            release(gather, scatter, 2)
            first_wait()
            weight_grad(2, top, hidden)

        def late():
            second_wait()
            both(scatter.begin, 2)
            weight_grad(0, ffn_in, grad_pair)
            both(scatter.begin, 0)
            weight_grad(1, None, grad_pair, padded)
            both(scatter.begin, 1)
            for a in (2, 0, 1):
                both(scatter.begin_near, a)

        sum_over_mates(2, grad_mid, work, early, late)

    def mixer_back(gather, scatter, src, depth):
        def work(total):
            grad, small[0:1, :] = norm_back(src[mine, :].astype(F32), gains[0:1, :], total)
            return grad_chunk[...] + grad

        spread(3, grad_proj, w_mixer, depth, part)

        def early():
            release(gather, scatter, 1)
            release(gather, scatter, 0)
            for a, h in ((2, 0), (2, 1), (0, 0), (0, 1)):
                scatter.pass_on(a, h)

        def late():
            for a, h in ((1, 0), (1, 1)):
                scatter.pass_on(a, h)
            weight_grad(3, grad_mid, mixer)
            weight_grad(4, normed, grad_proj.at[:, 0:depth])

        sum_over_mates(3, grad_in, work, early, late)

    def small_start(k):
        group = plane[k] if k < 2 else mates
        for j in range(3):
            i = k * 3 + j
            remote(small, small_in.at[i], small_send.at[i], small_recv.at[i], group[j]).start()

    def small_add(k):
        for j in range(3):
            arrived(small, small_send.at[k * 3 + j])
            arrived(small, small_recv.at[k * 3 + j])
        summed = small[...] + small_in[k * 3] + small_in[k * 3 + 1] + small_in[k * 3 + 2]
        if k == 2:
            row = lax.broadcasted_iota(jnp.int32, summed.shape, 0)
            summed = jnp.where(row == 3, small[...], summed)
        small[...] = summed

    def both(step, a):
        for h in (0, 1):
            step(a, h)

    widths = (3 * channels, 5 * channels // 3)

    def wrap_up(scatter, section):
        def finish(a):
            for h in (0, 1):
                if a == 4:
                    scatter.finish(a, h, (mixer_own if h == section else mixer_give).at[:, 0 : widths[section]])
                else:
                    scatter.finish(a, h, (sum_gate, sum_up, sum_down, sum_mix)[a].at[h])

        small_start(0)
        both(scatter.begin, 4)
        both(scatter.begin, 3)
        both(scatter.begin_near, 4)
        both(scatter.begin_near, 3)
        both(scatter.turn, 2)
        both(scatter.pass_on, 4)
        both(scatter.pass_on, 3)
        small_add(0)
        small_start(1)
        both(scatter.turn, 0)
        both(scatter.pass_back, 2)
        both(scatter.turn, 1)
        both(scatter.pass_back, 0)
        small_add(1)
        small_start(2)
        both(scatter.turn, 4)
        finish(2)
        both(scatter.turn, 3)
        both(scatter.pass_back, 1)
        finish(0)
        both(scatter.pass_back, 4)
        both(scatter.pass_back, 3)
        finish(1)
        small_add(2)
        give_small = remote(small, small_other, give_sem.at[4], give_sem.at[5], partner)
        give_small.start()
        finish(4)
        at = slice(0, widths[section])
        give_mixer = remote(mixer_give.at[:, at], mixer_other.at[:, at], give_sem.at[6], give_sem.at[7], partner)
        give_mixer.start()
        finish(3)
        for a in range(5):
            both(scatter.sent, a)
        give_small.wait()
        give_mixer.wait_send()
        arrived(mixer_other.at[:, 0 : widths[1 - section]], give_sem.at[7])


    def same(lag):
        seg = seg_col[...] + jnp.zeros((tokens, 128), jnp.int32)
        row = lax.broadcasted_iota(jnp.int32, (tokens, 128), 0)
        return jnp.where((seg == pltpu.roll(seg, lag, 0)) & (row % MBT >= lag), 1.0, 0.0)

    def pieces(j):
        at = [slice(i * channels + j * 128, i * channels + (j + 1) * 128) for i in range(3)]
        return [proj[:, a] for a in at], at

    def first():
        gather, scatter = movers(3 * channels)
        gather_most(gather)
        pl.semaphore_signal(go, inc=1, device_id=partner, device_id_type=MESH)
        norm_rows(own)
        gather.last(0)
        project(3 * channels // 128)
        for j in range(channels // 128):
            (b, c, e), _ = pieces(j)
            at = slice(j * 128, (j + 1) * 128)
            product = b * e
            total = taps[0:1, at] * product
            for lag in (1, 2):
                total = total + taps[lag : lag + 1, at] * (pltpu.roll(product, lag, 0) * same(lag))
            mixed[:, at] = total
            mixer[:, at] = (c * total).astype(BF)
        gather.last(1)

        after_mixer(own, lambda: gather.relay(2), lambda: gather.relay(3))
        ffn_forward(gather)
        spread(1, hidden, w_down, padded, part)
        sum_over_mates(1, result, add_middle)
        give = remote(result, sent, give_sem.at[0], give_sem.at[1], partner)
        give.start()
        give.wait_send()
        arrived(top, give_sem.at[3])
        ffn_backward(gather, scatter, lambda: release(gather, scatter, 3), nothing)
        for j in range(channels // 128):
            (b, c, e), at = pieces(j)
            lane = slice(j * 128, (j + 1) * 128)
            grad_y = dot(grad_mid[...], matrix(w_mix, lane))
            product = b * e
            grad_mixed = grad_y * c
            grad_product = taps[0:1, lane] * grad_mixed
            sums = [jnp.sum(grad_mixed * product, axis=0, keepdims=True)]
            for lag in (1, 2):
                masked = grad_mixed * same(lag)
                sums.append(jnp.sum(masked * pltpu.roll(product, lag, 0), axis=0, keepdims=True))
                grad_product = grad_product + taps[lag : lag + 1, lane] * pltpu.roll(masked, tokens - lag, 0)
            for k in range(3):
                small[3:4, at[k]] = sums[k]
            grad_proj[:, at[0]] = (grad_product * e).astype(BF)
            grad_proj[:, at[1]] = (grad_y * mixed[:, lane]).astype(BF)
            grad_proj[:, at[2]] = (grad_product * b).astype(BF)
        mixer_back(gather, scatter, own, 3 * channels)
        wrap_up(scatter, 0)


    half = channels // 3
    lane_of = lax.broadcasted_iota(jnp.int32, (1, half), 1)
    keep = [jnp.where(lane_of // HEAD == k, 1.0, 0.0) for k in (0, 1)]

    def per_head(values):
        first_sum = jnp.sum(values * keep[0], axis=-1, keepdims=True)
        second_sum = jnp.sum(values * keep[1], axis=-1, keepdims=True)
        return (first_sum * keep[0] + second_sum * keep[1]) * (1.0 / HEAD)

    def across(values):
        low = lane_of % HEAD < HEAD // 2
        return jnp.where(low, pltpu.roll(values, half - HEAD // 2, 1), pltpu.roll(values, HEAD // 2, 1))

    def allowed(block):
        at = slice(block * MBT, (block + 1) * MBT)
        t = lax.broadcasted_iota(jnp.int32, (MBT, MBT), 0)
        u = lax.broadcasted_iota(jnp.int32, (MBT, MBT), 1)
        return jnp.where((seg_col[at, :] == seg_row[:, at]) & (u <= t), 1.0, 0.0)

    def turn_tables():
        for block in range(blocks):
            at = slice(block * MBT, (block + 1) * MBT)
            offset = jnp.sum(allowed(block), axis=1, keepdims=True) - 1.0
            column = lax.broadcasted_iota(jnp.int32, (MBT, MBT), 1).astype(F32)
            pick = jnp.where(column == offset, 1.0, 0.0).astype(BF)
            for k in (0, 1):
                turns[k, at, :] = dot(pick, tables[k, 0]) + dot(pick, tables[k, 1]) + dot(pick, tables[k, 2])

    inv_sqrt = HEAD ** (-0.5)

    def masked(i, block, k):
        at = slice(block * MBT, (block + 1) * MBT)
        return heads[i, at, :] * keep[k].astype(BF)

    def second():
        gather, scatter = movers(5 * half)
        turn_tables()
        top[...] = own[...]
        grad_proj[:, 5 * half :] = jnp.zeros((tokens, grad_proj.shape[1] - 5 * half), BF)
        pl.semaphore_wait(go, 1)
        gather_most(gather)
        gather.relay(2)
        arrived(sent, give_sem.at[1])
        norm_rows(sent)
        gather.last(0)
        project(5)
        for i in range(4):
            raw = proj[:, i * half : (i + 1) * half]
            gain = qk_gains[min(i // 3, 1) : min(i // 3, 1) + 1, :]
            value = raw * lax.rsqrt(per_head(raw * raw) + epsilon) * gain
            heads[i] = (value * turns[0] + across(value) * turns[1]).astype(BF)
        heads[4] = proj[:, 4 * half : 5 * half].astype(BF)
        for block in range(blocks):
            at = slice(block * MBT, (block + 1) * MBT)
            ok = allowed(block)
            for g in range(3):
                attended = jnp.zeros((MBT, half), F32)
                for k in (0, 1):
                    score = dot_bt(heads[g, at, :], masked(3, block, k)) * inv_sqrt
                    score = jnp.where(ok > 0.0, score, neg_large)
                    power = jnp.exp(score - jnp.max(score, axis=-1, keepdims=True))
                    weight = power / jnp.sum(power, axis=-1, keepdims=True)
                    soft[(block * 3 + g) * 2 + k] = weight
                    attended = attended + dot(weight.astype(BF), masked(4, block, k))
                mixer[at, g * half : (g + 1) * half] = attended.astype(BF)
        gather.last(1)
        after_mixer(sent, lambda: gather.relay(3), nothing)
        ffn_forward(gather)

        def late_start():
            spread(1, hidden, w_down, padded, late_part, False)
            release(gather, scatter, 3)

        ffn_backward(gather, scatter, late_start, lambda: sum_start(1, late_part))
        for block in range(blocks):
            at = slice(block * MBT, (block + 1) * MBT)
            grad_key = jnp.zeros((MBT, half), F32)
            grad_value = jnp.zeros((MBT, half), F32)
            for g in range(3):
                grad_att = dot(grad_mid[at, :], matrix(w_mix, slice(g * half, (g + 1) * half))).astype(BF)
                grad_query = jnp.zeros((MBT, half), F32)
                for k in (0, 1):
                    weight = soft[(block * 3 + g) * 2 + k]
                    grad_soft = dot_bt(grad_att, masked(4, block, k))
                    delta = jnp.sum(weight * grad_soft, axis=-1, keepdims=True)
                    grad_score = (weight * (grad_soft - delta)).astype(BF)
                    grad_query = grad_query + dot(grad_score, masked(3, block, k))
                    grad_key = grad_key + dot_at(grad_score, masked(g, block, k))
                    grad_value = grad_value + dot_at(weight.astype(BF), grad_att * keep[k].astype(BF))
                grad_heads[g, at, :] = grad_query * inv_sqrt
            grad_heads[3, at, :] = grad_key * inv_sqrt
            grad_proj[at, 4 * half : 5 * half] = grad_value.astype(BF)
            if block == 0:
                sum_middle(1, late_part, result, add_middle)
        gain_rows = [jnp.zeros((1, half), F32)] * 2
        for i in range(4):
            raw = proj[:, i * half : (i + 1) * half]
            which = min(i // 3, 1)
            gain = qk_gains[which : which + 1, :]
            grad = grad_heads[i]
            grad = grad * turns[0] - across(grad) * turns[1]
            factor = lax.rsqrt(per_head(raw * raw) + epsilon)
            weighted = grad * gain
            gain_rows[which] = gain_rows[which] + jnp.sum(grad * raw * factor, axis=0, keepdims=True)
            grad = factor * weighted - raw * (factor * factor * factor) * per_head(raw * weighted)
            grad_proj[:, i * half : (i + 1) * half] = grad.astype(BF)
        small[2:3, 0:half] = gain_rows[0]
        small[2:3, half : 2 * half] = gain_rows[1]
        mixer_back(gather, scatter, sent, 5 * half)
        give = remote(grad_in, top, give_sem.at[2], give_sem.at[3], partner)
        give.start()
        wrap_up(scatter, 1)
        sum_end(1, result)
        give.wait_send()

    pl.when(s == 0)(first)
    pl.when(s == 1)(second)


def rope_parts():
    frequency = rope_base ** (-np.arange(HEAD // 2, dtype=np.float64) * 2.0 / HEAD)
    angles = (np.arange(MBT, dtype=np.float32)[:, None] * frequency.astype(np.float32)[None, :]).astype(np.float32)
    cosine, sine = np.cos(angles.astype(np.float64)), np.sin(angles.astype(np.float64))
    both = (np.concatenate([cosine] * 4, axis=1), np.concatenate([-sine, sine, -sine, sine], axis=1))
    parts = []
    for table in both:
        left = table.astype(np.float32)
        for _ in range(3):
            piece = left.astype(jnp.bfloat16)
            parts.append(piece)
            left = left - piece.astype(np.float32)
    return jnp.asarray(np.stack(parts).reshape(2, 3, MBT, 2 * HEAD))


def both_blocks(own, segments, gains, taps, qk_gains, shards):
    tokens, width = own.shape
    channels, padded = shards[2].shape[-1], shards[4].shape[-1]
    wide = 3 * channels
    shape = jax.ShapeDtypeStruct
    rows, vmem = (tokens, width), pltpu.VMEM
    sums = [(2, ROWS, padded)] * 3 + [(2, ROWS, channels), (ROWS, wide), (ROWS, wide), (8, width), (8, width)]
    outs = [shape(rows, BF), shape(rows, BF)] + [shape(v, F32) for v in sums]
    n_vmem = len(outs)
    outs += [shape((4, 4, 2, ROWS, w), BF) for w in (padded, padded, padded, channels)] + [shape((2, 4, 4, ROWS, wide), BF)]
    scratch = [vmem((32, ROWS, w), BF) for w in (wide, channels, 2 * padded, padded)]
    scratch += [vmem((2, 3, ROWS, w), BF) for w in (padded, padded, padded, channels, wide)]
    scratch += [vmem((2, 4, 2, ROWS, padded), BF), vmem((2, 2, 4, ROWS, wide), BF), vmem((width, tokens), BF)]
    sizes = [width, wide, channels, width, 2 * padded, padded, width, width, width, width, width]
    scratch += [vmem((tokens, w), BF) for w in sizes]
    scratch += [
        vmem((4, 3, CHUNK, width), BF),
        vmem((CHUNK, width), F32),
        vmem((CHUNK, width), F32),
        vmem((tokens, wide), F32),
        vmem((tokens, channels), F32),
        vmem((2, tokens, padded), F32),
        vmem((5, tokens, 128), BF),
        vmem((6 * tokens // MBT, MBT, MBT), F32),
        vmem((2, tokens, 128), F32),
        vmem((4, tokens, 128), F32),
        vmem((ROWS, wide), F32),
        vmem((9, 8, width), F32),
        DMA((6,)),
        DMA((4,)),
        DMA((8, 16)),
        pltpu.SemaphoreType.REGULAR,
        DMA((4, 6)),
        DMA((4, 6)),
        DMA((8,)),
        DMA((2, 2)),
        DMA((10, 3)),
        DMA((10, 4)),
        DMA((10,)),
        pltpu.SemaphoreType.REGULAR((4,)),
        DMA((9,)),
        DMA((9,)),
    ]
    return pl.pallas_call(
        blocks_kernel,
        out_shape=outs,
        in_specs=[VM] * 7 + [ANY] * 5,
        out_specs=[VM] * n_vmem + [ANY] * 5,
        scratch_shapes=scratch,
        compiler_params=pltpu.CompilerParams(collective_id=0, has_side_effects=True, vmem_limit_bytes=60 * MIB),
        name="both_blocks",
    )(own, segments[:, None], segments[None, :], gains, taps, qk_gains, rope_parts(), *shards)[:n_vmem]


def local(ends, segment_ids, norm_gains, conv_in, conv_kernel, qkv_weight, qk_gains, mix_out, gate_up, down):
    is_first = lax.axis_index(SEC) == 0
    channels = mix_out.shape[1]
    hidden = gate_up.shape[3]
    padded = (hidden + 255) // 256 * 256
    kv, group, head = qkv_weight.shape[1], qkv_weight.shape[2] - 2, qkv_weight.shape[3]
    qkv_width = kv * (group + 2) * head
    taps = conv_kernel.shape[0]
    spare = ((0, 0), (0, padded - hidden))

    conv_rows = conv_in.reshape(ROWS, taps * channels)
    qkv_rows = qkv_weight.transpose(0, 2, 1, 3).reshape(ROWS, qkv_width)
    qkv_rows = jnp.pad(qkv_rows, ((0, 0), (0, taps * channels - qkv_width)))
    mix_rows = mix_out[0].T
    mix_turned = mix_rows.reshape(2 * ROWS, kv, group, head).transpose(0, 2, 1, 3).reshape(2 * ROWS, channels)
    gate_rows = jnp.pad(gate_up[0], ((0, 0),) + spare).reshape(2, ROWS, 2 * padded)
    down_rows = jnp.pad(down[0].T, spare).reshape(2, ROWS, padded)
    gains = jnp.concatenate([qk_gains, qk_gains], axis=1)
    shards = (
        jnp.where(is_first, conv_rows, qkv_rows),
        jnp.where(is_first, qkv_rows, conv_rows),
        jnp.where(is_first, mix_rows, mix_turned).reshape(2, ROWS, channels),
        gate_rows,
        down_rows,
    )
    result, grad_in, sum_gate, sum_up, sum_down, sum_mix, mixer_own, mixer_other, small_own, small_other = both_blocks(
        ends[0], segment_ids, norm_gains[0], conv_kernel, gains, shards
    )
    conv_grad = jnp.where(is_first, mixer_own, mixer_other)
    qkv_grad = jnp.where(is_first, mixer_other, mixer_own)[:, :qkv_width].reshape(ROWS, group + 2, kv, head)
    of_first = jnp.where(is_first, small_own, small_other)
    of_second = jnp.where(is_first, small_other, small_own)
    mix_grad = sum_mix.reshape(2 * ROWS, channels)
    mix_back = mix_grad.reshape(2 * ROWS, group, kv, head).transpose(0, 2, 1, 3).reshape(2 * ROWS, channels)
    return (
        result[None],
        grad_in.astype(F32)[None],
        small_own[None, 0:2],
        conv_grad.reshape(conv_in.shape),
        of_first[3, : taps * channels].reshape(taps, channels),
        qkv_grad.transpose(0, 2, 1, 3),
        of_second[2, : 4 * head].reshape(2, 2, head).sum(1),
        jnp.where(is_first, mix_grad, mix_back).T[None],
        jnp.stack([v.reshape(2 * ROWS, padded)[:, :hidden] for v in (sum_gate, sum_up)], axis=1)[None],
        sum_down.reshape(2 * ROWS, padded)[:, :hidden].T[None],
    )


def solution(mesh):
    dims = (
        P(SEC, DP, None),
        P(DP),
        P(SEC, None, None),
        P((SEC, DP), None, TEN),
        P(None, TEN),
        P((SEC, DP), TEN, None, None),
        P(),
        P(SEC, TEN, DP),
        P(SEC, DP, None, TEN),
        P(SEC, TEN, DP),
    )
    results = (dims[0], dims[0], dims[2], dims[3], dims[4], dims[5], dims[6], dims[7], dims[8], dims[9])
    return jax.shard_map(local, mesh=mesh, in_specs=dims, out_specs=results, check_vma=False)
```

```python
import functools

import jax
import jax.numpy as jnp
import numpy as np
from jax import lax
from jax.experimental import pallas as pl
from jax.experimental.pallas import tpu as pltpu
from jax.sharding import PartitionSpec as P

SEC, DP, TEN = "section", "dp", "tensor"
MESH = pl.DeviceIdType.MESH
F32, BF = jnp.float32, jnp.bfloat16
ANY = pl.BlockSpec(memory_space=pl.ANY)
VM = pl.BlockSpec(memory_space=pltpu.VMEM)
DMA = pltpu.SemaphoreType.DMA
MIB = 1 << 20

MBT = 128
ROWS = 48
CHUNK = 64
HEAD = 64
epsilon = 1e-05
rope_base = 1000000.0
neg_large = -1e30

HOME = (2, 2, 3, 1, 0)


def place():
    d = lax.axis_index(DP)
    return lax.axis_index(SEC), d // 4, d % 4, lax.axis_index(TEN)


def near(axis, y, x, step):
    return (y, (x + step) % 4) if axis == 0 else ((y + step) % 4, x)


def remote(src, dst, send_sem, recv_sem, device):
    return pltpu.make_async_remote_copy(
        src_ref=src, dst_ref=dst, send_sem=send_sem, recv_sem=recv_sem, device_id=device, device_id_type=MESH
    )


def arrived(ref, sem):
    pltpu.make_async_copy(ref, ref, sem).wait()


def cut(columns):
    return (columns // 128 + 1) // 2 * 128


def root(values):
    return lax.rsqrt(jnp.mean(values * values, axis=-1, keepdims=True) + epsilon)


def dot(a, b):
    return jnp.dot(a, b, preferred_element_type=F32)


def dot_bt(a, b):
    return lax.dot_general(a, b, (((1,), (1,)), ((), ())), preferred_element_type=F32)


def dot_at(a, b):
    return lax.dot_general(a, b, (((0,), (0,)), ((), ())), preferred_element_type=F32)


def norm_back(values, gain, grad):
    factor = root(values)
    weighted = grad * gain
    grad_in = factor * weighted - values * (factor * factor * factor) * jnp.mean(values * weighted, axis=-1, keepdims=True)
    return grad_in, jnp.sum(grad * values * factor, axis=0, keepdims=True)


def lanes(i, size=128, start=0):
    return pl.ds(pl.multiple_of(start + i * size, 128), size)


def times(count, body):
    def step(i, carry):
        body(i)
        return carry

    lax.fori_loop(0, count, step, 0)


def matrix(ref, columns):
    value = ref[:, :, columns]
    return value.reshape(value.shape[0] * value.shape[1], value.shape[2])


def add_rows(dst, pieces):
    rows = dst.shape[-2]
    three = len(dst.shape) == 3
    kind = BF if len(pieces) == 2 else F32

    def body(i):
        at = pl.ds(pl.multiple_of(i % (rows // 16) * 16, 16), 16)
        k = i // (rows // 16)
        get = (lambda r: r[k, at, :]) if three else (lambda r: r[at, :])
        total = get(pieces[0]).astype(kind)
        for p in pieces[1:]:
            total = total + get(p).astype(kind)
        if three:
            dst[k, at, :] = total.astype(dst.dtype)
        else:
            dst[at, :] = total.astype(dst.dtype)

    times((dst.shape[0] if three else 1) * (rows // 16), body)


class Gather:
    def __init__(self, weights, widths, shards, send_sem, recv_sem):
        self.weights, self.widths, self.shards = weights, widths, shards
        self.send_sem, self.recv_sem = send_sem, recv_sem
        self.s, self.y, self.x, self.z = place()

    def narrow(self, a, ref):
        return ref if self.widths[a] == ref.shape[-1] else ref.at[..., 0 : self.widths[a]]

    def block(self, a, h, yx):
        b = yx[0] * 4 + yx[1]
        return self.narrow(a, self.weights[a].at[h * 16 + b if a == 0 else b * 2 + h])

    def send(self, a, h, yx, lo, hi, to, src=None):
        ref = self.block(a, h, yx)
        if (lo, hi) != (0, self.widths[a]):
            ref = ref.at[:, lo:hi]
        recv = self.recv_sem.at[a * 2 + h, yx[0] * 4 + yx[1]]
        remote(ref if src is None else src, ref, self.send_sem.at[a], recv, (self.s, to[0] * 4 + to[1], self.z)).start()

    def wait(self, a, h, yx):
        arrived(self.block(a, h, yx), self.recv_sem.at[a * 2 + h, yx[0] * 4 + yx[1]])

    def near(self, axis, step):
        return near(axis, self.y, self.x, step)

    def start(self, arrays):
        for axis_of in (lambda h: h, lambda h: 1 - h):
            for a in arrays:
                for h in (0, 1):
                    src = None if self.shards[a] is None else self.shards[a].at[h]
                    for step in (1, -1):
                        self.send(a, h, (self.y, self.x), 0, self.widths[a], self.near(axis_of(h), step), src)

    def spread(self, arrays):
        for a in arrays:
            w = self.widths[a]
            c = cut(w)
            for h in (0, 1):
                for step, lo, hi in ((1, 0, c), (-1, c, w)):
                    src = self.near(h, -step)
                    self.wait(a, h, src)
                    self.send(a, h, src, lo, hi, self.near(h, step))
                    for on in (1, -1):
                        self.send(a, h, src, 0, w, self.near(1 - h, on))
        for a in arrays:
            for h in (0, 1):
                far = self.near(h, 2)
                self.wait(a, h, far)
                for on in (1, -1):
                    self.send(a, h, far, 0, self.widths[a], self.near(1 - h, on))

    def relay(self, a):
        w = self.widths[a]
        c = cut(w)
        for h in (0, 1):

            def body(j, h=h):
                line = self.near(h, j)
                for step, lo, hi in ((1, 0, c), (-1, c, w)):
                    src = near(1 - h, line[0], line[1], -step)
                    self.wait(a, h, src)
                    self.send(a, h, src, lo, hi, self.near(1 - h, step))

            times(4, body)

    def last(self, a):
        for h in (0, 1):

            def body(j, h=h):
                line = self.near(h, j)
                self.wait(a, h, near(1 - h, line[0], line[1], 2))

            times(4, body)

    def sent(self, a):
        arrived(self.narrow(a, self.weights[a].at[0:30]), self.send_sem.at[a])


class Scatter:
    def __init__(self, grads, weights, widths, extras, load_sem, recv_sem, send_sem, free):
        self.grads, self.weights, self.widths, self.extras = grads, weights, widths, extras
        self.load_sem, self.recv_sem, self.send_sem, self.free = load_sem, recv_sem, send_sem, free
        self.s, self.y, self.x, self.z = place()
        self.claimed = set()
        self.loads = {}

    def device(self, yx):
        return (self.s, yx[0] * 4 + yx[1], self.z)

    def near(self, axis, step):
        return near(axis, self.y, self.x, step)

    def release(self, home):
        for axis in (0, 1):
            for step in (1, -1):
                to = self.device(self.near(axis, step))
                pl.semaphore_signal(self.free.at[home], inc=1, device_id=to, device_id_type=MESH)

    def line(self, a, h, yx):
        if a == 4:
            ref = self.grads[a].at[h, yx[0]] if h == 0 else self.grads[a].at[h, :, yx[1]]
            return ref if self.widths[a] == ref.shape[-1] else ref.at[:, :, 0 : self.widths[a]]
        return self.grads[a].at[yx[0], :, h] if h == 0 else self.grads[a].at[:, yx[1], h]

    def room(self, a, h, lo, hi):
        ref = self.weights[HOME[a]].at[16 * h + lo : 16 * h + hi]
        start = self.widths[a] if a == 1 else 0
        if self.widths[a] != ref.shape[-1]:
            ref = ref.at[:, :, start : start + self.widths[a]]
        return ref

    def extra(self, a, h):
        ref = self.extras[a].at[h]
        return ref if self.widths[a] == ref.shape[-1] else ref.at[:, :, 0 : self.widths[a]]

    def move(self, a, h, i, src, dst, to):
        remote(src, dst, self.send_sem.at[a * 2 + h], self.recv_sem.at[a * 2 + h, i], self.device(to)).start()

    def load(self, a, h, i, src, dst):
        copy = pltpu.make_async_copy(src, dst, self.load_sem.at[a * 2 + h, i])
        copy.start()
        self.loads[a, h, i] = copy

    def begin(self, a, h):
        if HOME[a] not in self.claimed:
            pl.semaphore_wait(self.free.at[HOME[a]], 4)
            self.claimed.add(HOME[a])
        up, dn, far = (self.near(1 - h, step) for step in (1, -1, 2))
        self.move(a, h, 0, self.line(a, h, far).at[0:2], self.room(a, h, 0, 2), up)
        self.move(a, h, 0, self.line(a, h, far).at[2:4], self.room(a, h, 2, 4), dn)
        self.load(a, h, 0, self.line(a, h, up).at[0:2], self.room(a, h, 12, 14))
        self.load(a, h, 1, self.line(a, h, dn).at[2:4], self.room(a, h, 14, 16))

    def begin_near(self, a, h):
        up, dn = (self.near(1 - h, step) for step in (1, -1))
        self.move(a, h, 1, self.line(a, h, up).at[2:4], self.room(a, h, 6, 8), up)
        self.move(a, h, 1, self.line(a, h, dn).at[0:2], self.room(a, h, 8, 10), dn)

    def pass_on(self, a, h):
        up, dn = (self.near(1 - h, step) for step in (1, -1))
        self.loads[a, h, 0].wait()
        self.loads[a, h, 1].wait()
        arrived(self.room(a, h, 0, 4), self.recv_sem.at[a * 2 + h, 0])
        mine = self.room(a, h, 12, 16)
        add_rows(mine, [mine, self.room(a, h, 0, 4)])
        self.move(a, h, 1, self.room(a, h, 12, 14), self.room(a, h, 4, 6), up)
        self.move(a, h, 1, self.room(a, h, 14, 16), self.room(a, h, 10, 12), dn)
        self.load(a, h, 2, self.line(a, h, (self.y, self.x)), self.room(a, h, 0, 4))

    def own(self, h):
        return self.x if h == 0 else self.y

    def turn(self, a, h):
        w = self.widths[a]
        c = cut(w)
        self.loads[a, h, 2].wait()
        arrived(self.room(a, h, 4, 12), self.recv_sem.at[a * 2 + h, 1])
        total, extra = self.room(a, h, 0, 4), self.extra(a, h)
        add_rows(total, [total, self.room(a, h, 4, 8), self.room(a, h, 8, 12)])
        up, dn = (self.near(h, step) for step in (1, -1))
        far, i_up, i_dn = ((self.own(h) + step) % 4 for step in (2, 1, -1))
        self.move(a, h, 2, total.at[far, :, 0:c], extra.at[0, :, 0:c], up)
        self.move(a, h, 2, total.at[far, :, c:w], extra.at[0, :, c:w], dn)
        self.move(a, h, 3, total.at[i_up, :, c:w], extra.at[1, :, c:w], up)
        self.move(a, h, 3, total.at[i_dn, :, 0:c], extra.at[2, :, 0:c], dn)

    def pass_back(self, a, h):
        w = self.widths[a]
        c = cut(w)
        total, extra = self.room(a, h, 0, 4), self.extra(a, h)
        up, dn = (self.near(h, step) for step in (1, -1))
        i_up, i_dn = ((self.own(h) + step) % 4 for step in (1, -1))
        arrived(extra.at[0], self.recv_sem.at[a * 2 + h, 2])
        lo, hi = extra.at[0, :, 0:c], extra.at[0, :, c:w]
        add_rows(lo, [lo, total.at[i_up, :, 0:c]])
        self.move(a, h, 3, lo, extra.at[1, :, 0:c], up)
        add_rows(hi, [hi, total.at[i_dn, :, c:w]])
        self.move(a, h, 3, hi, extra.at[2, :, c:w], dn)

    def finish(self, a, h, out):
        total, extra = self.room(a, h, 0, 4), self.extra(a, h)
        arrived(extra.at[1:3], self.recv_sem.at[a * 2 + h, 3])
        add_rows(out, [total.at[self.own(h)], extra.at[1], extra.at[2]])

    def sent(self, a, h):
        arrived(self.room(a, h, 0, 15), self.send_sem.at[a * 2 + h])


def blocks_kernel(
    own,
    seg_row,
    gains,
    taps,
    qk_pair,
    tables,
    shard_mix,
    shard_down,
    shard_conv,
    shard_qkv,
    shard_gate,
    result,
    grad_in,
    sum_pair,
    sum_down,
    sum_mix,
    sum_conv,
    sum_qkv,
    gains_out,
    taps_out,
    qk_out,
    grad_gate,
    grad_up,
    grad_down,
    grad_mix,
    grad_mixer,
    w_mixer,
    w_mix,
    w_gate,
    w_down,
    x_gate,
    x_up,
    x_down,
    x_mix,
    x_mixer,
    stage,
    stage_mixer,
    turned,
    normed,
    grad_proj,
    mixer,
    ffn_in,
    grad_pair,
    hidden,
    top,
    grad_mid,
    sent,
    part,
    late_part,
    inbox,
    middle,
    grad_chunk,
    proj,
    mixed,
    gate_up,
    heads,
    soft,
    turns,
    grad_heads,
    mixer_give,
    small_in,
    small,
    small_other,
    seg_wide,
    qk_gains,
    early_grad,
    copy_sem,
    gather_send,
    gather_recv,
    go,
    send_sem,
    recv_sem,
    give_sem,
    stage_sem,
    load_sem,
    sum_recv,
    sum_send,
    free,
    small_send,
    small_recv,
):
    s, y, x, z = place()
    d = y * 4 + x
    mates = [(s, d, (z + j) % 4) for j in (1, 2, 3)]
    partner = (1 - s, d, z)
    plane = [[(s, v[0] * 4 + v[1], z) for v in (near(k, y, x, j) for j in (1, 2, 3))] for k in (0, 1)]
    tokens, width = own.shape
    channels = mixer.shape[1]
    padded = hidden.shape[1]
    blocks = tokens // MBT
    weights = (w_mixer, w_mix, w_gate, w_down)
    grads = (grad_gate, grad_up, grad_down, grad_mix, grad_mixer)
    extras = (x_gate, x_up, x_down, x_mix, x_mixer)
    shards = (None, None, shard_gate, None)

    def movers(wide):
        gather = Gather(weights, (wide, channels, 2 * padded, padded), shards, gather_send, gather_recv)
        widths = (padded, padded, padded, channels, wide)
        return gather, Scatter(grads, weights, widths, extras, load_sem, sum_recv, sum_send, free)

    barrier = pltpu.get_barrier_semaphore()
    greeted = [partner] + mates + plane[0] + plane[1]
    for device in greeted:
        pl.semaphore_signal(barrier, inc=1, device_id=device, device_id_type=MESH)
    pl.semaphore_wait(barrier, len(greeted))

    def rows(k):
        return pl.ds(pl.multiple_of(k % 4 * CHUNK, CHUNK), CHUNK)

    mine = rows(z)


    index = d * 2
    third = taps.shape[1]
    conv_parts = [slice(k * third, (k + 1) * third) for k in range(3)]
    qkv_part = slice(0, shard_qkv.shape[1])
    swapped = [remote(shard_qkv, w_mixer.at[d, :, qkv_part], copy_sem.at[0], copy_sem.at[1], partner)]
    for k in range(3):
        to = w_mixer.at[16 + d, :, conv_parts[k]]
        swapped.append(remote(shard_conv.at[k], to, copy_sem.at[8 + k], copy_sem.at[11 + k], partner))
    kept = [pltpu.make_async_copy(shard_qkv, w_mixer.at[16 + d, :, qkv_part], copy_sem.at[2])]
    for k in range(3):
        kept.append(pltpu.make_async_copy(shard_conv.at[k], w_mixer.at[d, :, conv_parts[k]], copy_sem.at[2 if k == 0 else 5 + k]))

    def swap_start(section):
        for copy in swapped[:1] if section == 0 else swapped[1:]:
            copy.start()
        for copy in kept[1:] if section == 0 else kept[:1]:
            copy.start()

    def swap_end(section):
        for copy in kept[1:] if section == 0 else kept[:1]:
            copy.wait()
        for copy in swapped[:1] if section == 0 else swapped[1:]:
            copy.wait_send()
        for copy in swapped[1:] if section == 0 else swapped[:1]:
            copy.wait_recv()

    fills = [pltpu.make_async_copy(shard_gate, w_gate.at[pl.ds(index, 2)], copy_sem.at[4])]
    for copy in fills:
        copy.start()

    def regroup(values, outer, inner):
        parts = [values[:, (o * inner + i) * HEAD : (o * inner + i + 1) * HEAD] for i in range(inner) for o in range(outer)]
        return jnp.concatenate(parts, axis=1)

    def place_shards(section):
        values = shard_mix[...].astype(F32)
        values = regroup(values, 2, 3) if section == 1 else values
        w_mix[pl.ds(index, 2)] = values.astype(BF).reshape(2, ROWS, channels)
        inner = shard_down.shape[1]
        w_down[pl.ds(index, 2), :, inner - inner % 128 :] = jnp.zeros((2, ROWS, padded - inner + inner % 128), BF)
        w_down[pl.ds(index, 2), :, 0:inner] = shard_down[...].reshape(2, ROWS, inner)

    small[...] = jnp.zeros_like(small)
    seg_wide[...] = jnp.broadcast_to(seg_row[...].astype(F32), (MBT, tokens)).T

    def gather_most(gather, section):
        place_shards(section)
        gather.start((1,))
        swap_end(section)
        gather.start((0,))
        gather.start((2, 3))
        for copy in fills:
            copy.wait()
        for arrays in ((0, 1), (2, 3)):
            gather.spread(arrays)
        for a in (0, 1):
            gather.relay(a)


    def spread(phase, a, weight, depth, to, send=True):
        for k in range(2):
            value = weight[k * 16 : k * 16 + 16, :, 0:depth].reshape(16 * ROWS, depth)
            columns = slice(k * 16 * ROWS, (k + 1) * 16 * ROWS)
            to[:, columns] = dot_bt(a[:, 0:depth], value).astype(BF)
            if send:
                sum_start(phase, to, columns)

    def sum_start(phase, src, columns=slice(None)):
        for j in (2, 1, 3):
            sems = (send_sem.at[phase, j - 1], recv_sem.at[phase, j - 1])
            remote(src.at[rows(z + j), columns], inbox.at[phase, j - 1, :, columns], *sems, mates[j - 1]).start()

    def sum_middle(phase, src, full, work):
        total = src[mine, :].astype(F32)
        for j in range(3):
            arrived(inbox.at[phase, j], recv_sem.at[phase, j])
            total = total + inbox[phase, j].astype(F32)
        full[mine, :] = work(total).astype(BF)
        for j in (2, 1, 3):
            sems = (send_sem.at[phase, 2 + j], recv_sem.at[phase, 2 + j])
            remote(full.at[mine], full.at[mine], *sems, mates[j - 1]).start()

    def sum_end(phase, full):
        for j in (1, 2, 3):
            arrived(full.at[rows(z - j)], recv_sem.at[phase, 2 + j])
        for i in range(6):
            arrived(full.at[mine], send_sem.at[phase, i])

    def nothing():
        pass

    def sum_over_mates(phase, full, work, first_wait=nothing, second_wait=nothing):
        first_wait()
        sum_middle(phase, part, full, work)
        second_wait()
        sum_end(phase, full)


    def norm_rows(src):
        def body(i):
            values = src[rows(i), :].astype(F32)
            normed[rows(i), :] = (values * root(values) * gains[0:1, :]).astype(BF)

        times(tokens // CHUNK, body)

    def project(count):
        def body(j):
            proj[:, lanes(j)] = dot(normed[...], matrix(w_mixer, lanes(j)))

        times(count, body)

    def after_mixer(src, first_wait, second_wait):
        def work(total):
            value = src[mine, :].astype(F32) + total
            middle[...] = value
            return value * root(value) * gains[1:2, :]

        spread(0, mixer, w_mix, channels, part)
        sum_over_mates(0, ffn_in, work, first_wait, second_wait)

    def ffn_forward(gather):
        gather.last(2)
        for j in range(padded // 256):
            at = slice(j * 256, (j + 1) * 256)
            gate = dot(ffn_in[...], matrix(w_gate, at))
            up = dot(ffn_in[...], matrix(w_gate, slice(padded + j * 256, padded + (j + 1) * 256)))
            gate_up[0, :, at] = gate
            gate_up[1, :, at] = up
            hidden[:, at] = (gate * jax.nn.sigmoid(gate) * up).astype(BF)
        gather.last(3)

    def add_middle(total):
        return middle[...] + total

    staged = {}

    def drain(which, slot):
        if (which, slot) in staged:
            arrived(staged.pop((which, slot)), stage_sem.at[which, slot])

    def drain_all():
        for key in list(staged):
            drain(*key)

    def weight_grad(a, left, right, start=0):
        size = right.shape[-1] // 2 if a < 2 else right.shape[-1]
        tile = 896 if size % 896 == 0 else size // 3 if size % 384 == 0 and size > 384 else size
        buffer = stage_mixer if a == 4 else stage
        which = 1 if a == 4 else 0
        if left is not None:
            turned[...] = left[...].T
        whole = size == buffer.shape[-1]
        for t in range(4):
            slot = t % 2
            room = buffer.at[slot] if whole else buffer.at[slot, :, :, :, 0:size]
            drain(which, slot)
            for k in range(2):
                at = t * 384 + k * 192
                for j in range(size // tile):
                    columns = slice(start + j * tile, start + (j + 1) * tile)
                    value = dot(turned[at : at + 192, :], right[:, columns]).astype(BF)
                    for i in range(4):
                        b = k * 4 + i
                        b = (b // 4, b % 4) if a == 4 else (b // 2, b % 2)
                        buffer[slot, b[0], b[1], :, j * tile : (j + 1) * tile] = value[i * ROWS : (i + 1) * ROWS, :]
            to = grads[a].at[t // 2, t % 2 * 2 : t % 2 * 2 + 2] if a == 4 else grads[a].at[t]
            to = to if whole or a < 4 else to.at[:, :, :, 0:size]
            pltpu.make_async_copy(room, to, stage_sem.at[which, slot]).start()
            staged[which, slot] = room

    def release(gather, scatter, a):
        gather.sent(a)
        scatter.release(a)

    def ffn_late(scatter):
        drain_all()
        both(scatter.begin, 2)
        both(scatter.begin_near, 2)
        weight_grad(0, ffn_in, grad_pair)
        drain_all()
        both(scatter.begin, 0)
        both(scatter.begin_near, 0)
        weight_grad(1, None, grad_pair, padded)
        drain_all()
        both(scatter.begin, 1)
        both(scatter.begin_near, 1)
        both(scatter.pass_on, 2)

    def mixer_hooks(gather, scatter, depth):
        def early():
            release(gather, scatter, 1)
            release(gather, scatter, 0)
            weight_grad(4, normed, grad_proj.at[:, 0:depth])
            both(scatter.pass_on, 0)
            drain_all()
            both(scatter.begin, 4)
            both(scatter.begin_near, 4)

        def late():
            weight_grad(3, grad_mid, mixer)
            both(scatter.pass_on, 1)
            drain_all()
            both(scatter.begin, 3)
            both(scatter.begin_near, 3)
            both(scatter.pass_on, 4)

        return early, late

    def ffn_grads():
        for j in range(padded // 256):
            at = slice(j * 256, (j + 1) * 256)
            grad = dot(top[...], matrix(w_down, at))
            gate, up = gate_up[0, :, at], gate_up[1, :, at]
            sig = jax.nn.sigmoid(gate)
            grad_pair[:, at] = (grad * up * sig * (1.0 + gate * (1.0 - sig))).astype(BF)
            grad_pair[:, padded + j * 256 : padded + (j + 1) * 256] = (grad * gate * sig).astype(BF)

    def ffn_early_grad(gather):
        gather.last(3)
        for j in range(padded // 256):
            at = slice(j * 256, (j + 1) * 256)
            early_grad[:, at] = dot(top[...], matrix(w_down, at))

    def ffn_both_ways(gather):
        gather.last(2)
        for j in range(padded // 256):
            at = slice(j * 256, (j + 1) * 256)
            gate = dot(ffn_in[...], matrix(w_gate, at))
            up = dot(ffn_in[...], matrix(w_gate, slice(padded + j * 256, padded + (j + 1) * 256)))
            grad = early_grad[:, at]
            sig = jax.nn.sigmoid(gate)
            act = gate * sig
            hidden[:, at] = (act * up).astype(BF)
            grad_pair[:, at] = (grad * up * sig * (1.0 + gate * (1.0 - sig))).astype(BF)
            grad_pair[:, padded + j * 256 : padded + (j + 1) * 256] = (grad * act).astype(BF)

    def ffn_backward(early, late):
        def work(total):
            grad, small[1:2, :] = norm_back(middle[...], gains[1:2, :], total)
            grad = top[mine, :].astype(F32) + grad
            grad_chunk[...] = grad
            return grad

        spread(2, grad_pair, w_gate, 2 * padded, part)

        sum_over_mates(2, grad_mid, work, early, late)

    def mixer_back(src, depth, early, late):
        def work(total):
            grad, small[0:1, :] = norm_back(src[mine, :].astype(F32), gains[0:1, :], total)
            return grad_chunk[...] + grad

        spread(3, grad_proj, w_mixer, depth, part)

        sum_over_mates(3, grad_in, work, early, late)

    def small_start(k):
        group = plane[k] if k < 2 else mates
        for j in range(3):
            i = k * 3 + j
            remote(small, small_in.at[i], small_send.at[i], small_recv.at[i], group[j]).start()

    def small_add(k):
        for j in range(3):
            arrived(small, small_send.at[k * 3 + j])
            arrived(small, small_recv.at[k * 3 + j])
        summed = small[...] + small_in[k * 3] + small_in[k * 3 + 1] + small_in[k * 3 + 2]
        if k == 2:
            row = lax.broadcasted_iota(jnp.int32, summed.shape, 0)
            summed = jnp.where(row == 3, small[...], summed)
        small[...] = summed

    def both(step, a):
        for h in (0, 1):
            step(a, h)

    widths = (3 * channels, 5 * channels // 3)

    def wrap_up(scatter, section):
        def finish(a):
            for h in (0, 1):
                if a == 4:
                    own_sum = (sum_conv, sum_qkv)[section]
                    scatter.finish(a, h, own_sum if h == section else mixer_give.at[:, 0 : widths[section]])
                else:
                    scatter.finish(a, h, sum_pair.at[a, h] if a < 2 else (sum_down, sum_mix)[a - 2].at[h])

        small_start(0)
        both(scatter.turn, 2)
        both(scatter.pass_on, 3)
        both(scatter.turn, 0)
        small_add(0)
        small_start(1)
        both(scatter.turn, 4)
        both(scatter.pass_back, 2)
        both(scatter.turn, 1)
        both(scatter.pass_back, 0)
        small_add(1)
        small_start(2)
        both(scatter.turn, 3)
        both(scatter.pass_back, 4)
        both(scatter.pass_back, 1)
        finish(2)
        both(scatter.pass_back, 3)
        finish(0)
        small_add(2)
        give_small = remote(small, small_other, give_sem.at[4], give_sem.at[5], partner)
        give_small.start()
        finish(4)
        at = slice(0, widths[section])
        give_mixer = remote(mixer_give.at[:, at], (sum_conv, sum_qkv)[section], give_sem.at[6], give_sem.at[7], partner)
        give_mixer.start()
        finish(1)
        finish(3)
        for a in range(5):
            both(scatter.sent, a)
        give_small.wait()
        give_mixer.wait_send()
        arrived((sum_qkv, sum_conv)[section], give_sem.at[7])
        of_conv, of_qk = (small, small_other) if section == 0 else (small_other, small)
        if section == 1:
            for h in (0, 1):
                sum_mix[h] = regroup(sum_mix[h], 3, 2)
        gains_out[...] = small[0:2, :]
        for k in range(3):
            taps_out[k : k + 1, :] = of_conv[3:4, conv_parts[k]]
        for k in (0, 1):
            both_heads = of_qk[2:3, k * 128 : (k + 1) * 128]
            qk_out[k : k + 1, :] = (both_heads + pltpu.roll(both_heads, HEAD, 1))[:, 0:HEAD]


    def same(lag):
        seg = seg_wide[...]
        row = lax.broadcasted_iota(jnp.int32, (tokens, 128), 0)
        return jnp.where((seg == pltpu.roll(seg, lag, 0)) & (row % MBT >= lag), 1.0, 0.0)

    def pieces(j):
        at = [slice(i * channels + j * 128, i * channels + (j + 1) * 128) for i in range(3)]
        return [proj[:, a] for a in at], at

    def first():
        gather, scatter = movers(3 * channels)
        swap_start(0)
        gather_most(gather, 0)
        pl.semaphore_signal(go, inc=1, device_id=partner, device_id_type=MESH)
        norm_rows(own)
        gather.last(0)
        project(3 * channels // 128)
        for j in range(channels // 128):
            (b, c, e), _ = pieces(j)
            at = slice(j * 128, (j + 1) * 128)
            product = b * e
            total = taps[0:1, at] * product
            for lag in (1, 2):
                total = total + taps[lag : lag + 1, at] * (pltpu.roll(product, lag, 0) * same(lag))
            mixed[:, at] = total
            mixer[:, at] = (c * total).astype(BF)
        gather.last(1)

        after_mixer(own, lambda: gather.relay(2), lambda: gather.relay(3))
        ffn_forward(gather)
        spread(1, hidden, w_down, padded, part)
        sum_over_mates(1, result, add_middle)
        give = remote(result, sent, give_sem.at[0], give_sem.at[1], partner)
        give.start()
        give.wait_send()
        arrived(top, give_sem.at[3])

        def ffn_early():
            release(gather, scatter, 2)
            release(gather, scatter, 3)
            weight_grad(2, top, hidden)

        ffn_grads()
        ffn_backward(ffn_early, lambda: ffn_late(scatter))
        for j in range(channels // 128):
            (b, c, e), at = pieces(j)
            lane = slice(j * 128, (j + 1) * 128)
            grad_y = dot(grad_mid[...], matrix(w_mix, lane))
            product = b * e
            grad_mixed = grad_y * c
            grad_product = taps[0:1, lane] * grad_mixed
            sums = [jnp.sum(grad_mixed * product, axis=0, keepdims=True)]
            for lag in (1, 2):
                masked = grad_mixed * same(lag)
                sums.append(jnp.sum(masked * pltpu.roll(product, lag, 0), axis=0, keepdims=True))
                grad_product = grad_product + taps[lag : lag + 1, lane] * pltpu.roll(masked, tokens - lag, 0)
            for k in range(3):
                small[3:4, at[k]] = sums[k]
            grad_proj[:, at[0]] = (grad_product * e).astype(BF)
            grad_proj[:, at[1]] = (grad_y * mixed[:, lane]).astype(BF)
            grad_proj[:, at[2]] = (grad_product * b).astype(BF)

        early, late = mixer_hooks(gather, scatter, 3 * channels)
        mixer_back(own, 3 * channels, early, late)
        wrap_up(scatter, 0)


    half = channels // 3
    lane_of = lax.broadcasted_iota(jnp.int32, (1, half), 1)
    keep = [jnp.where(lane_of // HEAD == k, 1.0, 0.0) for k in (0, 1)]

    def per_head(values):
        first_sum = jnp.sum(values * keep[0], axis=-1, keepdims=True)
        second_sum = jnp.sum(values * keep[1], axis=-1, keepdims=True)
        return (first_sum * keep[0] + second_sum * keep[1]) * (1.0 / HEAD)

    def across(values):
        low = lane_of % HEAD < HEAD // 2
        return jnp.where(low, pltpu.roll(values, half - HEAD // 2, 1), pltpu.roll(values, HEAD // 2, 1))

    def allowed(block):
        at = slice(block * MBT, (block + 1) * MBT)
        t = lax.broadcasted_iota(jnp.int32, (MBT, MBT), 0)
        u = lax.broadcasted_iota(jnp.int32, (MBT, MBT), 1)
        return jnp.where((seg_wide[at, :] == seg_row[:, at].astype(F32)) & (u <= t), 1.0, 0.0)

    def turn_tables():
        for block in range(blocks):
            at = slice(block * MBT, (block + 1) * MBT)
            offset = jnp.sum(allowed(block), axis=1, keepdims=True) - 1.0
            column = lax.broadcasted_iota(jnp.int32, (MBT, MBT), 1).astype(F32)
            pick = jnp.where(column == offset, 1.0, 0.0).astype(BF)
            for k in (0, 1):
                turns[k, at, :] = dot(pick, tables[k, 0]) + dot(pick, tables[k, 1]) + dot(pick, tables[k, 2])

    inv_sqrt = HEAD ** (-0.5)

    def masked(i, block, k):
        at = slice(block * MBT, (block + 1) * MBT)
        return heads[i, at, :] * keep[k].astype(BF)

    def second():
        gather, scatter = movers(5 * half)
        swap_start(1)
        qk_gains[...] = jnp.concatenate([qk_pair[...], qk_pair[...]], axis=1)
        turn_tables()
        top[...] = own[...]
        grad_proj[:, 5 * half :] = jnp.zeros((tokens, grad_proj.shape[1] - 5 * half), BF)
        pl.semaphore_wait(go, 1)
        gather_most(gather, 1)
        gather.relay(2)
        arrived(sent, give_sem.at[1])
        norm_rows(sent)
        gather.last(0)
        project(5)
        for i in range(4):
            raw = proj[:, i * half : (i + 1) * half]
            gain = qk_gains[min(i // 3, 1) : min(i // 3, 1) + 1, :]
            value = raw * lax.rsqrt(per_head(raw * raw) + epsilon) * gain
            heads[i] = (value * turns[0] + across(value) * turns[1]).astype(BF)
        heads[4] = proj[:, 4 * half : 5 * half].astype(BF)
        for block in range(blocks):
            at = slice(block * MBT, (block + 1) * MBT)
            ok = allowed(block)
            for g in range(3):
                attended = jnp.zeros((MBT, half), F32)
                for k in (0, 1):
                    score = dot_bt(heads[g, at, :], masked(3, block, k)) * inv_sqrt
                    score = jnp.where(ok > 0.0, score, neg_large)
                    power = jnp.exp(score - jnp.max(score, axis=-1, keepdims=True))
                    weight = power / jnp.sum(power, axis=-1, keepdims=True)
                    soft[(block * 3 + g) * 2 + k] = weight
                    attended = attended + dot(weight.astype(BF), masked(4, block, k))
                mixer[at, g * half : (g + 1) * half] = attended.astype(BF)
        gather.last(1)
        after_mixer(sent, lambda: gather.relay(3), lambda: ffn_early_grad(gather))
        ffn_both_ways(gather)

        def ffn_early():
            release(gather, scatter, 2)
            spread(1, hidden, w_down, padded, late_part, False)
            release(gather, scatter, 3)
            weight_grad(2, top, hidden)

        def late():
            sum_start(1, late_part)
            ffn_late(scatter)

        ffn_backward(ffn_early, late)
        for block in range(blocks):
            at = slice(block * MBT, (block + 1) * MBT)
            grad_key = jnp.zeros((MBT, half), F32)
            grad_value = jnp.zeros((MBT, half), F32)
            for g in range(3):
                grad_att = dot(grad_mid[at, :], matrix(w_mix, slice(g * half, (g + 1) * half))).astype(BF)
                grad_query = jnp.zeros((MBT, half), F32)
                for k in (0, 1):
                    weight = soft[(block * 3 + g) * 2 + k]
                    grad_soft = dot_bt(grad_att, masked(4, block, k))
                    delta = jnp.sum(weight * grad_soft, axis=-1, keepdims=True)
                    grad_score = (weight * (grad_soft - delta)).astype(BF)
                    grad_query = grad_query + dot(grad_score, masked(3, block, k))
                    grad_key = grad_key + dot_at(grad_score, masked(g, block, k))
                    grad_value = grad_value + dot_at(weight.astype(BF), grad_att * keep[k].astype(BF))
                grad_heads[g, at, :] = grad_query * inv_sqrt
            grad_heads[3, at, :] = grad_key * inv_sqrt
            grad_proj[at, 4 * half : 5 * half] = grad_value.astype(BF)
            if block == 0:
                sum_middle(1, late_part, result, add_middle)
        gain_rows = [jnp.zeros((1, half), F32)] * 2
        for i in range(4):
            raw = proj[:, i * half : (i + 1) * half]
            which = min(i // 3, 1)
            gain = qk_gains[which : which + 1, :]
            grad = grad_heads[i]
            grad = grad * turns[0] - across(grad) * turns[1]
            factor = lax.rsqrt(per_head(raw * raw) + epsilon)
            weighted = grad * gain
            gain_rows[which] = gain_rows[which] + jnp.sum(grad * raw * factor, axis=0, keepdims=True)
            grad = factor * weighted - raw * (factor * factor * factor) * per_head(raw * weighted)
            grad_proj[:, i * half : (i + 1) * half] = grad.astype(BF)
        small[2:3, 0:half] = gain_rows[0]
        small[2:3, half : 2 * half] = gain_rows[1]

        early, late = mixer_hooks(gather, scatter, 5 * half)
        mixer_back(sent, 5 * half, early, late)
        give = remote(grad_in, top, give_sem.at[2], give_sem.at[3], partner)
        give.start()
        wrap_up(scatter, 1)
        sum_end(1, result)
        give.wait_send()

    pl.when(s == 0)(first)
    pl.when(s == 1)(second)


def rope_parts():
    frequency = rope_base ** (-np.arange(HEAD // 2, dtype=np.float64) * 2.0 / HEAD)
    angles = (np.arange(MBT, dtype=np.float32)[:, None] * frequency.astype(np.float32)[None, :]).astype(np.float32)
    cosine, sine = np.cos(angles.astype(np.float64)), np.sin(angles.astype(np.float64))
    both = (np.concatenate([cosine] * 4, axis=1), np.concatenate([-sine, sine, -sine, sine], axis=1))
    parts = []
    for table in both:
        left = table.astype(np.float32)
        for _ in range(3):
            piece = left.astype(jnp.bfloat16)
            parts.append(piece)
            left = left - piece.astype(np.float32)
    return jnp.asarray(np.stack(parts).reshape(2, 3, MBT, 2 * HEAD))


def both_blocks(own, segments, gains, taps, qk_gains, shards):
    tokens, width = own.shape
    channels, padded = shards[0].shape[-1], shards[4].shape[-1] // 2
    wide = 3 * channels
    shape = jax.ShapeDtypeStruct
    rows, vmem = (tokens, width), pltpu.VMEM
    sums = [(2, 2, ROWS, padded), (2, ROWS, padded), (2, ROWS, channels), (ROWS, wide), (ROWS, 5 * channels // 3)]
    sums += [(2, width), (3, channels), (2, HEAD)]
    outs = [shape(rows, BF), shape(rows, BF)] + [shape(v, F32) for v in sums]
    n_vmem = len(outs)
    outs += [shape((4, 4, 2, ROWS, w), BF) for w in (padded, padded, padded, channels)] + [shape((2, 4, 4, ROWS, wide), BF)]
    scratch = [vmem((32, ROWS, w), BF) for w in (wide, channels, 2 * padded, padded)]
    scratch += [vmem((2, 3, ROWS, w), BF) for w in (padded, padded, padded, channels, wide)]
    scratch += [vmem((2, 4, 2, ROWS, padded), BF), vmem((2, 2, 4, ROWS, wide), BF), vmem((width, tokens), BF)]
    sizes = [width, wide, channels, width, 2 * padded, padded, width, width, width, width, width]
    scratch += [vmem((tokens, w), BF) for w in sizes]
    scratch += [
        vmem((4, 3, CHUNK, width), BF),
        vmem((CHUNK, width), F32),
        vmem((CHUNK, width), F32),
        vmem((tokens, wide), F32),
        vmem((tokens, channels), F32),
        vmem((2, tokens, padded), F32),
        vmem((5, tokens, 128), BF),
        vmem((6 * tokens // MBT, MBT, MBT), F32),
        vmem((2, tokens, 128), F32),
        vmem((4, tokens, 128), F32),
        vmem((ROWS, wide), F32),
        vmem((9, 8, width), F32),
        vmem((8, width), F32),
        vmem((8, width), F32),
        vmem((tokens, 128), F32),
        vmem((2, 128), F32),
        vmem((tokens, padded), F32),
        DMA((14,)),
        DMA((4,)),
        DMA((8, 16)),
        pltpu.SemaphoreType.REGULAR,
        DMA((4, 6)),
        DMA((4, 6)),
        DMA((8,)),
        DMA((2, 2)),
        DMA((10, 3)),
        DMA((10, 4)),
        DMA((10,)),
        pltpu.SemaphoreType.REGULAR((4,)),
        DMA((9,)),
        DMA((9,)),
    ]
    return pl.pallas_call(
        blocks_kernel,
        out_shape=outs,
        in_specs=[VM] * 8 + [ANY] * 3,
        out_specs=[VM] * n_vmem + [ANY] * 5,
        scratch_shapes=scratch,
        compiler_params=pltpu.CompilerParams(collective_id=0, has_side_effects=True, vmem_limit_bytes=60 * MIB),
        name="both_blocks",
    )(own, segments[None, :], gains, taps, qk_gains, rope_parts(), *shards)[:n_vmem]


def local(ends, segment_ids, norm_gains, conv_in, conv_kernel, qkv_weight, qk_gains, mix_out, gate_up, down):
    channels = mix_out.shape[1]
    hidden = gate_up.shape[3]
    padded = (hidden + 255) // 256 * 256
    kv, group, head = qkv_weight.shape[1], qkv_weight.shape[2] - 2, qkv_weight.shape[3]
    qkv_width = kv * (group + 2) * head
    spare = ((0, 0), (0, padded - hidden))

    gate_rows = jnp.pad(gate_up[0], ((0, 0),) + spare).reshape(2, ROWS, 2 * padded)
    shards = (
        mix_out[0].T,
        down[0].T,
        conv_in.transpose(1, 0, 2),
        qkv_weight.transpose(0, 2, 1, 3).reshape(ROWS, qkv_width),
        gate_rows,
    )
    result, grad_in, sum_pair, sum_down, sum_mix, sum_conv, sum_qkv, gains_sum, taps_sum, qk_sum = both_blocks(
        ends[0], segment_ids, norm_gains[0], conv_kernel, qk_gains, shards
    )
    qkv_grad = sum_qkv.reshape(ROWS, group + 2, kv, head)
    return (
        result[None],
        grad_in.astype(F32)[None],
        gains_sum[None],
        sum_conv.reshape(conv_in.shape),
        taps_sum,
        qkv_grad.transpose(0, 2, 1, 3),
        qk_sum,
        sum_mix.reshape(2 * ROWS, channels).T[None],
        sum_pair.reshape(2, 2 * ROWS, padded)[:, :, :hidden].transpose(1, 0, 2)[None],
        sum_down.reshape(2 * ROWS, padded)[:, :hidden].T[None],
    )


def solution(mesh):
    dims = (
        P(SEC, DP, None),
        P(DP),
        P(SEC, None, None),
        P((SEC, DP), None, TEN),
        P(None, TEN),
        P((SEC, DP), TEN, None, None),
        P(),
        P(SEC, TEN, DP),
        P(SEC, DP, None, TEN),
        P(SEC, TEN, DP),
    )
    results = (dims[0], dims[0], dims[2], dims[3], dims[4], dims[5], dims[6], dims[7], dims[8], dims[9])
    return jax.shard_map(local, mesh=mesh, in_specs=dims, out_specs=results, check_vma=False)
```

```python
import functools

import jax
import jax.numpy as jnp
import numpy as np
from jax import lax
from jax.experimental import pallas as pl
from jax.experimental.pallas import tpu as pltpu
from jax.sharding import PartitionSpec as P

SEC, DP, TEN = "section", "dp", "tensor"
MESH = pl.DeviceIdType.MESH
F32, BF = jnp.float32, jnp.bfloat16
ANY = pl.BlockSpec(memory_space=pl.ANY)
VM = pl.BlockSpec(memory_space=pltpu.VMEM)
DMA = pltpu.SemaphoreType.DMA
MIB = 1 << 20

MBT = 128
ROWS = 48
CHUNK = 64
HEAD = 64
epsilon = 1e-05
rope_base = 1000000.0
neg_large = -1e30

HOME = (2, 2, 3, 1, 0)


def place():
    d = lax.axis_index(DP)
    return lax.axis_index(SEC), d // 4, d % 4, lax.axis_index(TEN)


def near(axis, y, x, step):
    return (y, (x + step) % 4) if axis == 0 else ((y + step) % 4, x)


def remote(src, dst, send_sem, recv_sem, device):
    return pltpu.make_async_remote_copy(
        src_ref=src, dst_ref=dst, send_sem=send_sem, recv_sem=recv_sem, device_id=device, device_id_type=MESH
    )


def arrived(ref, sem):
    pltpu.make_async_copy(ref, ref, sem).wait()


def cut(columns):
    return (columns // 128 + 1) // 2 * 128


def root(values):
    return lax.rsqrt(jnp.mean(values * values, axis=-1, keepdims=True) + epsilon)


def dot(a, b):
    return jnp.dot(a, b, preferred_element_type=F32)


def dot_bt(a, b):
    return lax.dot_general(a, b, (((1,), (1,)), ((), ())), preferred_element_type=F32)


def dot_at(a, b):
    return lax.dot_general(a, b, (((0,), (0,)), ((), ())), preferred_element_type=F32)


def norm_back(values, gain, grad):
    factor = root(values)
    weighted = grad * gain
    grad_in = factor * weighted - values * (factor * factor * factor) * jnp.mean(values * weighted, axis=-1, keepdims=True)
    return grad_in, jnp.sum(grad * values * factor, axis=0, keepdims=True)


def lanes(i, size=128, start=0):
    return pl.ds(pl.multiple_of(start + i * size, 128), size)


def times(count, body):
    def step(i, carry):
        body(i)
        return carry

    lax.fori_loop(0, count, step, 0)


def matrix(ref, columns):
    value = ref[:, :, columns]
    return value.reshape(value.shape[0] * value.shape[1], value.shape[2])


def add_rows(dst, pieces):
    rows = dst.shape[-2]
    three = len(dst.shape) == 3
    kind = BF if len(pieces) == 2 else F32

    def body(i):
        at = pl.ds(pl.multiple_of(i % (rows // 16) * 16, 16), 16)
        k = i // (rows // 16)
        get = (lambda r: r[k, at, :]) if three else (lambda r: r[at, :])
        total = get(pieces[0]).astype(kind)
        for p in pieces[1:]:
            total = total + get(p).astype(kind)
        if three:
            dst[k, at, :] = total.astype(dst.dtype)
        else:
            dst[at, :] = total.astype(dst.dtype)

    times((dst.shape[0] if three else 1) * (rows // 16), body)


class Gather:
    def __init__(self, weights, widths, shards, send_sem, recv_sem):
        self.weights, self.widths, self.shards = weights, widths, shards
        self.send_sem, self.recv_sem = send_sem, recv_sem
        self.s, self.y, self.x, self.z = place()

    def narrow(self, a, ref):
        return ref if self.widths[a] == ref.shape[-1] else ref.at[..., 0 : self.widths[a]]

    def block(self, a, h, yx):
        b = yx[0] * 4 + yx[1]
        return self.narrow(a, self.weights[a].at[h * 16 + b if a == 0 else b * 2 + h])

    def send(self, a, h, yx, lo, hi, to, src=None):
        ref = self.block(a, h, yx)
        if (lo, hi) != (0, self.widths[a]):
            ref = ref.at[:, lo:hi]
        recv = self.recv_sem.at[a * 2 + h, yx[0] * 4 + yx[1]]
        remote(ref if src is None else src, ref, self.send_sem.at[a], recv, (self.s, to[0] * 4 + to[1], self.z)).start()

    def wait(self, a, h, yx):
        arrived(self.block(a, h, yx), self.recv_sem.at[a * 2 + h, yx[0] * 4 + yx[1]])

    def near(self, axis, step):
        return near(axis, self.y, self.x, step)

    def start(self, arrays):
        for axis_of in (lambda h: h, lambda h: 1 - h):
            for a in arrays:
                for h in (0, 1):
                    src = None if self.shards[a] is None else self.shards[a].at[h]
                    for step in (1, -1):
                        self.send(a, h, (self.y, self.x), 0, self.widths[a], self.near(axis_of(h), step), src)

    def spread(self, arrays):
        for a in arrays:
            w = self.widths[a]
            c = cut(w)
            for h in (0, 1):
                for step, lo, hi in ((1, 0, c), (-1, c, w)):
                    src = self.near(h, -step)
                    self.wait(a, h, src)
                    self.send(a, h, src, lo, hi, self.near(h, step))
                    for on in (1, -1):
                        self.send(a, h, src, 0, w, self.near(1 - h, on))
        for a in arrays:
            for h in (0, 1):
                far = self.near(h, 2)
                self.wait(a, h, far)
                for on in (1, -1):
                    self.send(a, h, far, 0, self.widths[a], self.near(1 - h, on))

    def relay(self, a):
        w = self.widths[a]
        c = cut(w)
        for h in (0, 1):

            def body(j, h=h):
                line = self.near(h, j)
                for step, lo, hi in ((1, 0, c), (-1, c, w)):
                    src = near(1 - h, line[0], line[1], -step)
                    self.wait(a, h, src)
                    self.send(a, h, src, lo, hi, self.near(1 - h, step))

            times(4, body)

    def last(self, a):
        for h in (0, 1):

            def body(j, h=h):
                line = self.near(h, j)
                self.wait(a, h, near(1 - h, line[0], line[1], 2))

            times(4, body)

    def sent(self, a):
        arrived(self.narrow(a, self.weights[a].at[0:30]), self.send_sem.at[a])


class Scatter:
    def __init__(self, grads, weights, widths, extras, load_sem, recv_sem, send_sem, free):
        self.grads, self.weights, self.widths, self.extras = grads, weights, widths, extras
        self.load_sem, self.recv_sem, self.send_sem, self.free = load_sem, recv_sem, send_sem, free
        self.s, self.y, self.x, self.z = place()
        self.claimed = set()
        self.loads = {}

    def device(self, yx):
        return (self.s, yx[0] * 4 + yx[1], self.z)

    def near(self, axis, step):
        return near(axis, self.y, self.x, step)

    def release(self, home):
        for axis in (0, 1):
            for step in (1, -1):
                to = self.device(self.near(axis, step))
                pl.semaphore_signal(self.free.at[home], inc=1, device_id=to, device_id_type=MESH)

    def line(self, a, h, yx):
        if a == 4:
            ref = self.grads[a].at[h, yx[0]] if h == 0 else self.grads[a].at[h, :, yx[1]]
            return ref if self.widths[a] == ref.shape[-1] else ref.at[:, :, 0 : self.widths[a]]
        return self.grads[a].at[yx[0], :, h] if h == 0 else self.grads[a].at[:, yx[1], h]

    def room(self, a, h, lo, hi):
        ref = self.weights[HOME[a]].at[16 * h + lo : 16 * h + hi]
        start = self.widths[a] if a == 1 else 0
        if self.widths[a] != ref.shape[-1]:
            ref = ref.at[:, :, start : start + self.widths[a]]
        return ref

    def extra(self, a, h):
        ref = self.extras[a].at[h]
        return ref if self.widths[a] == ref.shape[-1] else ref.at[:, :, 0 : self.widths[a]]

    def move(self, a, h, i, src, dst, to):
        remote(src, dst, self.send_sem.at[a * 2 + h], self.recv_sem.at[a * 2 + h, i], self.device(to)).start()

    def load(self, a, h, i, src, dst):
        copy = pltpu.make_async_copy(src, dst, self.load_sem.at[a * 2 + h, i])
        copy.start()
        self.loads[a, h, i] = copy

    def begin(self, a, h):
        if HOME[a] not in self.claimed:
            pl.semaphore_wait(self.free.at[HOME[a]], 4)
            self.claimed.add(HOME[a])
        up, dn, far = (self.near(1 - h, step) for step in (1, -1, 2))
        self.move(a, h, 0, self.line(a, h, far).at[0:2], self.room(a, h, 0, 2), up)
        self.move(a, h, 0, self.line(a, h, far).at[2:4], self.room(a, h, 2, 4), dn)
        self.load(a, h, 0, self.line(a, h, up).at[0:2], self.room(a, h, 12, 14))
        self.load(a, h, 1, self.line(a, h, dn).at[2:4], self.room(a, h, 14, 16))

    def begin_near(self, a, h):
        up, dn = (self.near(1 - h, step) for step in (1, -1))
        self.move(a, h, 1, self.line(a, h, up).at[2:4], self.room(a, h, 6, 8), up)
        self.move(a, h, 1, self.line(a, h, dn).at[0:2], self.room(a, h, 8, 10), dn)

    def pass_on(self, a, h):
        up, dn = (self.near(1 - h, step) for step in (1, -1))
        self.loads[a, h, 0].wait()
        self.loads[a, h, 1].wait()
        arrived(self.room(a, h, 0, 4), self.recv_sem.at[a * 2 + h, 0])
        mine = self.room(a, h, 12, 16)
        add_rows(mine, [mine, self.room(a, h, 0, 4)])
        self.move(a, h, 1, self.room(a, h, 12, 14), self.room(a, h, 4, 6), up)
        self.move(a, h, 1, self.room(a, h, 14, 16), self.room(a, h, 10, 12), dn)
        self.load(a, h, 2, self.line(a, h, (self.y, self.x)), self.room(a, h, 0, 4))

    def own(self, h):
        return self.x if h == 0 else self.y

    def turn(self, a, h):
        w = self.widths[a]
        c = cut(w)
        self.loads[a, h, 2].wait()
        arrived(self.room(a, h, 4, 12), self.recv_sem.at[a * 2 + h, 1])
        total, extra = self.room(a, h, 0, 4), self.extra(a, h)
        add_rows(total, [total, self.room(a, h, 4, 8), self.room(a, h, 8, 12)])
        up, dn = (self.near(h, step) for step in (1, -1))
        far, i_up, i_dn = ((self.own(h) + step) % 4 for step in (2, 1, -1))
        self.move(a, h, 2, total.at[far, :, 0:c], extra.at[0, :, 0:c], up)
        self.move(a, h, 2, total.at[far, :, c:w], extra.at[0, :, c:w], dn)
        self.move(a, h, 3, total.at[i_up, :, c:w], extra.at[1, :, c:w], up)
        self.move(a, h, 3, total.at[i_dn, :, 0:c], extra.at[2, :, 0:c], dn)

    def pass_back(self, a, h):
        w = self.widths[a]
        c = cut(w)
        total, extra = self.room(a, h, 0, 4), self.extra(a, h)
        up, dn = (self.near(h, step) for step in (1, -1))
        i_up, i_dn = ((self.own(h) + step) % 4 for step in (1, -1))
        arrived(extra.at[0], self.recv_sem.at[a * 2 + h, 2])
        lo, hi = extra.at[0, :, 0:c], extra.at[0, :, c:w]
        add_rows(lo, [lo, total.at[i_up, :, 0:c]])
        self.move(a, h, 3, lo, extra.at[1, :, 0:c], up)
        add_rows(hi, [hi, total.at[i_dn, :, c:w]])
        self.move(a, h, 3, hi, extra.at[2, :, c:w], dn)

    def finish(self, a, h, out):
        total, extra = self.room(a, h, 0, 4), self.extra(a, h)
        arrived(extra.at[1:3], self.recv_sem.at[a * 2 + h, 3])
        add_rows(out, [total.at[self.own(h)], extra.at[1], extra.at[2]])

    def sent(self, a, h):
        arrived(self.room(a, h, 0, 15), self.send_sem.at[a * 2 + h])


def blocks_kernel(
    own,
    seg_row,
    gains,
    taps,
    qk_pair,
    tables,
    shard_mix,
    shard_down,
    shard_conv,
    shard_qkv,
    shard_gate,
    result,
    grad_in,
    sum_pair,
    sum_down,
    sum_mix,
    sum_conv,
    sum_qkv,
    gains_out,
    taps_out,
    qk_out,
    grad_gate,
    grad_up,
    grad_down,
    grad_mix,
    grad_mixer,
    w_mixer,
    w_mix,
    w_gate,
    w_down,
    x_gate,
    x_up,
    x_down,
    x_mix,
    x_mixer,
    stage,
    stage_mixer,
    turned,
    normed,
    grad_proj,
    mixer,
    ffn_in,
    grad_pair,
    hidden,
    top,
    grad_mid,
    sent,
    part,
    late_part,
    inbox,
    middle,
    grad_chunk,
    proj,
    mixed,
    gate_up,
    heads,
    soft,
    turns,
    grad_heads,
    mixer_give,
    small_in,
    small,
    small_other,
    seg_wide,
    qk_gains,
    early_grad,
    copy_sem,
    gather_send,
    gather_recv,
    go,
    send_sem,
    recv_sem,
    give_sem,
    stage_sem,
    load_sem,
    sum_recv,
    sum_send,
    free,
    small_send,
    small_recv,
):
    s, y, x, z = place()
    d = y * 4 + x
    mates = [(s, d, (z + j) % 4) for j in (1, 2, 3)]
    partner = (1 - s, d, z)
    plane = [[(s, v[0] * 4 + v[1], z) for v in (near(k, y, x, j) for j in (1, 2, 3))] for k in (0, 1)]
    tokens, width = own.shape
    channels = mixer.shape[1]
    padded = hidden.shape[1]
    blocks = tokens // MBT
    weights = (w_mixer, w_mix, w_gate, w_down)
    grads = (grad_gate, grad_up, grad_down, grad_mix, grad_mixer)
    extras = (x_gate, x_up, x_down, x_mix, x_mixer)
    shards = (None, None, shard_gate, None)

    def movers(wide):
        gather = Gather(weights, (wide, channels, 2 * padded, padded), shards, gather_send, gather_recv)
        widths = (padded, padded, padded, channels, wide)
        return gather, Scatter(grads, weights, widths, extras, load_sem, sum_recv, sum_send, free)

    barrier = pltpu.get_barrier_semaphore()
    greeted = [partner] + mates + plane[0] + plane[1]
    for device in greeted:
        pl.semaphore_signal(barrier, inc=1, device_id=device, device_id_type=MESH)
    pl.semaphore_wait(barrier, len(greeted))

    def rows(k):
        return pl.ds(pl.multiple_of(k % 4 * CHUNK, CHUNK), CHUNK)

    mine = rows(z)


    index = d * 2
    third = taps.shape[1]
    conv_parts = [slice(k * third, (k + 1) * third) for k in range(3)]
    qkv_part = slice(0, shard_qkv.shape[1])
    swapped = [remote(shard_qkv, w_mixer.at[d, :, qkv_part], copy_sem.at[0], copy_sem.at[1], partner)]
    for k in range(3):
        to = w_mixer.at[16 + d, :, conv_parts[k]]
        swapped.append(remote(shard_conv.at[k], to, copy_sem.at[8 + k], copy_sem.at[11 + k], partner))
    kept = [pltpu.make_async_copy(shard_qkv, w_mixer.at[16 + d, :, qkv_part], copy_sem.at[2])]
    for k in range(3):
        kept.append(pltpu.make_async_copy(shard_conv.at[k], w_mixer.at[d, :, conv_parts[k]], copy_sem.at[2 if k == 0 else 5 + k]))

    def swap_start(section):
        for copy in swapped[:1] if section == 0 else swapped[1:]:
            copy.start()
        for copy in kept[1:] if section == 0 else kept[:1]:
            copy.start()

    def swap_end(section):
        for copy in kept[1:] if section == 0 else kept[:1]:
            copy.wait()
        for copy in swapped[:1] if section == 0 else swapped[1:]:
            copy.wait_send()
        for copy in swapped[1:] if section == 0 else swapped[:1]:
            copy.wait_recv()

    fills = [pltpu.make_async_copy(shard_gate, w_gate.at[pl.ds(index, 2)], copy_sem.at[4])]
    for copy in fills:
        copy.start()

    def regroup(values, outer, inner):
        parts = [values[:, (o * inner + i) * HEAD : (o * inner + i + 1) * HEAD] for i in range(inner) for o in range(outer)]
        return jnp.concatenate(parts, axis=1)

    def place_shards(section):
        values = shard_mix[...].astype(F32)
        values = regroup(values, 2, 3) if section == 1 else values
        w_mix[pl.ds(index, 2)] = values.astype(BF).reshape(2, ROWS, channels)
        inner = shard_down.shape[1]
        w_down[pl.ds(index, 2), :, inner - inner % 128 :] = jnp.zeros((2, ROWS, padded - inner + inner % 128), BF)
        w_down[pl.ds(index, 2), :, 0:inner] = shard_down[...].reshape(2, ROWS, inner)

    small[...] = jnp.zeros_like(small)
    seg_wide[...] = jnp.broadcast_to(seg_row[...].astype(F32), (MBT, tokens)).T

    def gather_most(gather, section):
        place_shards(section)
        gather.start((1,))
        swap_end(section)
        gather.start((0,))
        gather.start((2, 3))
        for copy in fills:
            copy.wait()
        for arrays in ((0, 1), (2, 3)):
            gather.spread(arrays)
        for a in (0, 1):
            gather.relay(a)


    def spread(phase, a, weight, depth, to, send=True):
        for k in range(2):
            value = weight[k * 16 : k * 16 + 16, :, 0:depth].reshape(16 * ROWS, depth)
            columns = slice(k * 16 * ROWS, (k + 1) * 16 * ROWS)
            to[:, columns] = dot_bt(a[:, 0:depth], value).astype(BF)
            if send:
                sum_start(phase, to, columns)

    def sum_start(phase, src, columns=slice(None)):
        for j in (2, 1, 3):
            sems = (send_sem.at[phase, j - 1], recv_sem.at[phase, j - 1])
            remote(src.at[rows(z + j), columns], inbox.at[phase, j - 1, :, columns], *sems, mates[j - 1]).start()

    def sum_middle(phase, src, full, work):
        total = src[mine, :].astype(F32)
        for j in range(3):
            arrived(inbox.at[phase, j], recv_sem.at[phase, j])
            total = total + inbox[phase, j].astype(F32)
        full[mine, :] = work(total).astype(BF)
        for j in (2, 1, 3):
            sems = (send_sem.at[phase, 2 + j], recv_sem.at[phase, 2 + j])
            remote(full.at[mine], full.at[mine], *sems, mates[j - 1]).start()

    def sum_end(phase, full):
        for j in (1, 2, 3):
            arrived(full.at[rows(z - j)], recv_sem.at[phase, 2 + j])
        for i in range(6):
            arrived(full.at[mine], send_sem.at[phase, i])

    def nothing():
        pass

    def sum_over_mates(phase, full, work, first_wait=nothing, second_wait=nothing):
        first_wait()
        sum_middle(phase, part, full, work)
        second_wait()
        sum_end(phase, full)


    def norm_rows(src):
        def body(i):
            values = src[rows(i), :].astype(F32)
            normed[rows(i), :] = (values * root(values) * gains[0:1, :]).astype(BF)

        times(tokens // CHUNK, body)

    def project(count):
        for start in range(0, count * 128, 256):
            at = slice(start, min(start + 256, count * 128))
            proj[:, at] = dot(normed[...], matrix(w_mixer, at))

    def after_mixer(src, first_wait, second_wait):
        def work(total):
            value = src[mine, :].astype(F32) + total
            middle[...] = value
            return value * root(value) * gains[1:2, :]

        spread(0, mixer, w_mix, channels, part)
        sum_over_mates(0, ffn_in, work, first_wait, second_wait)

    def ffn_forward(gather):
        gather.last(2)
        for j in range(padded // 256):
            at = slice(j * 256, (j + 1) * 256)
            gate = dot(ffn_in[...], matrix(w_gate, at))
            up = dot(ffn_in[...], matrix(w_gate, slice(padded + j * 256, padded + (j + 1) * 256)))
            gate_up[0, :, at] = gate
            gate_up[1, :, at] = up
            hidden[:, at] = (gate * jax.nn.sigmoid(gate) * up).astype(BF)
        gather.last(3)

    def add_middle(total):
        return middle[...] + total

    staged = {}

    def drain(which, slot):
        if (which, slot) in staged:
            arrived(staged.pop((which, slot)), stage_sem.at[which, slot])

    def drain_all():
        for key in list(staged):
            drain(*key)

    def weight_grad(a, left, right, start=0):
        size = right.shape[-1] // 2 if a < 2 else right.shape[-1]
        tile = 896 if size % 896 == 0 else size // 3 if size % 384 == 0 and size > 384 else size
        buffer = stage_mixer if a == 4 else stage
        which = 1 if a == 4 else 0
        if left is not None:
            turned[...] = left[...].T
        whole = size == buffer.shape[-1]
        for t in range(4):
            slot = t % 2
            room = buffer.at[slot] if whole else buffer.at[slot, :, :, :, 0:size]
            drain(which, slot)
            for k in range(2):
                at = t * 384 + k * 192
                for j in range(size // tile):
                    columns = slice(start + j * tile, start + (j + 1) * tile)
                    value = dot(turned[at : at + 192, :], right[:, columns]).astype(BF)
                    for i in range(4):
                        b = k * 4 + i
                        b = (b // 4, b % 4) if a == 4 else (b // 2, b % 2)
                        buffer[slot, b[0], b[1], :, j * tile : (j + 1) * tile] = value[i * ROWS : (i + 1) * ROWS, :]
            to = grads[a].at[t // 2, t % 2 * 2 : t % 2 * 2 + 2] if a == 4 else grads[a].at[t]
            to = to if whole or a < 4 else to.at[:, :, :, 0:size]
            pltpu.make_async_copy(room, to, stage_sem.at[which, slot]).start()
            staged[which, slot] = room

    def release(gather, scatter, a):
        gather.sent(a)
        scatter.release(a)

    def ffn_late(scatter):
        drain_all()
        both(scatter.begin, 2)
        both(scatter.begin_near, 2)
        weight_grad(0, ffn_in, grad_pair)
        drain_all()
        both(scatter.begin, 0)
        both(scatter.begin_near, 0)
        weight_grad(1, None, grad_pair, padded)
        drain_all()
        both(scatter.begin, 1)
        both(scatter.begin_near, 1)
        both(scatter.pass_on, 2)

    def mixer_hooks(gather, scatter, depth):
        def early():
            release(gather, scatter, 1)
            release(gather, scatter, 0)
            weight_grad(4, normed, grad_proj.at[:, 0:depth])
            both(scatter.pass_on, 0)
            drain_all()
            both(scatter.begin, 4)
            both(scatter.begin_near, 4)

        def late():
            weight_grad(3, grad_mid, mixer)
            both(scatter.pass_on, 1)
            drain_all()
            both(scatter.begin, 3)
            both(scatter.begin_near, 3)
            both(scatter.pass_on, 4)

        return early, late

    def ffn_grads():
        for j in range(padded // 256):
            at = slice(j * 256, (j + 1) * 256)
            grad = dot(top[...], matrix(w_down, at))
            gate, up = gate_up[0, :, at], gate_up[1, :, at]
            sig = jax.nn.sigmoid(gate)
            grad_pair[:, at] = (grad * up * sig * (1.0 + gate * (1.0 - sig))).astype(BF)
            grad_pair[:, padded + j * 256 : padded + (j + 1) * 256] = (grad * gate * sig).astype(BF)

    def ffn_early_grad(gather):
        gather.last(3)
        for j in range(padded // 256):
            at = slice(j * 256, (j + 1) * 256)
            early_grad[:, at] = dot(top[...], matrix(w_down, at))

    def ffn_both_ways(gather):
        gather.last(2)
        for j in range(padded // 256):
            at = slice(j * 256, (j + 1) * 256)
            gate = dot(ffn_in[...], matrix(w_gate, at))
            up = dot(ffn_in[...], matrix(w_gate, slice(padded + j * 256, padded + (j + 1) * 256)))
            grad = early_grad[:, at]
            sig = jax.nn.sigmoid(gate)
            act = gate * sig
            hidden[:, at] = (act * up).astype(BF)
            grad_pair[:, at] = (grad * up * sig * (1.0 + gate * (1.0 - sig))).astype(BF)
            grad_pair[:, padded + j * 256 : padded + (j + 1) * 256] = (grad * act).astype(BF)

    def ffn_backward(early, late):
        def work(total):
            grad, small[1:2, :] = norm_back(middle[...], gains[1:2, :], total)
            grad = top[mine, :].astype(F32) + grad
            grad_chunk[...] = grad
            return grad

        spread(2, grad_pair, w_gate, 2 * padded, part)

        sum_over_mates(2, grad_mid, work, early, late)

    def mixer_back(src, depth, early, late):
        def work(total):
            grad, small[0:1, :] = norm_back(src[mine, :].astype(F32), gains[0:1, :], total)
            return grad_chunk[...] + grad

        spread(3, grad_proj, w_mixer, depth, part)

        sum_over_mates(3, grad_in, work, early, late)

    def small_start(k):
        group = plane[k] if k < 2 else mates
        for j in range(3):
            i = k * 3 + j
            remote(small, small_in.at[i], small_send.at[i], small_recv.at[i], group[j]).start()

    def small_add(k):
        for j in range(3):
            arrived(small, small_send.at[k * 3 + j])
            arrived(small, small_recv.at[k * 3 + j])
        summed = small[...] + small_in[k * 3] + small_in[k * 3 + 1] + small_in[k * 3 + 2]
        if k == 2:
            row = lax.broadcasted_iota(jnp.int32, summed.shape, 0)
            summed = jnp.where(row == 3, small[...], summed)
        small[...] = summed

    def both(step, a):
        for h in (0, 1):
            step(a, h)

    widths = (3 * channels, 5 * channels // 3)

    def wrap_up(scatter, section):
        def finish(a):
            for h in (0, 1):
                if a == 4:
                    own_sum = (sum_conv, sum_qkv)[section]
                    scatter.finish(a, h, own_sum if h == section else mixer_give.at[:, 0 : widths[section]])
                else:
                    scatter.finish(a, h, sum_pair.at[a, h] if a < 2 else (sum_down, sum_mix)[a - 2].at[h])

        small_start(0)
        both(scatter.turn, 2)
        both(scatter.pass_on, 3)
        both(scatter.turn, 0)
        small_add(0)
        small_start(1)
        both(scatter.turn, 4)
        both(scatter.pass_back, 2)
        both(scatter.turn, 1)
        both(scatter.pass_back, 0)
        small_add(1)
        small_start(2)
        both(scatter.turn, 3)
        both(scatter.pass_back, 4)
        both(scatter.pass_back, 1)
        finish(2)
        both(scatter.pass_back, 3)
        finish(0)
        small_add(2)
        give_small = remote(small, small_other, give_sem.at[4], give_sem.at[5], partner)
        give_small.start()
        finish(4)
        at = slice(0, widths[section])
        give_mixer = remote(mixer_give.at[:, at], (sum_conv, sum_qkv)[section], give_sem.at[6], give_sem.at[7], partner)
        give_mixer.start()
        finish(1)
        finish(3)
        for a in range(5):
            both(scatter.sent, a)
        give_small.wait()
        give_mixer.wait_send()
        arrived((sum_qkv, sum_conv)[section], give_sem.at[7])
        of_conv, of_qk = (small, small_other) if section == 0 else (small_other, small)
        if section == 1:
            for h in (0, 1):
                sum_mix[h] = regroup(sum_mix[h], 3, 2)
        gains_out[...] = small[0:2, :]
        for k in range(3):
            taps_out[k : k + 1, :] = of_conv[3:4, conv_parts[k]]
        for k in (0, 1):
            both_heads = of_qk[2:3, k * 128 : (k + 1) * 128]
            qk_out[k : k + 1, :] = (both_heads + pltpu.roll(both_heads, HEAD, 1))[:, 0:HEAD]


    def same(lag):
        seg = seg_wide[...]
        row = lax.broadcasted_iota(jnp.int32, (tokens, 128), 0)
        return jnp.where((seg == pltpu.roll(seg, lag, 0)) & (row % MBT >= lag), 1.0, 0.0)

    def pieces(j):
        at = [slice(i * channels + j * 128, i * channels + (j + 1) * 128) for i in range(3)]
        return [proj[:, a] for a in at], at

    def first():
        gather, scatter = movers(3 * channels)
        swap_start(0)
        gather_most(gather, 0)
        pl.semaphore_signal(go, inc=1, device_id=partner, device_id_type=MESH)
        norm_rows(own)
        gather.last(0)
        project(3 * channels // 128)
        for j in range(channels // 128):
            (b, c, e), _ = pieces(j)
            at = slice(j * 128, (j + 1) * 128)
            product = b * e
            total = taps[0:1, at] * product
            for lag in (1, 2):
                total = total + taps[lag : lag + 1, at] * (pltpu.roll(product, lag, 0) * same(lag))
            mixed[:, at] = total
            mixer[:, at] = (c * total).astype(BF)
        gather.last(1)

        after_mixer(own, lambda: gather.relay(2), lambda: gather.relay(3))
        ffn_forward(gather)
        spread(1, hidden, w_down, padded, part)
        sum_over_mates(1, result, add_middle)
        give = remote(result, sent, give_sem.at[0], give_sem.at[1], partner)
        give.start()
        give.wait_send()
        arrived(top, give_sem.at[3])

        def ffn_early():
            release(gather, scatter, 2)
            release(gather, scatter, 3)
            weight_grad(2, top, hidden)

        ffn_grads()
        ffn_backward(ffn_early, lambda: ffn_late(scatter))
        for j in range(channels // 128):
            (b, c, e), at = pieces(j)
            lane = slice(j * 128, (j + 1) * 128)
            grad_y = dot(grad_mid[...], matrix(w_mix, lane))
            product = b * e
            grad_mixed = grad_y * c
            grad_product = taps[0:1, lane] * grad_mixed
            sums = [jnp.sum(grad_mixed * product, axis=0, keepdims=True)]
            for lag in (1, 2):
                masked = grad_mixed * same(lag)
                sums.append(jnp.sum(masked * pltpu.roll(product, lag, 0), axis=0, keepdims=True))
                grad_product = grad_product + taps[lag : lag + 1, lane] * pltpu.roll(masked, tokens - lag, 0)
            for k in range(3):
                small[3:4, at[k]] = sums[k]
            grad_proj[:, at[0]] = (grad_product * e).astype(BF)
            grad_proj[:, at[1]] = (grad_y * mixed[:, lane]).astype(BF)
            grad_proj[:, at[2]] = (grad_product * b).astype(BF)

        early, late = mixer_hooks(gather, scatter, 3 * channels)
        mixer_back(own, 3 * channels, early, late)
        wrap_up(scatter, 0)


    half = channels // 3
    lane_of = lax.broadcasted_iota(jnp.int32, (1, half), 1)
    keep = [jnp.where(lane_of // HEAD == k, 1.0, 0.0) for k in (0, 1)]

    def per_head(values):
        first_sum = jnp.sum(values * keep[0], axis=-1, keepdims=True)
        second_sum = jnp.sum(values * keep[1], axis=-1, keepdims=True)
        return (first_sum * keep[0] + second_sum * keep[1]) * (1.0 / HEAD)

    def across(values):
        low = lane_of % HEAD < HEAD // 2
        return jnp.where(low, pltpu.roll(values, half - HEAD // 2, 1), pltpu.roll(values, HEAD // 2, 1))

    def allowed(block):
        at = slice(block * MBT, (block + 1) * MBT)
        t = lax.broadcasted_iota(jnp.int32, (MBT, MBT), 0)
        u = lax.broadcasted_iota(jnp.int32, (MBT, MBT), 1)
        return jnp.where((seg_wide[at, :] == seg_row[:, at].astype(F32)) & (u <= t), 1.0, 0.0)

    def turn_tables():
        for block in range(blocks):
            at = slice(block * MBT, (block + 1) * MBT)
            offset = jnp.sum(allowed(block), axis=1, keepdims=True) - 1.0
            column = lax.broadcasted_iota(jnp.int32, (MBT, MBT), 1).astype(F32)
            pick = jnp.where(column == offset, 1.0, 0.0).astype(BF)
            for k in (0, 1):
                turns[k, at, :] = dot(pick, tables[k, 0]) + dot(pick, tables[k, 1]) + dot(pick, tables[k, 2])

    inv_sqrt = HEAD ** (-0.5)

    def masked(i, block, k):
        at = slice(block * MBT, (block + 1) * MBT)
        return heads[i, at, :] * keep[k].astype(BF)

    def second():
        gather, scatter = movers(5 * half)
        swap_start(1)
        qk_gains[...] = jnp.concatenate([qk_pair[...], qk_pair[...]], axis=1)
        turn_tables()
        top[...] = own[...]
        grad_proj[:, 5 * half :] = jnp.zeros((tokens, grad_proj.shape[1] - 5 * half), BF)
        pl.semaphore_wait(go, 1)
        gather_most(gather, 1)
        gather.relay(2)
        arrived(sent, give_sem.at[1])
        norm_rows(sent)
        gather.last(0)
        project(5)
        for i in range(4):
            raw = proj[:, i * half : (i + 1) * half]
            gain = qk_gains[min(i // 3, 1) : min(i // 3, 1) + 1, :]
            value = raw * lax.rsqrt(per_head(raw * raw) + epsilon) * gain
            heads[i] = (value * turns[0] + across(value) * turns[1]).astype(BF)
        heads[4] = proj[:, 4 * half : 5 * half].astype(BF)
        for block in range(blocks):
            at = slice(block * MBT, (block + 1) * MBT)
            ok = allowed(block)
            for g in range(3):
                attended = jnp.zeros((MBT, half), F32)
                for k in (0, 1):
                    score = dot_bt(heads[g, at, :], masked(3, block, k)) * inv_sqrt
                    score = jnp.where(ok > 0.0, score, neg_large)
                    power = jnp.exp(score - jnp.max(score, axis=-1, keepdims=True))
                    weight = power / jnp.sum(power, axis=-1, keepdims=True)
                    soft[(block * 3 + g) * 2 + k] = weight
                    attended = attended + dot(weight.astype(BF), masked(4, block, k))
                mixer[at, g * half : (g + 1) * half] = attended.astype(BF)
        gather.last(1)
        after_mixer(sent, lambda: gather.relay(3), lambda: ffn_early_grad(gather))
        ffn_both_ways(gather)

        def ffn_early():
            release(gather, scatter, 2)
            spread(1, hidden, w_down, padded, late_part, False)
            release(gather, scatter, 3)
            weight_grad(2, top, hidden)

        def late():
            sum_start(1, late_part)
            ffn_late(scatter)

        ffn_backward(ffn_early, late)
        for block in range(blocks):
            at = slice(block * MBT, (block + 1) * MBT)
            grad_key = jnp.zeros((MBT, half), F32)
            grad_value = jnp.zeros((MBT, half), F32)
            for g in range(3):
                grad_att = dot(grad_mid[at, :], matrix(w_mix, slice(g * half, (g + 1) * half))).astype(BF)
                grad_query = jnp.zeros((MBT, half), F32)
                for k in (0, 1):
                    weight = soft[(block * 3 + g) * 2 + k]
                    grad_soft = dot_bt(grad_att, masked(4, block, k))
                    delta = jnp.sum(weight * grad_soft, axis=-1, keepdims=True)
                    grad_score = (weight * (grad_soft - delta)).astype(BF)
                    grad_query = grad_query + dot(grad_score, masked(3, block, k))
                    grad_key = grad_key + dot_at(grad_score, masked(g, block, k))
                    grad_value = grad_value + dot_at(weight.astype(BF), grad_att * keep[k].astype(BF))
                grad_heads[g, at, :] = grad_query * inv_sqrt
            grad_heads[3, at, :] = grad_key * inv_sqrt
            grad_proj[at, 4 * half : 5 * half] = grad_value.astype(BF)
            if block == 0:
                sum_middle(1, late_part, result, add_middle)
        gain_rows = [jnp.zeros((1, half), F32)] * 2
        for i in range(4):
            raw = proj[:, i * half : (i + 1) * half]
            which = min(i // 3, 1)
            gain = qk_gains[which : which + 1, :]
            grad = grad_heads[i]
            grad = grad * turns[0] - across(grad) * turns[1]
            factor = lax.rsqrt(per_head(raw * raw) + epsilon)
            weighted = grad * gain
            gain_rows[which] = gain_rows[which] + jnp.sum(grad * raw * factor, axis=0, keepdims=True)
            grad = factor * weighted - raw * (factor * factor * factor) * per_head(raw * weighted)
            grad_proj[:, i * half : (i + 1) * half] = grad.astype(BF)
        small[2:3, 0:half] = gain_rows[0]
        small[2:3, half : 2 * half] = gain_rows[1]

        early, late = mixer_hooks(gather, scatter, 5 * half)
        mixer_back(sent, 5 * half, early, late)
        give = remote(grad_in, top, give_sem.at[2], give_sem.at[3], partner)
        give.start()
        wrap_up(scatter, 1)
        sum_end(1, result)
        give.wait_send()

    pl.when(s == 0)(first)
    pl.when(s == 1)(second)


def rope_parts():
    frequency = rope_base ** (-np.arange(HEAD // 2, dtype=np.float64) * 2.0 / HEAD)
    angles = (np.arange(MBT, dtype=np.float32)[:, None] * frequency.astype(np.float32)[None, :]).astype(np.float32)
    cosine, sine = np.cos(angles.astype(np.float64)), np.sin(angles.astype(np.float64))
    both = (np.concatenate([cosine] * 4, axis=1), np.concatenate([-sine, sine, -sine, sine], axis=1))
    parts = []
    for table in both:
        left = table.astype(np.float32)
        for _ in range(3):
            piece = left.astype(jnp.bfloat16)
            parts.append(piece)
            left = left - piece.astype(np.float32)
    return jnp.asarray(np.stack(parts).reshape(2, 3, MBT, 2 * HEAD))


def both_blocks(own, segments, gains, taps, qk_gains, shards):
    tokens, width = own.shape
    channels, padded = shards[0].shape[-1], shards[4].shape[-1] // 2
    wide = 3 * channels
    shape = jax.ShapeDtypeStruct
    rows, vmem = (tokens, width), pltpu.VMEM
    sums = [(2, 2, ROWS, padded), (2, ROWS, padded), (2, ROWS, channels), (ROWS, wide), (ROWS, 5 * channels // 3)]
    sums += [(2, width), (3, channels), (2, HEAD)]
    outs = [shape(rows, BF), shape(rows, BF)] + [shape(v, F32) for v in sums]
    n_vmem = len(outs)
    outs += [shape((4, 4, 2, ROWS, w), BF) for w in (padded, padded, padded, channels)] + [shape((2, 4, 4, ROWS, wide), BF)]
    scratch = [vmem((32, ROWS, w), BF) for w in (wide, channels, 2 * padded, padded)]
    scratch += [vmem((2, 3, ROWS, w), BF) for w in (padded, padded, padded, channels, wide)]
    scratch += [vmem((2, 4, 2, ROWS, padded), BF), vmem((2, 2, 4, ROWS, wide), BF), vmem((width, tokens), BF)]
    sizes = [width, wide, channels, width, 2 * padded, padded, width, width, width, width, width]
    scratch += [vmem((tokens, w), BF) for w in sizes]
    scratch += [
        vmem((4, 3, CHUNK, width), BF),
        vmem((CHUNK, width), F32),
        vmem((CHUNK, width), F32),
        vmem((tokens, wide), F32),
        vmem((tokens, channels), F32),
        vmem((2, tokens, padded), F32),
        vmem((5, tokens, 128), BF),
        vmem((6 * tokens // MBT, MBT, MBT), F32),
        vmem((2, tokens, 128), F32),
        vmem((4, tokens, 128), F32),
        vmem((ROWS, wide), F32),
        vmem((9, 8, width), F32),
        vmem((8, width), F32),
        vmem((8, width), F32),
        vmem((tokens, 128), F32),
        vmem((2, 128), F32),
        vmem((tokens, padded), F32),
        DMA((14,)),
        DMA((4,)),
        DMA((8, 16)),
        pltpu.SemaphoreType.REGULAR,
        DMA((4, 6)),
        DMA((4, 6)),
        DMA((8,)),
        DMA((2, 2)),
        DMA((10, 3)),
        DMA((10, 4)),
        DMA((10,)),
        pltpu.SemaphoreType.REGULAR((4,)),
        DMA((9,)),
        DMA((9,)),
    ]
    return pl.pallas_call(
        blocks_kernel,
        out_shape=outs,
        in_specs=[VM] * 8 + [ANY] * 3,
        out_specs=[VM] * n_vmem + [ANY] * 5,
        scratch_shapes=scratch,
        compiler_params=pltpu.CompilerParams(collective_id=0, has_side_effects=True, vmem_limit_bytes=60 * MIB),
        name="both_blocks",
    )(own, segments[None, :], gains, taps, qk_gains, rope_parts(), *shards)[:n_vmem]


def local(ends, segment_ids, norm_gains, conv_in, conv_kernel, qkv_weight, qk_gains, mix_out, gate_up, down):
    channels = mix_out.shape[1]
    hidden = gate_up.shape[3]
    padded = (hidden + 255) // 256 * 256
    kv, group, head = qkv_weight.shape[1], qkv_weight.shape[2] - 2, qkv_weight.shape[3]
    qkv_width = kv * (group + 2) * head
    spare = ((0, 0), (0, padded - hidden))

    gate_rows = jnp.pad(gate_up[0], ((0, 0),) + spare).reshape(2, ROWS, 2 * padded)
    shards = (
        mix_out[0].T,
        down[0].T,
        conv_in.transpose(1, 0, 2),
        qkv_weight.transpose(0, 2, 1, 3).reshape(ROWS, qkv_width),
        gate_rows,
    )
    result, grad_in, sum_pair, sum_down, sum_mix, sum_conv, sum_qkv, gains_sum, taps_sum, qk_sum = both_blocks(
        ends[0], segment_ids, norm_gains[0], conv_kernel, qk_gains, shards
    )
    qkv_grad = sum_qkv.reshape(ROWS, group + 2, kv, head)
    return (
        result[None],
        grad_in.astype(F32)[None],
        gains_sum[None],
        sum_conv.reshape(conv_in.shape),
        taps_sum,
        qkv_grad.transpose(0, 2, 1, 3),
        qk_sum,
        sum_mix.reshape(2 * ROWS, channels).T[None],
        sum_pair.reshape(2, 2 * ROWS, padded)[:, :, :hidden].transpose(1, 0, 2)[None],
        sum_down.reshape(2 * ROWS, padded)[:, :hidden].T[None],
    )


def solution(mesh):
    dims = (
        P(SEC, DP, None),
        P(DP),
        P(SEC, None, None),
        P((SEC, DP), None, TEN),
        P(None, TEN),
        P((SEC, DP), TEN, None, None),
        P(),
        P(SEC, TEN, DP),
        P(SEC, DP, None, TEN),
        P(SEC, TEN, DP),
    )
    results = (dims[0], dims[0], dims[2], dims[3], dims[4], dims[5], dims[6], dims[7], dims[8], dims[9])
    return jax.shard_map(local, mesh=mesh, in_specs=dims, out_specs=results, check_vma=False)
```
